32 devices in a mesh: pb: 4 (over x, core), pa: 8 (over z, y).
Axes of the slice: x: 2, y: 2, z: 4, core: 2. Of those that a mesh axis runs over, the one named last changes fastest.
Arguments:
- passages: bfloat16 [16384, 768], P(('pb', 'pa')), may hold values from -6 to 6
- queries: bfloat16 [4096, 768], P(('pb', 'pa')), may hold values from -6 to 6
- passage_ids: int32 [16384], P(('pb', 'pa')), may hold values from 0 to 30521, as said below
- query_ids: int32 [4096], P(('pb', 'pa')), may hold values from 0 to 30521, as said below
- batch_length: int32 [16], replicated, may hold values from 128 to 512, as said below
- query_batch: int32 [128], P(('pb', 'pa')), may hold values from 0 to 3
- project_in: bfloat16 [768, 2304], replicated, may hold values from -0.21875 to 0.21875
- project_out: bfloat16 [768, 768], replicated, may hold values from -1.25 to 1.25
- expand_weight: bfloat16 [768, 3072], replicated, may hold values from -0.21875 to 0.21875
- expand_bias: float32 [3072], replicated, may hold values from -3 to 3
- reduce_weight: bfloat16 [3072, 768], replicated, may hold values from -0.109375 to 0.109375
- norm_gains: float32 [2, 768], replicated, may hold values from 0.5 to 1.5
- biases: float32 [6, 768], replicated, may hold values from -1.25 to 1.25
- term_weight: float32 [768], replicated, may hold values from -0.21875 to 0.21875
- term_bias: float32 [1], replicated, may hold values from -3 to 3
- out_grad: bfloat16 [16384, 768], P(('pb', 'pa')), may hold values from -6 to 6
- score_grad: float32 [128, 32], P('pb', 'pa'), may hold values from -6 to 6
Outputs:
- scores: float32 [128, 32], P('pb', 'pa')
- passage_out: bfloat16 [16384, 768], P(('pb', 'pa'))
- passage_grad: bfloat16 [16384, 768], P(('pb', 'pa'))
- query_grad: bfloat16 [4096, 768], P(('pb', 'pa'))
- project_in_grad: float32 [768, 2304], P('pa')
- project_out_grad: float32 [768, 768], P('pa')
- expand_grad: float32 [768, 3072], P('pa')
- expand_bias_grad: float32 [3072], P('pa')
- reduce_grad: float32 [3072, 768], P('pa')
- gains_grad: float32 [2, 768], P(None, 'pa')
- biases_grad: float32 [6, 768], P(None, 'pa')
- term_weight_grad: float32 [768], P('pa')
- term_bias_grad: float32 [1], replicated
The draws below stay inside these ranges and needn't reach their ends.
Inputs may be any that keep to these rules, and one draw needn't show every extreme that they name: passage_ids and query_ids share which ids are frequent. `query_ids`: they share their frequent ids with passage_ids. `batch_length`: each batch's passages are all 128 or all 512 tokens long; both lengths occur. `query_batch`: the batch among the 4 batches of the query's group.
All inputs are finite; a program needn't handle non-finite values.
Results may differ from the reference program's by a relative error of at most 0.013.
Values sent between devices are 32-bit elements; how exact they have to be, the bound alone decides.
No kernel may reach another device: no remote copies, remote signals or barrier semaphores. Data moves between devices by JAX's collectives and lax.ppermute only.
A program may use at most 192 MiB of HBM per device.

```python
import jax
import jax.numpy as jnp
from jax import lax

D = 768
HEADS = 12
HEAD = 64
FF = 3072
VOCAB = 30522
LONG = 512
SHORT = 128
QLEN = 32
BATCH_PB = 4
PTOK_DEV = 512
Q_DEV = 4
QTOK_DEV = 128
QUERIES = 128
QTOK = 4096
PTOK = 16384
SLOTS = 32
NBATCH = 16
N_PB = 4
N_PA = 8


def drawn_normal(key, salt, rows):
    drawn = jax.random.normal(jax.random.fold_in(key, salt), (rows, D), jnp.float32)
    return jnp.clip(drawn, -6.0, 6.0)


def draw_passages(key, part):
    return drawn_normal(key, 23, PTOK).astype(jnp.bfloat16)


def draw_queries(key, part):
    return drawn_normal(key, 29, QTOK).astype(jnp.bfloat16)


def skewed_ids(key, salt, count):
    order = jax.random.permutation(jax.random.fold_in(key, 7), VOCAB).astype(jnp.int32)
    level_key, pick_key = jax.random.split(jax.random.fold_in(key, salt))
    levels = jax.random.randint(level_key, (count,), 7, 16)
    upper = jnp.minimum(jnp.left_shift(jnp.ones_like(levels), levels), VOCAB)
    picks = jax.random.randint(pick_key, (count,), 0, upper)
    drawn = order[picks]
    drawn = drawn.at[0].set(0)
    drawn = drawn.at[1].set(VOCAB - 1)
    return drawn.astype(jnp.int32)


def draw_passage_ids(key, part):
    return skewed_ids(key, 11, PTOK)


def draw_query_ids(key, part):
    return skewed_ids(key, 13, QTOK)


def draw_batch_length(key, part):
    coins = jax.random.randint(jax.random.fold_in(key, 17), (NBATCH,), 0, 2)
    coins = coins.at[1].set(1 - coins[0])
    return jnp.where(coins == 1, LONG, SHORT).astype(jnp.int32)


def touch_ends(result, own_key, least, high):
    shape = result.shape
    spot = [jax.random.randint(jax.random.fold_in(own_key, axis), (), 0, shape[axis]) for axis in range(len(shape))]
    result = result.at[tuple(spot)].set(least)
    longest = shape.index(max(shape))
    spot[longest] = (spot[longest] + 1) % shape[longest]
    return result.at[tuple(spot)].set(high)


def block_levels(key, shape, shards, low, top_value):
    level = 1.0
    for dim, parts in shards:
        steps = jax.random.uniform(jax.random.fold_in(jax.random.fold_in(key, 6), dim), (parts,), jnp.float32, low / len(shards), top_value / len(shards))
        level = level * jnp.repeat(jnp.exp(steps), shape[dim] // parts).reshape((-1,) + (1,) * (len(shape) - 1 - dim))
    return level


def normal_values(rng, extent, deviation, limit, cuts=(), kind=jnp.bfloat16):
    level = block_levels(rng, extent, cuts, -0.22, 0.18) if cuts else 1.0
    values = jax.random.normal(rng, extent, jnp.float32) * deviation * level
    return jnp.minimum(jnp.maximum(values, -limit), limit).astype(kind)


def setup_inputs(seed: int = 0) -> dict:
    splits = jax.random.split(jax.random.key(seed), 18)
    return {
        "passages": draw_passages(jax.random.fold_in(splits[17], 71), 0),
        "queries": draw_queries(jax.random.fold_in(splits[17], 71), 0),
        "passage_ids": draw_passage_ids(jax.random.fold_in(splits[17], 71), 0),
        "query_ids": draw_query_ids(jax.random.fold_in(splits[17], 71), 0),
        "batch_length": draw_batch_length(jax.random.fold_in(splits[17], 71), 0),
        "query_batch": touch_ends(jax.random.randint(splits[5], (QUERIES,), 0, BATCH_PB), jax.random.fold_in(splits[5], 1), 0, BATCH_PB - 1).astype(jnp.int32),
        "project_in": normal_values(splits[6], (D, 3 * D), D ** -0.5, 0.21875),
        "project_out": normal_values(splits[7], (D, D), (D // 32) ** -0.5, 1.25),
        "expand_weight": normal_values(splits[8], (D, FF), D ** -0.5, 0.21875),
        "expand_bias": normal_values(splits[9], (FF,), 0.5, 3.0, (), jnp.float32),
        "reduce_weight": normal_values(splits[10], (FF, D), FF ** -0.5, 0.109375),
        "norm_gains": jnp.clip(1.0 + 0.1 * jax.random.normal(splits[11], (2, D), jnp.float32), 0.5, 1.5),
        "biases": normal_values(splits[12], (6, D), 0.2, 1.25, (), jnp.float32),
        "term_weight": normal_values(splits[13], (D,), D ** -0.5, 0.21875, (), jnp.float32),
        "term_bias": normal_values(splits[14], (1,), 0.5, 3.0, (), jnp.float32),
        "out_grad": normal_values(splits[15], (PTOK, D), 1.0, 6.0, ((0, 32),)),
        "score_grad": normal_values(splits[16], (QUERIES, SLOTS), 1.0, 6.0, ((0, 4), (1, 8)), jnp.float32),
    }


@jax.custom_vjp
def low(v):
    return lax.optimization_barrier(v.astype(jnp.bfloat16)).astype(jnp.float32)

@jax.custom_vjp
def low_back(v):
    return v

def low_keep(v):
    return (low(v), None)

def low_pass(kept, grad):
    return (grad,)

def back_keep(v):
    return (v, None)

def back_low(kept, grad):
    return (low(grad),)
low.defvjp(low_keep, low_pass)
low_back.defvjp(back_keep, back_low)
HIGH = lax.Precision.HIGHEST
NEG = -1e+30
LN_EPS = 1e-12

def matmul(left, right):
    return jnp.dot(left, right, precision=HIGH)

def layer_norm(total, gain, shift):
    centre = lax.optimization_barrier(jnp.mean(total, axis=-1, keepdims=True))
    centred = total - centre
    variance = lax.optimization_barrier(jnp.mean(centred * centred, axis=-1, keepdims=True))
    return centred * lax.rsqrt(variance + LN_EPS) * gain + shift

def attend(query, key, value, segment):
    length = query.shape[0]
    heads_query = query.reshape(length, HEADS, HEAD)
    heads_key = key.reshape(length, HEADS, HEAD)
    heads_value = value.reshape(length, HEADS, HEAD)
    logits = low_back(jnp.einsum('qhd,khd->hqk', heads_query, heads_key, precision=HIGH) * HEAD ** (-0.5))
    allowed = (segment[:, None] == segment[None, :])[None]
    weights = jax.nn.softmax(jnp.where(allowed, logits, NEG), axis=-1)
    mixed = jnp.einsum('hqk,khd->qhd', low(weights), heads_value, precision=HIGH)
    return mixed.reshape(length, HEADS * HEAD)

def encode(tokens, pass_segment, query_segment, params):
    project_in, project_out, expand_weight, expand_bias, reduce_weight, norm_gains, biases, term_weight, term_bias = params
    n_pass = pass_segment.shape[0]
    width = tokens.shape[1]
    bias_in = jnp.concatenate([biases[0], jnp.zeros_like(biases[0]), biases[1]])
    mixed = low(low_back(matmul(tokens, project_in) + bias_in))
    query_all = mixed[:, :width]
    key_all = mixed[:, width:2 * width]
    value_all = mixed[:, 2 * width:]
    block_count = n_pass // LONG

    def passage_part(matrix):
        return matrix[:n_pass].reshape(block_count, LONG, width)
    attended_pass = jax.vmap(attend)(passage_part(query_all), passage_part(key_all), passage_part(value_all), pass_segment.reshape(block_count, LONG)).reshape(n_pass, width)
    attended_query = attend(query_all[n_pass:], key_all[n_pass:], value_all[n_pass:], query_segment)
    attended = low(low_back(jnp.concatenate([attended_pass, attended_query], axis=0)))
    branch = low_back(matmul(attended, project_out) + biases[2])
    first_out = layer_norm(tokens + branch, norm_gains[0], biases[4])
    expanded = low_back(matmul(low(first_out), expand_weight) + expand_bias)
    reduced = low_back(matmul(low(jax.nn.gelu(expanded, approximate=False)), reduce_weight) + biases[3])
    second_out = layer_norm(first_out + reduced, norm_gains[1], biases[5])
    term = jax.nn.softplus(matmul(second_out, term_weight) + term_bias[0])
    return (second_out[:n_pass], term[:n_pass], term[n_pass:])

def reference(passages, queries, passage_ids, query_ids, batch_length, query_batch, project_in, project_out, expand_weight, expand_bias, reduce_weight, norm_gains, biases, term_weight, term_bias, out_grad, score_grad):
    devices = N_PB * N_PA
    per_batch = N_PA // BATCH_PB
    block_index = jnp.arange(devices, dtype=jnp.int32)
    local_batch = block_index % N_PA // per_batch
    batch_of = block_index // N_PA * BATCH_PB + local_batch
    lengths = batch_length[batch_of]
    positions = jnp.arange(PTOK_DEV, dtype=jnp.int32)
    pass_segments = positions[None, :] // lengths[:, None]
    query_segment = jnp.arange(QTOK_DEV, dtype=jnp.int32) // QLEN
    slot_range = jnp.arange(PTOK_DEV // SHORT, dtype=jnp.int32)
    group_ids = query_ids.reshape(N_PB, N_PA * QTOK_DEV)
    token_batch = jnp.repeat(query_batch, QLEN).reshape(N_PB, N_PA * QTOK_DEV)
    pass_ids = passage_ids.reshape(devices, PTOK_DEV)
    group_of = (block_index // N_PA).astype(jnp.int32)

    def forward(pass_rows, query_rows, params):
        pass_blocks = pass_rows.reshape(devices, PTOK_DEV, -1)
        query_blocks = query_rows.reshape(devices, QTOK_DEV, -1)

        def one_device(items):
            pass_block, query_block, segment = items
            return encode(jnp.concatenate([pass_block, query_block], axis=0), segment, query_segment, params)
        outputs, pass_terms, query_terms = lax.map(jax.checkpoint(one_device), (pass_blocks, query_blocks, pass_segments))
        group_terms = query_terms.reshape(N_PB, N_PA * QTOK_DEV)

        def one_score(items):
            terms_here, ids_here, segment, group, batch_here = items
            terms_group = lax.dynamic_index_in_dim(group_terms, group, 0, keepdims=False)
            ids_group = lax.dynamic_index_in_dim(group_ids, group, 0, keepdims=False)
            tags_group = lax.dynamic_index_in_dim(token_batch, group, 0, keepdims=False)
            weighted = terms_group * (tags_group == batch_here).astype(jnp.float32)
            matches = (ids_group[:, None] == ids_here[None, :]).astype(jnp.float32)
            placed = low(terms_here)[:, None] * (segment[:, None] == slot_range[None, :]).astype(jnp.float32)
            per_token = low_back(matmul(matches, placed))
            return lax.optimization_barrier(jnp.sum((weighted[:, None] * per_token).reshape(N_PA * Q_DEV, QLEN, -1), axis=1))
        scores = lax.map(jax.checkpoint(one_score), (pass_terms, pass_ids, pass_segments, group_of, local_batch))
        scores = scores.reshape(N_PB, N_PA, N_PA * Q_DEV, PTOK_DEV // SHORT).transpose(0, 2, 1, 3)
        scores = scores.reshape(N_PB * N_PA * Q_DEV, N_PA * (PTOK_DEV // SHORT))
        return (outputs.reshape(devices * PTOK_DEV, -1), scores)
    params = (project_in.astype(jnp.float32), project_out.astype(jnp.float32), expand_weight.astype(jnp.float32), expand_bias.astype(jnp.float32), reduce_weight.astype(jnp.float32), norm_gains.astype(jnp.float32), biases.astype(jnp.float32), term_weight.astype(jnp.float32), term_bias.astype(jnp.float32))
    (outputs, scores), pullback = jax.vjp(forward, passages.astype(jnp.float32), queries.astype(jnp.float32), params)
    pass_grad, query_grad_all, param_grads = pullback((out_grad.astype(jnp.float32), score_grad.astype(jnp.float32)))
    return (scores, outputs.astype(jnp.bfloat16), pass_grad.astype(jnp.bfloat16), query_grad_all.astype(jnp.bfloat16), param_grads[0], param_grads[1], param_grads[2], param_grads[3], param_grads[4], param_grads[5], param_grads[6], param_grads[7], param_grads[8])
```

```python
from functools import partial

import jax
import jax.numpy as jnp
from jax import lax
from jax.sharding import PartitionSpec as P

HEADS = 12
HEAD = 64
LONG = 512
QLEN = 32
BATCH_PB = 4


NEG = -1e30
HIGH = lax.Precision.HIGHEST
LN_EPS = 1e-12


def project(left, right):
    return jnp.dot(left, right, preferred_element_type=jnp.float32)


def project_back(left, right):
    return lax.dot_general(
        left, right, (((1,), (1,)), ((), ())), preferred_element_type=jnp.float32
    )


def contract_rows(left, right):
    return lax.dot_general(
        left, right, (((0,), (0,)), ((), ())), preferred_element_type=jnp.float32
    )


def column_sum(matrix):
    return jnp.sum(matrix, axis=0, dtype=jnp.float32)


def norm_forward(total, gain, shift):
    centred = total - jnp.mean(total, axis=-1, keepdims=True)
    inverse = lax.rsqrt(jnp.mean(centred * centred, axis=-1, keepdims=True) + LN_EPS)
    normed = centred * inverse
    return (normed * gain + shift, normed, inverse)


def norm_backward(grad, normed, inverse, gain):
    scaled = grad * gain
    centred = scaled - jnp.mean(scaled, axis=-1, keepdims=True)
    return inverse * (centred - normed * jnp.mean(scaled * normed, axis=-1, keepdims=True))


def split_heads(matrix):
    return matrix.reshape(matrix.shape[0], HEADS, HEAD)


def attend_forward(query, key, value, segment):
    logits = jnp.einsum(
        "qhd,khd->hqk", split_heads(query), split_heads(key), preferred_element_type=jnp.float32
    ) * HEAD ** (-0.5)
    allowed = (segment[:, None] == segment[None, :])[None]
    logits = jnp.where(allowed, logits, NEG)
    highest = jnp.max(logits, axis=-1, keepdims=True)
    powers = jnp.exp(logits - highest)
    totals = jnp.sum(powers, axis=-1, keepdims=True)
    weights = (powers / totals).astype(jnp.bfloat16)
    mixed = jnp.einsum(
        "hqk,khd->qhd", weights, split_heads(value), preferred_element_type=jnp.float32
    )
    return (mixed.reshape(query.shape[0], -1), highest + jnp.log(totals))


def attend_backward(query, key, value, segment, log_total, grad_mixed):
    scale = HEAD ** (-0.5)
    heads_query = split_heads(query)
    heads_key = split_heads(key)
    heads_value = split_heads(value)
    heads_grad = split_heads(grad_mixed)
    logits = (
        jnp.einsum("qhd,khd->hqk", heads_query, heads_key, preferred_element_type=jnp.float32)
        * scale
    )
    allowed = (segment[:, None] == segment[None, :])[None]
    weights = jnp.where(allowed, jnp.exp(logits - log_total), 0.0)
    grad_weights = jnp.einsum(
        "qhd,khd->hqk", heads_grad, heads_value, preferred_element_type=jnp.float32
    )
    grad_value = jnp.einsum(
        "hqk,qhd->khd", weights.astype(jnp.bfloat16), heads_grad, preferred_element_type=jnp.float32
    )
    grad_logits = (
        weights * (grad_weights - jnp.sum(weights * grad_weights, axis=-1, keepdims=True))
    ).astype(jnp.bfloat16)
    grad_query = (
        jnp.einsum("hqk,khd->qhd", grad_logits, heads_key, preferred_element_type=jnp.float32)
        * scale
    )
    grad_key = (
        jnp.einsum("hqk,qhd->khd", grad_logits, heads_query, preferred_element_type=jnp.float32)
        * scale
    )
    length = query.shape[0]
    return jnp.concatenate(
        [
            grad_query.reshape(length, -1),
            grad_key.reshape(length, -1),
            grad_value.reshape(length, -1),
        ],
        axis=1,
    )


GROUP_FIRST = (("pb", 2), ("pa", 1))
ROW_FIRST = (("pa", 1), ("pb", 2))


def swap(value, axis, distance):
    return lax.ppermute(
        value, axis, [(i, i ^ distance) for i in range(lax.axis_size(axis))]
    )


def bit(axis, distance):
    return (lax.axis_index(axis) // distance) % 2


def pick(value, index, dim):
    return lax.dynamic_index_in_dim(value, index, dim, keepdims=False)


def group_gather(mine):
    count = lax.axis_size("pa")
    me = lax.axis_index("pa")
    ahead = [mine]
    for shift in range(1, count):
        ahead.append(
            lax.ppermute(mine, "pa", [((i + shift) % count, i) for i in range(count)])
        )
    twice = jnp.concatenate(ahead + ahead, axis=1)
    width = mine.shape[1]
    return lax.dynamic_slice_in_dim(twice, (count - me) * width, count * width, axis=1)


def group_scatter(whole):
    count = lax.axis_size("pa")
    me = lax.axis_index("pa")
    blocks = whole.reshape(count, -1)
    total = pick(blocks, me, 0)
    for shift in range(1, count):
        block = pick(blocks, (me + shift) % count, 0)
        total = total + lax.ppermute(
            block, "pa", [(i, (i + shift) % count) for i in range(count)]
        )
    return total


def steps_of(order):
    steps = [(axis, distance) for axis, distance in order]
    distance = 2
    while distance < lax.axis_size("pa"):
        steps.append(("pa", distance))
        distance *= 2
    return steps


def tree_sum(send, keep, order):
    names = []
    distance = lax.axis_size("pa") // 2
    while distance:
        names.append(("pa", distance))
        distance //= 2
    names.append(("pb", 2))
    received = swap(send, "pb", 1)
    for axis, distance in steps_of(order):
        dim = names.index((axis, distance))
        names.pop(dim)
        mine = bit(axis, distance)
        send = pick(keep, 1 - mine, dim) + pick(received, 1 - mine, dim)
        keep = pick(keep, mine, dim) + pick(received, mine, dim)
        received = swap(send, axis, distance)
    mine = keep + received
    other = swap(mine, "pb", 2)
    high = bit("pb", 2)
    return jnp.where(high == 0, jnp.stack([mine, other]), jnp.stack([other, mine]))


def cut(matrix):
    bits = lax.axis_size("pa").bit_length() - 1
    rows = matrix.shape[0] >> (bits + 1)
    return matrix.reshape((2,) * (bits + 1) + (rows, matrix.shape[1]))


def summed_rows(left, right, order):
    core = bit("pb", 1)
    half = right.shape[1] // 2
    parts = [
        cut(contract_rows(left, lax.dynamic_slice_in_dim(right, side * half, half, axis=1)))
        for side in (1 - core, core)
    ]
    mine = tree_sum(parts[0], parts[1], order)
    mine = mine.reshape(-1, half)
    other = swap(mine, "pb", 1)
    return jnp.where(
        core == 0, jnp.concatenate([mine, other], 1), jnp.concatenate([other, mine], 1)
    )


def summed_vectors(vectors):
    count = lax.axis_size("pa")
    core = bit("pb", 1)
    shares = [v.reshape(count, -1) for v in vectors]
    packed = jnp.concatenate(shares, axis=1)
    used = packed.shape[1]
    lanes = -(-used // 512) * 128
    packed = jnp.pad(packed, ((0, 0), (0, 4 * lanes - used)))
    packed = packed.reshape(count, 2, 2, 1, lanes)
    parts = [pick(packed, 1 - core, 2), pick(packed, core, 2)]
    parts = [p.reshape((2,) * (count.bit_length() - 1) + (2, 1, lanes)) for p in parts]
    mine = tree_sum(parts[0], parts[1], GROUP_FIRST)
    other = swap(mine, "pb", 1)
    both = jnp.where(core == 0, jnp.stack([mine, other], 1), jnp.stack([other, mine], 1))
    flat = both.reshape(-1)
    totals = []
    first = 0
    for share in shares:
        totals.append(flat[first : first + share.shape[1]])
        first += share.shape[1]
    return totals


def on_device(
    passages,
    queries,
    passage_ids,
    query_ids,
    batch_length,
    query_batch,
    project_in,
    project_out,
    expand_weight,
    expand_bias,
    reduce_weight,
    norm_gains,
    biases,
    term_weight,
    term_bias,
    out_grad,
    score_grad,
):
    axis_count = lax.axis_size("pa")
    group_index = lax.axis_index("pb")
    member_index = lax.axis_index("pa")
    local_batch = member_index // (axis_count // BATCH_PB)
    length = batch_length[group_index * BATCH_PB + local_batch]
    n_pass = passages.shape[0]
    n_query = queries.shape[0]
    width = passages.shape[1]
    tokens = jnp.concatenate([passages, queries], axis=0)
    segments = []
    first = 0
    segments.append((first, LONG, lax.iota(jnp.int32, LONG) // length))
    segments.append((n_pass, n_query, lax.iota(jnp.int32, n_query) // QLEN))
    zero_bias = jnp.zeros_like(biases[0])
    mixed = (
        project(tokens, project_in) + jnp.concatenate([biases[0], zero_bias, biases[1]])
    ).astype(jnp.bfloat16)
    pieces = []
    log_totals = []
    for first, count, segment in segments:
        rows_here = mixed[first : first + count]
        attended_here, log_here = attend_forward(
            rows_here[:, :width],
            rows_here[:, width : 2 * width],
            rows_here[:, 2 * width :],
            segment,
        )
        pieces.append(attended_here)
        log_totals.append(log_here)
    attended = jnp.concatenate(pieces, axis=0).astype(jnp.bfloat16)
    first_out, normed_one, inverse_one = norm_forward(
        tokens.astype(jnp.float32) + project(attended, project_out) + biases[2],
        norm_gains[0],
        biases[4],
    )
    first_low = first_out.astype(jnp.bfloat16)
    expanded = project(first_low, expand_weight) + expand_bias
    hidden = jax.nn.gelu(expanded, approximate=False).astype(jnp.bfloat16)
    second_out, normed_two, inverse_two = norm_forward(
        first_out + project(hidden, reduce_weight) + biases[3], norm_gains[1], biases[5]
    )
    term_pre = jnp.dot(second_out, term_weight, precision=HIGH) + term_bias[0]
    term = jax.nn.softplus(term_pre)
    passage_out = second_out[:n_pass].astype(jnp.bfloat16)
    query_tags = jnp.broadcast_to(query_batch[:, None], (query_batch.shape[0], QLEN)).reshape(-1)
    gathered = group_gather(
        jnp.stack([term[n_pass:], query_ids.astype(jnp.float32), query_tags.astype(jnp.float32)])
    )
    group_ids = gathered[1].astype(jnp.int32)
    group_mask = (gathered[2].astype(jnp.int32) == local_batch).astype(jnp.float32)
    weighted = gathered[0] * group_mask
    group_queries = score_grad.shape[0]
    slot_count = score_grad.shape[1]
    slot_table = (lax.iota(jnp.int32, n_pass) // length)[:, None] == lax.iota(
        jnp.int32, slot_count
    )[None, :]
    placed = jnp.where(
        slot_table, term[:n_pass].astype(jnp.bfloat16)[:, None], jnp.zeros((), jnp.bfloat16)
    )
    token_grad = jnp.broadcast_to(
        score_grad[:, None, :], (group_queries, QLEN, slot_count)
    ).reshape(-1, slot_count)
    score_weight = (token_grad * weighted[:, None]).astype(jnp.bfloat16)
    first = 0
    matches = (group_ids[:, None] == passage_ids[None, first : first + LONG]).astype(jnp.bfloat16)
    per_token = project(matches, placed)
    placed_grads = contract_rows(matches, score_weight)
    scores = jnp.sum(
        (weighted[:, None] * per_token).reshape(group_queries, QLEN, slot_count), axis=1
    )
    pass_term_grad = jnp.sum(jnp.where(slot_table, placed_grads, 0.0), axis=1)
    query_term_grad = group_scatter(jnp.sum(token_grad * per_token, axis=1) * group_mask)
    pre_grad = jnp.concatenate([pass_term_grad, query_term_grad]) * jax.nn.sigmoid(term_pre)
    term_weight_grad = jnp.dot(pre_grad, second_out, precision=HIGH)
    term_bias_grad = jnp.sum(pre_grad)
    second_grad = (
        jnp.concatenate(
            [out_grad.astype(jnp.float32), jnp.zeros((n_query, width), jnp.float32)], axis=0
        )
        + pre_grad[:, None] * term_weight[None, :]
    )
    sum_two_grad = norm_backward(second_grad, normed_two, inverse_two, norm_gains[1])
    reduce_out_grad = sum_two_grad.astype(jnp.bfloat16)
    hidden_grad = project_back(reduce_out_grad, reduce_weight)
    expanded_grad = jax.vjp(partial(jax.nn.gelu, approximate=False), expanded)[1](hidden_grad)[
        0
    ].astype(jnp.bfloat16)
    first_grad = project_back(expanded_grad, expand_weight) + sum_two_grad
    sum_one_grad = norm_backward(first_grad, normed_one, inverse_one, norm_gains[0])
    branch_grad = sum_one_grad.astype(jnp.bfloat16)
    attended_grad = project_back(branch_grad, project_out).astype(jnp.bfloat16)
    mixed_parts = []
    for (first, count, segment), log_here in zip(segments, log_totals):
        rows_here = mixed[first : first + count]
        mixed_parts.append(
            attend_backward(
                rows_here[:, :width],
                rows_here[:, width : 2 * width],
                rows_here[:, 2 * width :],
                segment,
                log_here,
                attended_grad[first : first + count],
            )
        )
    mixed_grad = jnp.concatenate(mixed_parts, axis=0).astype(jnp.bfloat16)
    input_grad = project_back(mixed_grad, project_in) + sum_one_grad
    reduce_total = summed_rows(hidden, reduce_out_grad, ROW_FIRST)
    expand_total = summed_rows(first_low, expanded_grad, GROUP_FIRST)
    out_total = summed_rows(attended, branch_grad, GROUP_FIRST)
    in_total = summed_rows(tokens, mixed_grad, ROW_FIRST)
    gain_one = jnp.sum(first_grad * normed_one, axis=0)
    gain_two = jnp.sum(second_grad * normed_two, axis=0)
    shift_query = column_sum(mixed_grad[:, :width])
    shift_value = column_sum(mixed_grad[:, 2 * width :])
    shift_branch = column_sum(branch_grad)
    shift_reduce = column_sum(reduce_out_grad)
    shift_first = jnp.sum(first_grad, axis=0)
    shift_second = jnp.sum(second_grad, axis=0)
    expand_shift = column_sum(expanded_grad)
    vectors = summed_vectors(
        [
            gain_one,
            gain_two,
            shift_query,
            shift_value,
            shift_branch,
            shift_reduce,
            shift_first,
            shift_second,
            expand_shift,
            term_weight_grad,
            jnp.broadcast_to(term_bias_grad, (axis_count,)),
        ]
    )
    matrices = (in_total, out_total, expand_total, reduce_total)
    gains_grad = jnp.stack([vectors[0], vectors[1]])
    biases_grad = jnp.stack(
        [vectors[2], vectors[3], vectors[4], vectors[5], vectors[6], vectors[7]]
    )
    return (
        scores,
        passage_out,
        input_grad[:n_pass].astype(jnp.bfloat16),
        input_grad[n_pass:].astype(jnp.bfloat16),
        matrices[0],
        matrices[1],
        matrices[2],
        vectors[8],
        matrices[3],
        gains_grad,
        biases_grad,
        vectors[9],
        vectors[10],
    )


def solution(mesh):
    return jax.shard_map(
        on_device,
        mesh=mesh,
        in_specs=(
            P(("pb", "pa"), None),
            P(("pb", "pa"), None),
            P(("pb", "pa")),
            P(("pb", "pa")),
            P(),
            P(("pb", "pa")),
            P(),
            P(),
            P(),
            P(),
            P(),
            P(),
            P(),
            P(),
            P(),
            P(("pb", "pa"), None),
            P("pb", "pa"),
        ),
        out_specs=(
            P("pb", "pa"),
            P(("pb", "pa"), None),
            P(("pb", "pa"), None),
            P(("pb", "pa"), None),
            P("pa", None),
            P("pa", None),
            P("pa", None),
            P("pa"),
            P("pa", None),
            P(None, "pa"),
            P(None, "pa"),
            P("pa"),
            P(),
        ),
        check_vma=False,
    )
```

```python
from functools import partial

import jax
import jax.numpy as jnp
from jax import lax
from jax.experimental import pallas as pl
from jax.experimental.pallas import tpu as pltpu
from jax.sharding import PartitionSpec as P

HEADS = 12
HEAD = 64
LONG = 512
QLEN = 32
BATCH_PB = 4

NEG = -1e30
HIGH = lax.Precision.HIGHEST
LN_EPS = 1e-12
SCALE = HEAD ** (-0.5)
BLOCK = 256
TILE = 128
F32 = jnp.float32
BF16 = jnp.bfloat16

IN_VMEM = pl.BlockSpec(memory_space=pltpu.VMEM)
IN_SMEM = pl.BlockSpec(memory_space=pltpu.SMEM)
IN_PLACE = pl.BlockSpec(memory_space=pl.ANY)


def shape(dims, dtype):
    return (tuple(dims), dtype)


def dot(left, right):
    return jnp.dot(left, right, preferred_element_type=F32)


def dot_nt(left, right, precision=None):
    return lax.dot_general(
        left, right, (((1,), (1,)), ((), ())), preferred_element_type=F32, precision=precision
    )


def dot_tn(left, right):
    return lax.dot_general(left, right, (((0,), (0,)), ((), ())), preferred_element_type=F32)


def columns(index, width, first=0):
    return pl.ds(pl.multiple_of(first + index * width, TILE), width)


def tiles(count):
    return [slice(first, first + TILE) for first in range(0, count, TILE)]


def row_sum(matrix):
    return jnp.sum(matrix, axis=0, keepdims=True)


def fetch(pairs, sems, first=0):
    copies = [
        pltpu.make_async_copy(source, target, sems.at[first + i]) for i, (source, target) in enumerate(pairs)
    ]
    for copy in copies:
        copy.start()
    return copies


def finish_all(copies):
    for copy in copies:
        copy.wait()


def norm_forward(total):
    centred = total - jnp.mean(total, axis=-1, keepdims=True)
    inverse = lax.rsqrt(jnp.mean(centred * centred, axis=-1, keepdims=True) + LN_EPS)
    return centred * inverse, inverse


def norm_backward(scaled, normed, inverse):
    centred = scaled - jnp.mean(scaled, axis=-1, keepdims=True)
    return inverse * (centred - normed * jnp.mean(scaled * normed, axis=-1, keepdims=True))


def head_lanes(sub):
    lane = lax.broadcasted_iota(jnp.int32, (1, 2 * HEAD), 1)
    return (lane // HEAD) == sub


def same_slot(count, length):
    rows = lax.broadcasted_iota(jnp.int32, (count, count), 0) // length
    cols = lax.broadcasted_iota(jnp.int32, (count, count), 1) // length
    return jnp.where(rows == cols, 0.0, NEG)


def attend(mixed, turned, stats, first, count, width, mask):
    rows = slice(first, first + count)

    def pair(hp, carry):
        key = mixed[rows, columns(hp, 2 * HEAD, width)]
        value = mixed[rows, columns(hp, 2 * HEAD, 2 * width)].T
        ones = jnp.ones((16, count), BF16)
        for sub in (0, 1):
            key_here = jnp.where(head_lanes(sub), key, jnp.zeros_like(key))
            value_here = jnp.concatenate([value[sub * HEAD : (sub + 1) * HEAD], ones])
            logits = dot_nt(key_here, mixed[rows, columns(hp, 2 * HEAD)]) + mask[...]
            highest = jnp.max(logits, axis=0, keepdims=True)
            summed = dot(value_here, jnp.exp(logits - highest).astype(BF16))
            total = summed[HEAD : HEAD + 1]
            out_rows = pl.ds(pl.multiple_of((2 * hp + sub) * HEAD, HEAD), HEAD)
            turned[out_rows, rows] = (summed[:HEAD] / total).astype(BF16)
            stats[2 * hp + sub, :, rows] = highest + jnp.log(total)
        return carry

    lax.fori_loop(0, HEADS // 2, pair, 0, unroll=2)


def grow(rows, first, count, expand, cols, expand_bias, hidden, slope):
    for at in range(0, count, min(BLOCK, count)):
        tile = slice(at, at + min(BLOCK, count))
        value = dot(rows[first + at : first + tile.stop, :], expand[:, cols]) + expand_bias[:, cols]
        lower = 0.5 + 0.5 * lax.erf(value * (0.5**0.5))
        hidden[tile, cols] = (value * lower).astype(BF16)
        density = jnp.exp(-0.5 * value * value) * 0.3989422804014327
        slope[tile, cols] = (lower + value * density).astype(BF16)


def by_piece(block, hidden, out):
    shard, piece = lax.div(block, 3), lax.rem(block, 3)
    return hidden.at[:, columns(block, TILE)], out.at[piece, :, columns(shard, TILE)]


def close_forward(total, normed_one, first, count, gains, biases, term_weight, term_bias, normed, inverse, pre, passage_out, tell):
    for i, tile in enumerate(tiles(count)):
        base = normed_one[first + tile.start : first + tile.stop, :] * gains[0:1, :] + biases[4:5, :]
        unit, scale = norm_forward(base + total[tile, :] + biases[3:4, :])
        normed[tile, :] = unit
        inverse[tile, :] = scale
        second = unit * gains[1:2, :] + biases[5:6, :]
        pre[tile, :] = jnp.sum(second * term_weight[...], axis=-1, keepdims=True) + term_bias[0]
        if passage_out is not None:
            passage_out[tile, :] = second.astype(BF16)
        tell(i, tile)


def softplus(value):
    return jnp.maximum(value, 0.0) + jnp.log1p(jnp.exp(-jnp.abs(value)))


def sigmoid(value):
    return 1.0 / (1.0 + jnp.exp(-value))


def forward_one(
    length, passages, queries, project_in, project_out, expand, reduce, expand_bias, gains, biases,
    term_weight, term_bias, query_ids, query_batch,
    mixed_out, attended_out, turned_out, stats, normed_out, inverse_one, low_out,
    hidden_out, slope_out, normed_two, inverse_two, pre, known,
    in_here, out_here, expand_here, reduce_here, mixed, attended, turned, normed_one, low, hidden, slope,
    mask, query_mask, total, sems, out_sems,
):
    n_pass, width = passages.shape
    n_query = queries.shape[0]
    count = n_pass + n_query
    parts = [slice(i * width, (i + 1) * width) for i in range(3)]
    copies = fetch(
        [(project_in.at[:, part], in_here.at[:, part]) for part in parts]
        + [(project_out, out_here), (expand, expand_here), (reduce, reduce_here)],
        sems,
    )
    mask[...] = same_slot(n_pass, length[0])
    query_mask[...] = same_slot(n_query, QLEN)
    for part in range(3):
        copies[part].wait()
        for source, first, rows in ((passages, 0, n_pass), (queries, n_pass, n_query)):
            value = dot(source[...], in_here[:, parts[part]])
            if part != 1:
                value = value + biases[part // 2 : part // 2 + 1, :]
            if part == 0:
                value = value * SCALE
            mixed[first : first + rows, parts[part]] = value.astype(BF16)
    puts = fetch([(mixed, mixed_out)], out_sems)
    attend(mixed, turned, stats, n_pass, n_query, width, query_mask)
    attend(mixed, turned, stats, 0, n_pass, width, mask)
    attended[...] = turned[...].T
    puts += fetch([(turned, turned_out), (attended, attended_out)], out_sems, 1)
    copies[3].wait()
    total[...] = dot(attended[...], out_here[...])
    for tile in reversed(tiles(count)):
        source, at = (passages, tile.start) if tile.start < n_pass else (queries, tile.start - n_pass)
        unit, scale = norm_forward(source[at : at + TILE, :].astype(F32) + total[tile, :] + biases[2:3, :])
        normed_one[tile, :] = unit
        inverse_one[tile, :] = scale
        low[tile, :] = (unit * gains[0:1, :] + biases[4:5, :]).astype(BF16)
    puts += fetch([(normed_one, normed_out), (low, low_out)], out_sems, 3)
    copies[4].wait()
    wide = 2 * BLOCK

    def block(j, carry):
        grow(low, n_pass, n_query, expand_here, columns(j, wide), expand_bias, hidden, slope)
        return carry

    lax.fori_loop(0, expand.shape[1] // wide, block, 0, unroll=2)
    puts += fetch(
        [by_piece(i, hidden, hidden_out) for i in range(expand.shape[1] // TILE)] + [(slope, slope_out)], out_sems, 5
    )
    copies[5].wait()
    total[0:n_query, :] = dot(hidden[...], reduce_here[...])
    close_forward(
        total, normed_one, n_pass, n_query, gains, biases, term_weight, term_bias, normed_two, inverse_two, pre, None,
        lambda i, tile: None,
    )
    known[0, 0:1, :] = jnp.broadcast_to(softplus(pre[...]), (n_query, TILE)).T[0:1, :]
    known[0, 1:2, :] = query_ids[...].astype(F32)
    owner = lax.broadcasted_iota(jnp.int32, (1, n_query), 1) // QLEN
    tags = jnp.zeros((1, n_query), F32)
    for query in range(n_query // QLEN):
        tags = jnp.where(owner == query, query_batch[query].astype(F32), tags)
    known[0, 2:3, :] = tags
    finish_all(puts)


def forward_two(
    low, normed_one, expand, reduce, expand_bias, gains, biases, term_weight, term_bias,
    hidden_out, slope_out, normed_out, inverse_two, pre, passage_out,
    low_here, one_here, expand_here, reduce_here, hidden, slope, normed_two, second, total, sems, out_sems,
):
    count = second.shape[0]
    wide = 2 * BLOCK
    blocks = expand.shape[1] // wide
    rows = pl.ds(0, count)
    low_copy = fetch([(low.at[rows, :], low_here)], sems)[0]
    chunks = fetch([(expand.at[:, columns(j, wide)], expand_here.at[:, columns(j, wide)]) for j in range(blocks)], sems, 1)
    late = fetch([(reduce, reduce_here), (normed_one.at[rows, :], one_here)], sems, 1 + blocks)
    low_copy.wait()
    puts = []
    for j in range(blocks):
        chunks[j].wait()
        cols = columns(j, wide)
        grow(low_here, 0, count, expand_here, cols, expand_bias, hidden, slope)
        first = j * (wide // TILE)
        puts += fetch([by_piece(first + i, hidden, hidden_out) for i in range(wide // TILE)], out_sems, first)
        puts += fetch([(slope.at[:, cols], slope_out.at[:, cols])], out_sems, blocks * (wide // TILE) + j)
    late[0].wait()
    total[...] = dot(hidden[...], reduce_here[...])
    late[1].wait()
    base = blocks * (wide // TILE) + blocks

    def tell(i, tile):
        puts.extend(
            fetch([(normed_two.at[tile, :], normed_out.at[tile, :]), (second.at[tile, :], passage_out.at[tile, :])], out_sems, base + 2 * i)
        )

    close_forward(
        total, one_here, 0, count, gains, biases, term_weight, term_bias, normed_two, inverse_two, pre, second, tell
    )
    finish_all(puts)


def match(here, known, score_grad, passage_ids, pre, scores, pass_grad, query_part):
    members, _, tokens = known.shape
    n_pass = passage_ids.shape[1]
    slots = scores.shape[1]
    per_query = scores.shape[0] // members
    slot = lax.broadcasted_iota(jnp.int32, (n_pass, slots), 0) // here[0]
    table = slot == lax.broadcasted_iota(jnp.int32, (n_pass, slots), 1)
    placed = jnp.where(table, softplus(pre[...]), 0.0).astype(BF16)
    who = lax.broadcasted_iota(jnp.int32, scores.shape[:1] + (tokens,), 0)
    token = lax.broadcasted_iota(jnp.int32, scores.shape[:1] + (tokens,), 1) // QLEN
    mine = jnp.broadcast_to(passage_ids[...].astype(F32), (8, n_pass)).T[:, 0:1]

    def member(b, carry):
        scored, placed_grads = carry
        facts = known[b]
        matches = jnp.where(mine == facts[1:2, :], 1.0, 0.0).astype(BF16)
        per_token = dot_tn(placed, matches)
        masked = jnp.where(facts[2:3, :] == here[1].astype(F32), 1.0, 0.0)
        weighted = facts[0:1, :] * masked
        spread = jnp.where(who == token + b * per_query, 1.0, 0.0)
        grad = lax.dot_general(
            score_grad[...], spread, (((0,), (0,)), ((), ())), preferred_element_type=F32, precision=HIGH
        )
        placed_grads = placed_grads + dot_nt(matches, (grad * weighted).astype(BF16))
        scored = scored + dot_nt(spread, per_token * weighted, HIGH)
        query_part[b] = row_sum(grad * per_token) * masked
        return scored, placed_grads

    scored, placed_grads = lax.fori_loop(
        0, members, member, (jnp.zeros(scores.shape, F32), jnp.zeros((n_pass, slots), F32)), unroll=min(members, 8)
    )
    scores[...] = scored
    pass_grad[...] = jnp.sum(jnp.where(table, placed_grads, 0.0), axis=1, keepdims=True)


def backward_rows(
    with_out, first, term_grad, pre, out_grad, normed_two, inverse_two, slope, normed_one, inverse_one, low_one, expand, reduce,
    gains, biases, term_weight,
    reduce_turned, expanded_grad, low_turned, sum_one, branch_grad, sums, expand_shift,
    grad_here, two_here, slope_here, one_here, low_here, expand_here, reduce_here, grown, turned, low_side, sum_here, branch_here,
    sum_two, reduce_out_grad, sems, out_sems,
):
    count, width = branch_grad.shape
    deep = slope.shape[1]
    wide = 2 * BLOCK
    blocks = deep // wide
    here = pl.ds(first, count)
    early = [
        fetch(
            [(normed_two.at[tile, :], two_here.at[tile, :])]
            + ([(out_grad.at[tile, :], grad_here.at[tile, :])] if with_out else []),
            sems,
            2 * i,
        )
        for i, tile in enumerate(tiles(count))
    ]
    base = 2 * (count // TILE)
    chunks = [
        fetch(
            [
                (reduce.at[columns(j, wide), :], reduce_here.at[columns(j, wide), :]),
                (slope.at[:, columns(j, wide)], slope_here.at[:, columns(j, wide)]),
            ],
            sems,
            base + 2 * j,
        )
        for j in range(blocks)
    ]
    base += 2 * blocks
    late = fetch([(low_one.at[here, :], low_here), (expand, expand_here), (normed_one.at[here, :], one_here)], sems, base)
    if not with_out:
        spread = jnp.broadcast_to(term_grad[...], (TILE, count)).T
    totals = [jnp.zeros((1, width), F32) for _ in range(8)]
    for i, tile in enumerate(tiles(count)):
        grad_in = term_grad[tile, :] if with_out else spread[:, 0:1]
        pre_grad = grad_in * sigmoid(pre[tile, :])
        finish_all(early[i])
        unit = two_here[tile, :]
        second_grad = pre_grad * term_weight[...]
        if with_out:
            second_grad = second_grad + grad_here[tile, :].astype(F32)
        back = norm_backward(second_grad * gains[1:2, :], unit, inverse_two[tile, :])
        rounded = back.astype(BF16)
        sum_two[tile, :] = back
        reduce_out_grad[tile, :] = rounded
        totals[1] = totals[1] + row_sum(second_grad * unit)
        totals[3] = totals[3] + row_sum(rounded.astype(F32))
        totals[5] = totals[5] + row_sum(second_grad)
        totals[6] = totals[6] + row_sum(pre_grad * (unit * gains[1:2, :] + biases[5:6, :]))
        totals[7] = totals[7] + row_sum(jnp.broadcast_to(pre_grad, (TILE, width)))
    turned[...] = reduce_out_grad[...].T
    puts = fetch([(turned, reduce_turned)], out_sems)
    for j in range(blocks):
        cols = columns(j, wide)
        finish_all(chunks[j])
        grad = dot_nt(reduce_out_grad[...], reduce_here[cols, :]) * slope_here[:, cols].astype(F32)
        rounded = grad.astype(BF16)
        grown[:, cols] = rounded
        expand_shift[:, cols] = row_sum(rounded.astype(F32))
        puts += fetch([(grown.at[:, cols], expanded_grad.at[:, cols])], out_sems, 1 + j)
    late[0].wait()
    low_side[...] = low_here[...].T
    puts += fetch([(low_side, low_turned)], out_sems, 1 + blocks)
    late[1].wait()
    sum_two[...] = sum_two[...] + dot_nt(grown[...], expand_here[...])
    late[2].wait()
    for i, tile in enumerate(tiles(count)):
        first_grad = sum_two[tile, :]
        unit = one_here[tile, :]
        back = norm_backward(first_grad * gains[0:1, :], unit, inverse_one[first + tile.start : first + tile.stop, :])
        rounded = back.astype(BF16)
        sum_here[tile, :] = back
        branch_here[tile, :] = rounded
        puts += fetch(
            [(sum_here.at[tile, :], sum_one.at[tile, :]), (branch_here.at[tile, :], branch_grad.at[tile, :])], out_sems, 2 + blocks + 2 * i
        )
        totals[0] = totals[0] + row_sum(first_grad * unit)
        totals[2] = totals[2] + row_sum(rounded.astype(F32))
        totals[4] = totals[4] + row_sum(first_grad)
    for i, total in enumerate(totals):
        sums[i : i + 1, :] = total
    finish_all(puts)


def attend_backward(mixed, attended_grad, stats, inner, mixed_grad, logit_grads, first, count, width, mask, tell):
    rows = slice(first, first + count)
    step = min(BLOCK, count)

    def pair(hp, carry):
        query = mixed[rows, columns(hp, 2 * HEAD)]
        grad = attended_grad[rows, columns(hp, 2 * HEAD)]
        query_grad = jnp.zeros((count, 2 * HEAD), F32)
        kept = []
        for sub in (0, 1):
            lanes = head_lanes(sub)
            total = stats[2 * hp + sub, :, rows]
            level = inner[2 * hp + sub, :, rows]
            for at in range(0, count, step):
                tile = slice(at, at + step)
                here = slice(first + at, first + at + step)
                key = mixed[here, columns(hp, 2 * HEAD, width)]
                value = mixed[here, columns(hp, 2 * HEAD, 2 * width)]
                key_here = jnp.where(lanes, key, jnp.zeros_like(key))
                value_here = jnp.where(lanes, value, jnp.zeros_like(value))
                weights = jnp.exp(dot_nt(key_here, query) + (mask[tile, :] - total))
                logit_grad = (weights * (dot_nt(value_here, grad) - level)).astype(BF16)
                logit_grads[sub, tile, 0:count] = logit_grad
                kept.append((dot(logit_grad, query), dot(weights.astype(BF16), grad)))
        for i, at in enumerate(range(0, count, step)):
            here = slice(first + at, first + at + step)
            for part in (0, 1):
                mixed_grad[here, columns(hp, 2 * HEAD, (part + 1) * width)] = jnp.where(
                    head_lanes(0), kept[i][part], kept[i + count // step][part]
                ).astype(BF16)
        for sub in (0, 1):
            key = mixed[rows, columns(hp, 2 * HEAD, width)]
            key_here = jnp.where(head_lanes(sub), key, jnp.zeros_like(key))
            query_grad = query_grad + dot_tn(logit_grads[sub, 0:count, 0:count], key_here)
        mixed_grad[rows, columns(hp, 2 * HEAD)] = (query_grad * SCALE).astype(BF16)
        tell(hp)
        return carry

    lax.fori_loop(0, HEADS // 2, pair, 0)


def backward_attention(
    length, passages, queries, pass_grad, query_grad, project_out, mixed, attended, stats,
    grad_out, turned_out, shifts,
    out_here, pass_here, query_here, mixed_here, attended_here, mixed_grad, turned,
    attended_grad, inner, logit_grads, mask, query_mask, sems, out_sems,
):
    n_pass, width = passages.shape
    n_query = queries.shape[0]
    count = n_pass + n_query
    copies = fetch(
        [(project_out, out_here), (pass_grad, pass_here), (query_grad, query_here), (attended, attended_here), (mixed, mixed_here)],
        sems,
    )
    query_mask[...] = same_slot(n_query, QLEN)
    mask[...] = same_slot(n_pass, length[0])
    turned[:, 0:n_pass] = passages[...].T
    turned[:, n_pass:count] = queries[...].T
    puts = fetch([(turned, turned_out)], out_sems)
    finish_all(copies[:3])
    attended_grad[0:n_pass, :] = dot_nt(pass_here[...], out_here[...]).astype(BF16)
    attended_grad[n_pass:count, :] = dot_nt(query_here[...], out_here[...]).astype(BF16)
    heads = 16
    owner = lax.broadcasted_iota(jnp.int32, (heads, width), 1) // HEAD
    spread = jnp.where(owner == lax.broadcasted_iota(jnp.int32, (heads, width), 0), 1.0, 0.0)
    copies[3].wait()
    for tile in tiles(count):
        product = attended_grad[tile, :].astype(F32) * attended_here[tile, :].astype(F32)
        levels = dot_nt(spread, product, HIGH)
        for head in range(HEADS):
            inner[head, :, tile] = levels[head : head + 1, :]
    copies[4].wait()
    attend_backward(
        mixed_here, attended_grad, stats, inner, mixed_grad, logit_grads, n_pass, n_query, width, query_mask, lambda hp: None
    )
    late = slice(n_pass, count)
    puts += fetch([(mixed_grad.at[late, :], grad_out.at[late, :])], out_sems, 1)

    def columns_of(hp):
        return [
            (mixed_grad.at[0:n_pass, columns(hp, 2 * HEAD, part * width)], grad_out.at[0:n_pass, columns(hp, 2 * HEAD, part * width)])
            for part in range(3)
        ]

    attend_backward(
        mixed_here, attended_grad, stats, inner, mixed_grad, logit_grads, 0, n_pass, width, mask,
        lambda hp: fetch(columns_of(hp), out_sems, 2 + 3 * hp),
    )
    for i, first in enumerate((0, 2 * width)):
        shifts[i : i + 1, :] = row_sum(mixed_grad[:, first : first + width].astype(F32))
    for hp in range(HEADS // 2):
        for part, (source, target) in enumerate(columns_of(hp)):
            pltpu.make_async_copy(source, target, out_sems.at[2 + 3 * hp + part]).wait()
    finish_all(puts)


def backward_input(
    mixed_grad, pass_sum, query_sum, project_in, pass_out, query_out, grad_here, pass_here, query_here, in_here, sems
):
    n_pass, width = pass_out.shape
    blocks = width // BLOCK
    copies = fetch(
        [(mixed_grad, grad_here), (pass_sum, pass_here), (query_sum, query_here)]
        + [(project_in.at[columns(j, BLOCK), :], in_here.at[columns(j, BLOCK), :]) for j in range(blocks)],
        sems,
    )
    finish_all(copies[:3])
    for j in range(blocks):
        cols = columns(j, BLOCK)
        copies[3 + j].wait()
        weight = in_here[cols, :]
        pass_out[:, cols] = (dot_nt(grad_here[0:n_pass, :], weight) + pass_here[:, cols]).astype(BF16)
        query_out[:, cols] = (dot_nt(grad_here[n_pass:, :], weight) + query_here[:, cols]).astype(BF16)


def inner_piece(members, piece, core, refs, emit):
    low_pass, low_query, grad_pass, grad_query, reduce_pass, reduce_query, hidden_pass, hidden_query = refs[:8]
    low, grad_p, grad_q, turn_p, turn_q, hid_p, hid_q, sems = refs[8:]
    width = low_pass.shape[0]
    n_pass = grad_pass.shape[0]
    spread = grad_pass.shape[1]
    shard = width // members
    cols = pl.ds(pl.multiple_of(core * (spread // 2) + piece * (spread // 6), TILE), spread // 6)
    half = pl.ds(pl.multiple_of(core * (width // 2), TILE), width // 2)
    copies = fetch(
        [
            (low_pass, low.at[:, 0:n_pass]), (low_query, low.at[:, n_pass:]),
            (grad_pass.at[:, cols], grad_p), (grad_query.at[:, cols], grad_q),
            (reduce_pass.at[half, :], turn_p), (reduce_query.at[half, :], turn_q),
            (hidden_pass.at[piece], hid_p), (hidden_query.at[piece], hid_q),
        ],
        sems,
    )
    finish_all(copies[:4])
    for first in range(0, width, width // 2):
        rows = slice(first, first + width // 2)
        part = dot(low[rows, 0:n_pass], grad_p[...]) + dot(low[rows, n_pass:], grad_q[...])
        for at in range(0, width // 2, shard // 2):
            leaf, side = divmod((first + at) // (shard // 2), 2)
            for block in range(spread // 6 // TILE):
                emit(leaf, side, block * (shard // 2), part[at : at + shard // 2, block * TILE : (block + 1) * TILE])
    base = (shard // 2) * (spread // 6 // TILE)
    finish_all(copies[4:])
    for leaf in range(0, members, 4):
        span = slice(leaf * TILE, (leaf + 4) * TILE)
        part = dot(turn_p[...], hid_p[:, span]) + dot(turn_q[...], hid_q[:, span])
        for i in range(4):
            for side in (0, 1):
                emit(leaf + i, side, base, part[side * (width // 4) : (side + 1) * (width // 4), i * TILE : (i + 1) * TILE])


def outer_piece(members, piece, core, refs, emit):
    turned, mixed_grad, attended, branch_pass, branch_query = refs[:5]
    rows_here, grad, attended_here, branch_p, branch_q, sems = refs[5:]
    width = turned.shape[0]
    n_pass = branch_pass.shape[0]
    shard = width // members
    wide = width // 2
    cols = pl.ds(pl.multiple_of(core * 3 * wide + piece * wide, TILE), wide)
    narrow = pl.ds(pl.multiple_of(core * wide + piece * TILE, TILE), TILE)
    copies = fetch(
        [
            (turned, rows_here), (mixed_grad.at[:, cols], grad), (attended, attended_here),
            (branch_pass.at[:, narrow], branch_p), (branch_query.at[:, narrow], branch_q),
        ],
        sems,
    )
    finish_all(copies[:2])

    def spread(first_block, make):
        for first in range(0, width, width // 2):
            part = make(slice(first, first + width // 2))
            for at in range(0, width // 2, shard // 2):
                leaf, side = divmod((first + at) // (shard // 2), 2)
                for lane in range(0, part.shape[1], TILE):
                    emit(leaf, side, (first_block + lane // TILE) * (shard // 2), part[at : at + shard // 2, lane : lane + TILE])

    spread(0, lambda rows: dot(rows_here[rows, :], grad[...]))
    finish_all(copies[2:])
    spread(
        wide // TILE,
        lambda rows: dot(attended_here[rows, 0:n_pass], branch_p[...]) + dot(attended_here[rows, n_pass:], branch_q[...]),
    )


def piece_out(make, given, piece, sides, *refs):
    out = refs[given]

    def emit(leaf, side, row, part):
        out[leaf, side, row : row + part.shape[0], :] = part

    make(piece, 1 - sides[0], refs[:given] + refs[given + 1 :], emit)


def piece_kept(make, given, piece, bit_at, sides, *refs):
    received, leaves, stays = refs[given : given + 3]
    came, both, own_sems = refs[-3:]
    arrival = fetch([(received, came)], own_sems)
    waited = []

    def emit(leaf, side, row, part):
        if not waited:
            finish_all(arrival)
            waited.append(True)
        index = 2 * leaf + side
        high, bit, rest = index >> (bit_at + 1), (index >> bit_at) & 1, index & ((1 << bit_at) - 1)
        here = jnp.where(sides[1] == bit, 0, 1)
        rows = slice(row, row + part.shape[0])
        both[here, (high << bit_at) + rest, rows, :] = part + came[leaf, side, rows, :]

    make(piece, sides[0], refs[:given] + refs[given + 3 : -3], emit)
    finish_all(fetch([(both.at[1], leaves), (both.at[0], stays)], own_sems, 1))


def finish_inner(sides, mine, near, other, beyond, expand, reduce):
    rows, wide = expand.shape
    half = rows // 2
    blocks = wide // 6 // TILE
    deep = reduce.shape[1] // 2
    for far, pair in enumerate(((mine, near), (other, beyond))):
        core = jnp.bitwise_xor(sides[0], far)
        for piece in range(3):
            for there, source in enumerate(pair):
                side = pl.multiple_of(jnp.bitwise_xor(sides[1], there) * half, 8)
                for block in range(blocks):
                    at = core * (wide // 2) + (piece * blocks + block) * TILE
                    expand[pl.ds(side, half), pl.ds(pl.multiple_of(at, TILE), TILE)] = source[
                        piece, block * half : (block + 1) * half, :
                    ]
            parts = [source[piece, blocks * half :, :] for source in pair]
            low = jnp.where(sides[1] == 0, parts[0], parts[1])
            high = jnp.where(sides[1] == 0, parts[1], parts[0])
            reduce[piece * TILE : (piece + 1) * TILE, pl.ds(pl.multiple_of(core * deep, TILE), deep)] = (
                jnp.concatenate([low, high]).T
            )


def finish_outer(sides, mine, near, other, beyond, project_in, project_out):
    rows, wide = project_in.shape
    half = rows // 2
    for far, pair in enumerate(((mine, near), (other, beyond))):
        core = jnp.bitwise_xor(sides[0], far)
        for there, source in enumerate(pair):
            side = pl.multiple_of(jnp.bitwise_xor(sides[1], there) * half, 8)
            for piece in range(3):
                for block in range(4):
                    part = source[piece, block * half : (block + 1) * half, :]
                    if block < 3:
                        at = core * (wide // 2) + (piece * 3 + block) * TILE
                        project_in[pl.ds(side, half), pl.ds(pl.multiple_of(at, TILE), TILE)] = part
                    else:
                        at = core * (wide // 6) + piece * TILE
                        project_out[pl.ds(side, half), pl.ds(pl.multiple_of(at, TILE), TILE)] = part


def run(kernel, outs, kinds, scratch, us, args, after=(), limit=58):
    specs = {"s": IN_SMEM, "v": IN_VMEM, "h": IN_PLACE}
    shapes = [jax.ShapeDtypeStruct(dims, dtype) for _, dims, dtype in outs]
    given = [
        pltpu.with_memory_space_constraint(a, pltpu.HBM) if kind == "h" else a for a, kind in zip(args, kinds)
    ]
    many = len(outs) > 1
    known = len(args)

    def body(*refs):
        kernel(*refs[:known], *refs[known + len(after) :])

    return pl.pallas_call(
        body,
        out_shape=shapes if many else shapes[0],
        in_specs=[specs[kind] for kind in kinds] + [IN_PLACE] * len(after),
        out_specs=[specs[o[0]] for o in outs] if many else specs[outs[0][0]],
        scratch_shapes=scratch,
        compiler_params=pltpu.CompilerParams(vmem_limit_bytes=limit << 20),
        cost_estimate=pl.CostEstimate(flops=0, bytes_accessed=1024, transcendentals=0),
    )(*given, *[pltpu.with_memory_space_constraint(a, pltpu.HBM) for a in after])


def contract_rows(left, right):
    return lax.dot_general(
        left, right, (((0,), (0,)), ((), ())), preferred_element_type=F32
    )


GROUP_FIRST = (("pb", 2), ("pa", 1))
ROW_FIRST = (("pa", 1), ("pb", 2))


def swap(value, axis, distance):
    return lax.ppermute(
        value, axis, [(i, i ^ distance) for i in range(lax.axis_size(axis))]
    )


def bit(axis, distance):
    return (lax.axis_index(axis) >> (distance.bit_length() - 1)) & 1


def pick(value, index, dim):
    return lax.dynamic_index_in_dim(value, index, dim, keepdims=False)


def group_gather(mine):
    distance = 1
    while distance < lax.axis_size("pa"):
        other = swap(mine, "pa", distance)
        mine = jnp.where(
            bit("pa", distance) == 0, jnp.concatenate([mine, other]), jnp.concatenate([other, mine])
        )
        distance *= 2
    return mine


def group_scatter(whole):
    distance = lax.axis_size("pa") // 2
    while distance:
        halves = whole.reshape((2, -1) + whole.shape[1:])
        mine = bit("pa", distance)
        whole = pick(halves, mine, 0) + swap(pick(halves, 1 - mine, 0), "pa", distance)
        distance //= 2
    return whole


def steps_of(order):
    steps = [(axis, distance) for axis, distance in order]
    distance = 2
    while distance < lax.axis_size("pa"):
        steps.append(("pa", distance))
        distance *= 2
    return steps


def tree_sum(send, keep, order):
    names = []
    distance = lax.axis_size("pa") // 2
    while distance:
        names.append(("pa", distance))
        distance //= 2
    names.append(("pb", 2))
    received = swap(send, "pb", 1)
    for axis, distance in steps_of(order):
        dim = names.index((axis, distance))
        names.pop(dim)
        mine = bit(axis, distance)
        send = pick(keep, 1 - mine, dim) + pick(received, 1 - mine, dim)
        keep = pick(keep, mine, dim) + pick(received, mine, dim)
        received = swap(send, axis, distance)
    mine = keep + received
    other = swap(mine, "pb", 2)
    high = bit("pb", 2)
    return jnp.where(high == 0, jnp.stack([mine, other]), jnp.stack([other, mine]))


def cut(matrix):
    bits = lax.axis_size("pa").bit_length() - 1
    rows = matrix.shape[0] >> (bits + 1)
    return matrix.reshape((2,) * (bits + 1) + (rows, matrix.shape[1]))


def summed_rows(left, right, order):
    core = bit("pb", 1)
    half = right.shape[1] // 2
    parts = [
        cut(contract_rows(left, lax.dynamic_slice_in_dim(right, side * half, half, axis=1)))
        for side in (1 - core, core)
    ]
    mine = tree_sum(parts[0], parts[1], order)
    mine = mine.reshape(-1, half)
    other = swap(mine, "pb", 1)
    return jnp.where(
        core == 0, jnp.concatenate([mine, other], 1), jnp.concatenate([other, mine], 1)
    )


def total_of_all(value):
    distance = 1
    while distance < lax.axis_size("pb"):
        value = value + swap(value, "pb", distance)
        distance *= 2
    distance = 1
    while distance < lax.axis_size("pa"):
        value = value + swap(value, "pa", distance)
        distance *= 2
    return value


LEAF_BITS = (("pa", 4), ("pa", 2), ("pa", 1), ("pb", 2))
PIECE_ORDERS = (
    (("pb", 2), ("pa", 1), ("pa", 2), ("pa", 4)),
    (("pa", 1), ("pb", 2), ("pa", 2), ("pa", 4)),
    (("pa", 2), ("pa", 4), ("pb", 2), ("pa", 1)),
)


def open_exchange(make, args, scratch, members, rows, times, after_send=(), after_keep=()):
    core = bit("pb", 1)
    leaves = 2 * members
    kinds = "s" + "h" * len(args)
    dims = (members, 2, rows, TILE)
    received = []
    for piece in range(3):
        sent = run(
            partial(piece_out, make, len(args), piece), [("v", dims, F32)], kinds, scratch, times[0],
            (jnp.stack([core, core]),) + args, after_send,
        )
        received.append(swap(sent, "pb", 1))
    held = []
    sent = []
    for piece, order in enumerate(PIECE_ORDERS):
        axis, distance = order[0]
        place = LEAF_BITS.index(order[0])
        sides = jnp.stack([core, bit(axis, distance)])
        half = ("h", (leaves // 2, rows, TILE), F32)
        leaving, staying = run(
            partial(piece_kept, make, len(args), piece, len(LEAF_BITS) - 1 - place),
            [half, half],
            kinds + "h",
            scratch
            + [pltpu.VMEM(dims, F32), pltpu.VMEM((2, leaves // 2, rows, TILE), F32), pltpu.SemaphoreType.DMA((3,))],
            times[1],
            (sides,) + args + (received[piece],),
            after_keep,
        )
        names = [b for b in LEAF_BITS if b != order[0]]
        held.append((names, staying, swap(leaving, axis, distance)))
        sent.append(leaving)
    return held, tuple(sent)


def advance(held, step, rows):
    moved = []
    sent = []
    for (names, staying, came), order in zip(held, PIECE_ORDERS):
        axis, distance = order[step]
        dim = names.index(order[step])
        dims = (2,) * len(names) + (rows, TILE)
        mine = bit(axis, distance)
        staying, came = staying.reshape(dims), came.reshape(dims)
        leaving = pick(staying, 1 - mine, dim) + pick(came, 1 - mine, dim)
        staying = pick(staying, mine, dim) + pick(came, mine, dim)
        moved.append((names[:dim] + names[dim + 1 :], staying, swap(leaving, axis, distance)))
        sent.append(leaving)
    return moved, tuple(sent)


def close_exchange(held):
    return jnp.stack([staying + came for _, staying, came in held])


def arrived(held):
    return tuple(came for _, _, came in held)


def on_device(
    passages, queries, passage_ids, query_ids, batch_length, query_batch, project_in, project_out, expand_weight,
    expand_bias, reduce_weight, norm_gains, biases, term_weight, term_bias, out_grad, score_grad,
):
    members = lax.axis_size("pa")
    member_index = lax.axis_index("pa")
    core = bit("pb", 1)
    local_batch = member_index // (members // BATCH_PB)
    length = lax.dynamic_slice_in_dim(
        batch_length, lax.axis_index("pb") * BATCH_PB + local_batch, 1, axis=0
    )
    n_pass, width = passages.shape
    n_query = queries.shape[0]
    count = n_pass + n_query
    deep = expand_weight.shape[1]
    slots = score_grad.shape[1]
    bias_row = expand_bias[None]
    term_row = term_weight[None]

    blocks = deep // (2 * BLOCK)
    by_three = (3, n_pass, deep // 3)
    weights = [pltpu.VMEM(expand_weight.shape, BF16), pltpu.VMEM(reduce_weight.shape, BF16)]

    def vmem(*dims, dtype=BF16):
        return pltpu.VMEM(dims, dtype)

    def sems(number):
        return pltpu.SemaphoreType.DMA((number,))

    (
        mixed, attended, attended_turned, stats, normed_one, inverse_one, low,
        hidden_query, slope_query, unit_query, scale_query, pre_query, known,
    ) = run(
        forward_one,
        [
            ("h", (count, 3 * width), BF16), ("h", (count, width), BF16),
            ("h", (width, count), BF16), ("v", (HEADS, 1, count), F32), ("h", (count, width), F32),
            ("v", (count, 1), F32), ("h", (count, width), BF16), ("h", (3, n_query, deep // 3), BF16),
            ("h", (n_query, deep), BF16), ("v", (n_query, width), F32), ("v", (n_query, 1), F32),
            ("v", (n_query, 1), F32), ("v", (1, 3, n_query), F32),
        ],
        "svvhhhhvvvvsvs",
        [
            vmem(*project_in.shape), vmem(*project_out.shape), *weights, vmem(count, 3 * width), vmem(count, width),
            vmem(width, count), vmem(count, width, dtype=F32), vmem(count, width), vmem(n_query, deep), vmem(n_query, deep),
            vmem(n_pass, n_pass, dtype=F32), vmem(n_query, n_query, dtype=F32), vmem(count, width, dtype=F32),
            sems(6), sems(6 + deep // TILE),
        ],
        25,
        (length, passages, queries, project_in, project_out, expand_weight, reduce_weight, bias_row, norm_gains,
         biases, term_row, term_bias, query_ids[None], query_batch),
    )
    known = group_gather(known)
    hidden, slope, unit_pass, scale_pass, pre_pass, passage_out = run(
        forward_two,
        [
            ("h", by_three, BF16), ("h", (n_pass, deep), BF16), ("h", (n_pass, width), F32),
            ("v", (n_pass, 1), F32), ("v", (n_pass, 1), F32), ("h", (n_pass, width), BF16),
        ],
        "hhhhvvvvs",
        [
            vmem(n_pass, width), vmem(n_pass, width, dtype=F32), *weights, vmem(n_pass, deep), vmem(n_pass, deep),
            vmem(n_pass, width, dtype=F32), vmem(n_pass, width), vmem(n_pass, width, dtype=F32),
            sems(3 + blocks), sems(deep // TILE + blocks + 2 * (n_pass // TILE)),
        ],
        12,
        (low, normed_one, expand_weight, reduce_weight, bias_row, norm_gains, biases, term_row, term_bias),
    )
    scores, pass_term_grad, query_part = run(
        match,
        [("v", score_grad.shape, F32), ("v", (n_pass, 1), F32), ("v", (members, 1, n_query), F32)],
        "svvvv",
        [],
        5,
        (jnp.concatenate([length, local_batch.reshape(1)]), known, score_grad, passage_ids[None], pre_pass),
    )
    query_term_grad = group_scatter(query_part)

    def back(with_out, term_grad, pre, unit, scale, slope_here, first, rows):
        return run(
            partial(backward_rows, with_out, first),
            [
                ("h", (width, rows), BF16), ("h", (rows, deep), BF16), ("h", (width, rows), BF16),
                ("h", (rows, width), F32), ("h", (rows, width), BF16), ("v", (8, width), F32), ("v", (1, deep), F32),
            ],
            "vvhhvhhvhhhvvv",
            [
                vmem(rows, width), vmem(rows, width, dtype=F32), vmem(rows, deep), vmem(rows, width, dtype=F32), vmem(rows, width),
                *weights, vmem(rows, deep), vmem(width, rows), vmem(width, rows), vmem(rows, width, dtype=F32), vmem(rows, width),
                vmem(rows, width, dtype=F32), vmem(rows, width),
                sems(3 + 2 * blocks + 2 * (rows // TILE)), sems(2 + blocks + 2 * (rows // TILE)),
            ],
            12 if with_out else 6,
            (term_grad if with_out else term_grad[0], pre, out_grad, unit, scale, slope_here, normed_one, inverse_one, low,
             expand_weight, reduce_weight, norm_gains, biases, term_row),
        )

    rg_pass, eg_pass, low_pass, one_pass, bg_pass, sums_pass, shift_pass = back(
        True, pass_term_grad, pre_pass, unit_pass, scale_pass, slope, 0, n_pass
    )
    rg_query, eg_query, low_query, one_query, bg_query, sums_query, shift_query = back(
        False, query_term_grad, pre_query, unit_query, scale_query, slope_query, n_pass, n_query
    )
    fits = deep // members == 3 * TILE
    if fits:
        rows = deep // 2 // 3 // TILE * (width // members // 2) + width // 4
        inner, inner_sent = open_exchange(
            partial(inner_piece, members),
            (low_pass, low_query, eg_pass, eg_query, rg_pass, rg_query, hidden, hidden_query),
            [
                vmem(width, count), vmem(n_pass, deep // 6), vmem(n_query, deep // 6), vmem(width // 2, n_pass),
                vmem(width // 2, n_query), vmem(n_pass, deep // 3), vmem(n_query, deep // 3), sems(8),
            ],
            members,
            rows,
            (4.5, 5),
        )
        inner_rows = rows
    else:
        inner_sent = outer_sent = ()
    mixed_grad, turned, mixed_shifts = run(
        backward_attention,
        [("h", (count, 3 * width), BF16), ("h", (width, count), BF16), ("v", (2, width), F32)],
        "svvhhhhhv",
        [
            vmem(*project_out.shape), vmem(n_pass, width), vmem(n_query, width), vmem(count, 3 * width), vmem(count, width),
            vmem(count, 3 * width), vmem(width, count), vmem(count, width), vmem(HEADS, 1, count, dtype=F32),
            vmem(2, n_pass, n_pass), vmem(n_pass, n_pass, dtype=F32), vmem(n_query, n_query, dtype=F32),
            sems(5), sems(2 + 3 * (HEADS // 2)),
        ],
        18,
        (length, passages, queries, bg_pass, bg_query, project_out, mixed, attended, stats),
        inner_sent,
    )
    if fits:
        rows = 4 * (width // members // 2)
        second, second_sent = advance(inner, 1, inner_rows)
        outer, outer_sent = open_exchange(
            partial(outer_piece, members),
            (turned, mixed_grad, attended_turned, bg_pass, bg_query),
            [
                vmem(width, count), vmem(count, width // 2), vmem(width, count), vmem(n_pass, TILE), vmem(n_query, TILE),
                sems(5),
            ],
            members,
            rows,
            (5, 6),
            arrived(inner) + second_sent,
            arrived(second),
        )
        outer_rows = rows
        third, third_sent = advance(second, 2, inner_rows)
        outer_sent += third_sent
    passage_grad, query_grad = run(
        backward_input,
        [("v", (n_pass, width), BF16), ("v", (n_query, width), BF16)],
        "hhhh",
        [
            vmem(count, 3 * width), vmem(n_pass, width, dtype=F32), vmem(n_query, width, dtype=F32), vmem(*project_in.shape),
            sems(3 + width // BLOCK),
        ],
        5,
        (mixed_grad, one_pass, one_query, project_in),
        outer_sent,
    )
    sums = sums_pass + sums_query
    vectors = total_of_all(
        jnp.concatenate([sums, mixed_shifts, (shift_pass + shift_query).reshape(-1, width)])
    )
    if fits:
        sides = jnp.stack([core, bit("pb", 2)])
        inner = advance(third, 3, inner_rows)[0]
        for step in (1, 2, 3):
            outer = advance(outer, step, outer_rows)[0]
        inner = close_exchange(inner)
        outer = close_exchange(outer)

        def finish(kernel, mine, outs):
            near = swap(mine, "pb", 2)
            args = (sides, mine, near, swap(mine, "pb", 1), swap(near, "pb", 1))
            return run(kernel, outs, "svvvv", [], 3, args)

        expand_total, reduce_total = finish(
            finish_inner, inner, [("v", (width // members, deep), F32), ("v", (deep // members, width), F32)]
        )
        in_total, out_total = finish(
            finish_outer, outer, [("v", (width // members, 3 * width), F32), ("v", (width // members, width), F32)]
        )
    else:
        in_order = [h.reshape(3, h.shape[1], -1, TILE).transpose(1, 2, 0, 3).reshape(-1, deep) for h in (hidden, hidden_query)]
        whole = [jnp.concatenate(pair, axis) for pair, axis in (
            (in_order, 0), ((rg_pass, rg_query), 1), ((eg_pass, eg_query), 0), ((bg_pass, bg_query), 0),
        )]
        reduce_total = summed_rows(whole[0], whole[1].T, ROW_FIRST)
        expand_total = summed_rows(low, whole[2], GROUP_FIRST)
        out_total = summed_rows(attended, whole[3], GROUP_FIRST)
        in_total = summed_rows(turned.T, mixed_grad, ROW_FIRST)
    share = width // members
    mine = lax.dynamic_slice_in_dim(vectors[:10], member_index * share, share, axis=1)
    expand_shift = lax.dynamic_slice_in_dim(
        vectors[10:].reshape(-1), member_index * (deep // members), deep // members
    )
    return (
        scores,
        passage_out,
        passage_grad,
        query_grad,
        in_total,
        out_total,
        expand_total,
        expand_shift,
        reduce_total,
        mine[:2],
        jnp.concatenate([mine[8:10], mine[2:6]]),
        mine[6],
        vectors[7, :1],
    )


def solution(mesh):
    return jax.shard_map(
        on_device,
        mesh=mesh,
        in_specs=(
            P(("pb", "pa"), None),
            P(("pb", "pa"), None),
            P(("pb", "pa")),
            P(("pb", "pa")),
            P(),
            P(("pb", "pa")),
            P(),
            P(),
            P(),
            P(),
            P(),
            P(),
            P(),
            P(),
            P(),
            P(("pb", "pa"), None),
            P("pb", "pa"),
        ),
        out_specs=(
            P("pb", "pa"),
            P(("pb", "pa"), None),
            P(("pb", "pa"), None),
            P(("pb", "pa"), None),
            P("pa", None),
            P("pa", None),
            P("pa", None),
            P("pa"),
            P("pa", None),
            P(None, "pa"),
            P(None, "pa"),
            P("pa"),
            P(),
        ),
        check_vma=False,
    )
```

```python
from functools import partial

import jax
import jax.numpy as jnp
from jax import lax
from jax.experimental import pallas as pl
from jax.experimental.pallas import tpu as pltpu
from jax.sharding import PartitionSpec as P

HEADS = 12
HEAD = 64
LONG = 512
QLEN = 32
BATCH_PB = 4

NEG = -1e30
HIGH = lax.Precision.HIGHEST
LN_EPS = 1e-12
SCALE = HEAD ** (-0.5)
BLOCK = 256
TILE = 128
F32 = jnp.float32
BF16 = jnp.bfloat16

IN_VMEM = pl.BlockSpec(memory_space=pltpu.VMEM)
IN_SMEM = pl.BlockSpec(memory_space=pltpu.SMEM)
IN_PLACE = pl.BlockSpec(memory_space=pl.ANY)


def shape(dims, dtype):
    return (tuple(dims), dtype)


def dot(left, right):
    return jnp.dot(left, right, preferred_element_type=F32)


def dot_nt(left, right, precision=None):
    return lax.dot_general(
        left, right, (((1,), (1,)), ((), ())), preferred_element_type=F32, precision=precision
    )


def dot_tn(left, right):
    return lax.dot_general(left, right, (((0,), (0,)), ((), ())), preferred_element_type=F32)


def columns(index, width, first=0):
    return pl.ds(pl.multiple_of(first + index * width, TILE), width)


def tiles(count):
    return [slice(first, first + TILE) for first in range(0, count, TILE)]


def row_sum(matrix):
    return jnp.sum(matrix, axis=0, keepdims=True)


def fetch(pairs, sems, first=0):
    copies = [
        pltpu.make_async_copy(source, target, sems.at[first + i]) for i, (source, target) in enumerate(pairs)
    ]
    for copy in copies:
        copy.start()
    return copies


def finish_all(copies):
    for copy in copies:
        copy.wait()


def norm_forward(total):
    centred = total - jnp.mean(total, axis=-1, keepdims=True)
    inverse = lax.rsqrt(jnp.mean(centred * centred, axis=-1, keepdims=True) + LN_EPS)
    return centred * inverse, inverse


def norm_backward(scaled, normed, inverse):
    centred = scaled - jnp.mean(scaled, axis=-1, keepdims=True)
    return inverse * (centred - normed * jnp.mean(scaled * normed, axis=-1, keepdims=True))


def head_lanes(sub):
    lane = lax.broadcasted_iota(jnp.int32, (1, 2 * HEAD), 1)
    return (lane // HEAD) == sub


def same_slot(count, length):
    rows = lax.broadcasted_iota(jnp.int32, (count, count), 0) // length
    cols = lax.broadcasted_iota(jnp.int32, (count, count), 1) // length
    return jnp.where(rows == cols, 0.0, NEG)


def attend(mixed, turned, stats, first, count, width, mask):
    rows = slice(first, first + count)

    def pair(hp, carry):
        key = mixed[rows, columns(hp, 2 * HEAD, width)]
        value = mixed[rows, columns(hp, 2 * HEAD, 2 * width)].T
        for sub in (0, 1):
            key_here = jnp.where(head_lanes(sub), key, jnp.zeros_like(key))
            logits = dot_nt(key_here, mixed[rows, columns(hp, 2 * HEAD)]) + mask[...]
            highest = jnp.max(logits, axis=0, keepdims=True)
            powers = jnp.exp(logits - highest)
            total = jnp.sum(powers, axis=0, keepdims=True)
            weights = (powers * (1.0 / total)).astype(BF16)
            out_rows = pl.ds(pl.multiple_of((2 * hp + sub) * HEAD, HEAD), HEAD)
            turned[out_rows, rows] = dot(value[sub * HEAD : (sub + 1) * HEAD], weights).astype(BF16)
            stats[2 * hp + sub, :, rows] = highest + jnp.log(total)
        return carry

    lax.fori_loop(0, HEADS // 2, pair, 0, unroll=2)


def grow(rows, first, count, expand, cols, expand_bias, hidden, slope):
    for at in range(0, count, min(BLOCK, count)):
        tile = slice(at, at + min(BLOCK, count))
        value = dot(rows[first + at : first + tile.stop, :], expand[:, cols]) + expand_bias[:, cols]
        lower = 0.5 + 0.5 * lax.erf(value * (0.5**0.5))
        hidden[tile, cols] = (value * lower).astype(BF16)
        density = jnp.exp(-0.5 * value * value) * 0.3989422804014327
        slope[tile, cols] = (lower + value * density).astype(BF16)


def by_piece(block, hidden, out):
    shard, piece = lax.div(block, 3), lax.rem(block, 3)
    return hidden.at[:, columns(block, TILE)], out.at[piece, :, columns(shard, TILE)]


def close_forward(total, normed_one, first, count, gains, biases, term_weight, term_bias, normed, inverse, pre, passage_out, tell):
    for i, tile in enumerate(tiles(count)):
        base = normed_one[first + tile.start : first + tile.stop, :] * gains[0:1, :] + biases[4:5, :]
        unit, scale = norm_forward(base + total[tile, :] + biases[3:4, :])
        normed[tile, :] = unit
        inverse[tile, :] = scale
        second = unit * gains[1:2, :] + biases[5:6, :]
        pre[tile, :] = jnp.sum(second * term_weight[...], axis=-1, keepdims=True) + term_bias[0]
        if passage_out is not None:
            passage_out[tile, :] = second.astype(BF16)
        tell(i, tile)


def softplus(value):
    return jnp.maximum(value, 0.0) + jnp.log1p(jnp.exp(-jnp.abs(value)))


def sigmoid(value):
    return 1.0 / (1.0 + jnp.exp(-value))


def forward_one(
    length, passages, queries, project_in, project_out, expand, reduce, expand_bias, gains, biases,
    term_weight, term_bias, query_ids, query_batch,
    mixed_out, attended_out, turned_out, stats, normed_out, inverse_one, low_out,
    hidden_out, slope_out, normed_two, inverse_two, pre, known,
    in_here, out_here, expand_here, reduce_here, mixed, attended, turned, normed_one, low, hidden, slope,
    mask, query_mask, total, sems, out_sems,
):
    n_pass, width = passages.shape
    n_query = queries.shape[0]
    count = n_pass + n_query
    parts = [slice(i * width, (i + 1) * width) for i in range(3)]
    copies = fetch(
        [(project_in.at[:, part], in_here.at[:, part]) for part in parts]
        + [(project_out, out_here), (expand, expand_here), (reduce, reduce_here)],
        sems,
    )
    mask[...] = same_slot(n_pass, length[0])
    query_mask[...] = same_slot(n_query, QLEN)
    for part in range(3):
        copies[part].wait()
        for source, first, rows in ((passages, 0, n_pass), (queries, n_pass, n_query)):
            value = dot(source[...], in_here[:, parts[part]])
            if part != 1:
                value = value + biases[part // 2 : part // 2 + 1, :]
            if part == 0:
                value = value * SCALE
            mixed[first : first + rows, parts[part]] = value.astype(BF16)
    puts = fetch([(mixed, mixed_out)], out_sems)
    attend(mixed, turned, stats, n_pass, n_query, width, query_mask)
    attend(mixed, turned, stats, 0, n_pass, width, mask)
    attended[...] = turned[...].T
    puts += fetch([(turned, turned_out), (attended, attended_out)], out_sems, 1)
    copies[3].wait()
    total[...] = dot(attended[...], out_here[...])
    for tile in reversed(tiles(count)):
        source, at = (passages, tile.start) if tile.start < n_pass else (queries, tile.start - n_pass)
        unit, scale = norm_forward(source[at : at + TILE, :].astype(F32) + total[tile, :] + biases[2:3, :])
        normed_one[tile, :] = unit
        inverse_one[tile, :] = scale
        low[tile, :] = (unit * gains[0:1, :] + biases[4:5, :]).astype(BF16)
    puts += fetch([(normed_one, normed_out), (low, low_out)], out_sems, 3)
    copies[4].wait()
    wide = 2 * BLOCK

    def block(j, carry):
        grow(low, n_pass, n_query, expand_here, columns(j, wide), expand_bias, hidden, slope)
        return carry

    lax.fori_loop(0, expand.shape[1] // wide, block, 0, unroll=2)
    puts += fetch(
        [by_piece(i, hidden, hidden_out) for i in range(expand.shape[1] // TILE)] + [(slope, slope_out)], out_sems, 5
    )
    copies[5].wait()
    total[0:n_query, :] = dot(hidden[...], reduce_here[...])
    close_forward(
        total, normed_one, n_pass, n_query, gains, biases, term_weight, term_bias, normed_two, inverse_two, pre, None,
        lambda i, tile: None,
    )
    known[0, 0:1, :] = jnp.broadcast_to(softplus(pre[...]), (n_query, TILE)).T[0:1, :]
    known[0, 1:2, :] = query_ids[...].astype(F32)
    owner = lax.broadcasted_iota(jnp.int32, (1, n_query), 1) // QLEN
    tags = jnp.zeros((1, n_query), F32)
    for query in range(n_query // QLEN):
        tags = jnp.where(owner == query, query_batch[query].astype(F32), tags)
    known[0, 2:3, :] = tags
    finish_all(puts)


def forward_two(
    low, normed_one, expand, reduce, expand_bias, gains, biases, term_weight, term_bias,
    hidden_out, slope_out, normed_out, inverse_two, pre, passage_out,
    low_here, one_here, expand_here, reduce_here, hidden, slope, normed_two, second, total, sems, out_sems,
):
    count = second.shape[0]
    wide = 2 * BLOCK
    blocks = expand.shape[1] // wide
    rows = pl.ds(0, count)
    low_copy = fetch([(low.at[rows, :], low_here)], sems)[0]
    chunks = fetch([(expand.at[:, columns(j, wide)], expand_here.at[:, columns(j, wide)]) for j in range(blocks)], sems, 1)
    late = fetch([(reduce, reduce_here), (normed_one.at[rows, :], one_here)], sems, 1 + blocks)
    low_copy.wait()
    puts = []
    for j in range(blocks):
        chunks[j].wait()
        cols = columns(j, wide)
        grow(low_here, 0, count, expand_here, cols, expand_bias, hidden, slope)
        first = j * (wide // TILE)
        puts += fetch([by_piece(first + i, hidden, hidden_out) for i in range(wide // TILE)], out_sems, first)
        puts += fetch([(slope.at[:, cols], slope_out.at[:, cols])], out_sems, blocks * (wide // TILE) + j)
    late[0].wait()
    total[...] = dot(hidden[...], reduce_here[...])
    late[1].wait()
    base = blocks * (wide // TILE) + blocks

    def tell(i, tile):
        puts.extend(
            fetch([(normed_two.at[tile, :], normed_out.at[tile, :]), (second.at[tile, :], passage_out.at[tile, :])], out_sems, base + 2 * i)
        )

    close_forward(
        total, one_here, 0, count, gains, biases, term_weight, term_bias, normed_two, inverse_two, pre, second, tell
    )
    finish_all(puts)


def match(here, known, score_grad, passage_ids, pre, scores, pass_grad, query_part):
    members, _, tokens = known.shape
    n_pass = passage_ids.shape[1]
    slots = scores.shape[1]
    per_query = scores.shape[0] // members
    slot = lax.broadcasted_iota(jnp.int32, (n_pass, slots), 0) // here[0]
    table = slot == lax.broadcasted_iota(jnp.int32, (n_pass, slots), 1)
    placed = jnp.where(table, softplus(pre[...]), 0.0).astype(BF16)
    who = lax.broadcasted_iota(jnp.int32, scores.shape[:1] + (tokens,), 0)
    token = lax.broadcasted_iota(jnp.int32, scores.shape[:1] + (tokens,), 1) // QLEN
    mine = jnp.broadcast_to(passage_ids[...].astype(F32), (8, n_pass)).T[:, 0:1]

    def member(b, carry):
        scored, placed_grads = carry
        facts = known[b]
        matches = jnp.where(mine == facts[1:2, :], 1.0, 0.0).astype(BF16)
        per_token = dot_tn(placed, matches)
        masked = jnp.where(facts[2:3, :] == here[1].astype(F32), 1.0, 0.0)
        weighted = facts[0:1, :] * masked
        spread = jnp.where(who == token + b * per_query, 1.0, 0.0)
        grad = lax.dot_general(
            score_grad[...], spread, (((0,), (0,)), ((), ())), preferred_element_type=F32, precision=HIGH
        )
        placed_grads = placed_grads + dot_nt(matches, (grad * weighted).astype(BF16))
        scored = scored + dot_nt(spread, per_token * weighted, HIGH)
        query_part[b] = row_sum(grad * per_token) * masked
        return scored, placed_grads

    scored, placed_grads = lax.fori_loop(
        0, members, member, (jnp.zeros(scores.shape, F32), jnp.zeros((n_pass, slots), F32)), unroll=min(members, 8)
    )
    scores[...] = scored
    pass_grad[...] = jnp.sum(jnp.where(table, placed_grads, 0.0), axis=1, keepdims=True)


def backward_rows(
    with_out, first, term_grad, pre, out_grad, normed_two, inverse_two, slope, normed_one, inverse_one, low_one, expand, reduce,
    gains, biases, term_weight,
    reduce_turned, expanded_grad, low_turned, sum_one, branch_grad, sums, expand_shift,
    grad_here, two_here, slope_here, one_here, low_here, expand_here, reduce_here, grown, turned, low_side, sum_here, branch_here,
    sum_two, reduce_out_grad, sems, out_sems, begin=lambda: None, then=lambda *made: [],
):
    count, width = branch_grad.shape
    deep = slope.shape[1]
    wide = 2 * BLOCK
    blocks = deep // wide
    here = pl.ds(first, count)
    early = [
        fetch(
            [(normed_two.at[tile, :], two_here.at[tile, :])]
            + ([(out_grad.at[tile, :], grad_here.at[tile, :])] if with_out else []),
            sems,
            2 * i,
        )
        for i, tile in enumerate(tiles(count))
    ]
    base = 2 * (count // TILE)
    chunks = [
        fetch(
            [
                (reduce.at[columns(j, wide), :], reduce_here.at[columns(j, wide), :]),
                (slope.at[:, columns(j, wide)], slope_here.at[:, columns(j, wide)]),
            ],
            sems,
            base + 2 * j,
        )
        for j in range(blocks)
    ]
    base += 2 * blocks
    late = fetch([(low_one.at[here, :], low_here), (expand, expand_here), (normed_one.at[here, :], one_here)], sems, base)
    begin()
    if not with_out:
        spread = jnp.broadcast_to(term_grad[...], (TILE, count)).T
    totals = [jnp.zeros((1, width), F32) for _ in range(8)]
    for i, tile in enumerate(tiles(count)):
        grad_in = term_grad[tile, :] if with_out else spread[:, 0:1]
        pre_grad = grad_in * sigmoid(pre[tile, :])
        finish_all(early[i])
        unit = two_here[tile, :]
        second_grad = pre_grad * term_weight[...]
        if with_out:
            second_grad = second_grad + grad_here[tile, :].astype(F32)
        back = norm_backward(second_grad * gains[1:2, :], unit, inverse_two[tile, :])
        rounded = back.astype(BF16)
        sum_two[tile, :] = back
        reduce_out_grad[tile, :] = rounded
        totals[1] = totals[1] + row_sum(second_grad * unit)
        totals[3] = totals[3] + row_sum(rounded.astype(F32))
        totals[5] = totals[5] + row_sum(second_grad)
        totals[6] = totals[6] + row_sum(pre_grad * (unit * gains[1:2, :] + biases[5:6, :]))
        totals[7] = totals[7] + row_sum(jnp.broadcast_to(pre_grad, (TILE, width)))
    turned[...] = reduce_out_grad[...].T
    puts = fetch([(turned, reduce_turned)], out_sems)
    for j in range(blocks):
        cols = columns(j, wide)
        finish_all(chunks[j])
        grad = dot_nt(reduce_out_grad[...], reduce_here[cols, :]) * slope_here[:, cols].astype(F32)
        rounded = grad.astype(BF16)
        grown[:, cols] = rounded
        expand_shift[:, cols] = row_sum(rounded.astype(F32))
        puts += fetch([(grown.at[:, cols], expanded_grad.at[:, cols])], out_sems, 1 + j)
    late[0].wait()
    low_side[...] = low_here[...].T
    puts += fetch([(low_side, low_turned)], out_sems, 1 + blocks)
    late[1].wait()
    sum_two[...] = sum_two[...] + dot_nt(grown[...], expand_here[...])
    late[2].wait()
    for i, tile in enumerate(tiles(count)):
        first_grad = sum_two[tile, :]
        unit = one_here[tile, :]
        back = norm_backward(first_grad * gains[0:1, :], unit, inverse_one[first + tile.start : first + tile.stop, :])
        rounded = back.astype(BF16)
        sum_here[tile, :] = back
        branch_here[tile, :] = rounded
        puts += fetch(
            [(sum_here.at[tile, :], sum_one.at[tile, :]), (branch_here.at[tile, :], branch_grad.at[tile, :])], out_sems, 2 + blocks + 2 * i
        )
        totals[0] = totals[0] + row_sum(first_grad * unit)
        totals[2] = totals[2] + row_sum(rounded.astype(F32))
        totals[4] = totals[4] + row_sum(first_grad)
    for i, total in enumerate(totals):
        sums[i : i + 1, :] = total
    puts += then(grown, turned, low_side)
    finish_all(puts)


def backward_query(members, first, sides, *refs):
    given, low_pass, grad_pass, reduce_pass, hidden_pass, hidden_query = refs[:14], *refs[14:19]
    made, sent = refs[19:26], refs[26:29]
    own, (low, grad, turn, hid_p, hid_q, buffers, sems, out_sems) = refs[29:45], refs[45:]
    core = 1 - sides[0]
    spread = grad_pass.shape[1]
    width = low_pass.shape[0]
    copies = []

    def begin():
        wide = pl.ds(pl.multiple_of(core * (spread // 2), TILE), spread // 2)
        half = pl.ds(pl.multiple_of(core * (width // 2), TILE), width // 2)
        pairs = [
            (low_pass, low), (grad_pass.at[:, wide], grad), (reduce_pass.at[half, :], turn),
            (hidden_pass, hid_p), (hidden_query, hid_q),
        ]
        copies.extend(fetch(pairs, sems))

    def then(grown, turned, low_side):
        finish_all(copies)
        puts = []
        for piece in range(3):

            def emit(leaf, side, row, part):
                buffers[piece, leaf, side, row : row + part.shape[0], :] = part

            def tell(rows, place):
                puts.extend(
                    fetch([(buffers.at[piece, :, :, rows, :], sent[piece].at[:, :, rows, :])], out_sems, 2 * piece + place)
                )

            third = spread // 6
            inner_leaves(
                members, low, low_side, grad.at[:, piece * third : (piece + 1) * third],
                grown.at[:, pl.ds(pl.multiple_of(core * (spread // 2) + piece * third, TILE), third)],
                turn, turned.at[pl.ds(pl.multiple_of(core * (width // 2), TILE), width // 2), :],
                hid_p.at[piece], hid_q.at[piece], emit, tell,
            )
        return puts

    backward_rows(False, first, *given, *made, *own, begin=begin, then=then)


def attend_backward(mixed, attended_grad, stats, inner, mixed_grad, logit_grads, first, count, width, mask, tell):
    rows = slice(first, first + count)
    step = min(BLOCK, count)

    def pair(hp, carry):
        query = mixed[rows, columns(hp, 2 * HEAD)]
        grad = attended_grad[rows, columns(hp, 2 * HEAD)]
        query_grad = jnp.zeros((count, 2 * HEAD), F32)
        kept = []
        for sub in (0, 1):
            lanes = head_lanes(sub)
            total = stats[2 * hp + sub, :, rows]
            level = inner[2 * hp + sub, :, rows]
            for at in range(0, count, step):
                tile = slice(at, at + step)
                here = slice(first + at, first + at + step)
                key = mixed[here, columns(hp, 2 * HEAD, width)]
                value = mixed[here, columns(hp, 2 * HEAD, 2 * width)]
                key_here = jnp.where(lanes, key, jnp.zeros_like(key))
                value_here = jnp.where(lanes, value, jnp.zeros_like(value))
                weights = jnp.exp(dot_nt(key_here, query) + (mask[tile, :] - total))
                logit_grad = (weights * (dot_nt(value_here, grad) - level)).astype(BF16)
                logit_grads[sub, tile, 0:count] = logit_grad
                kept.append((dot(logit_grad, query), dot(weights.astype(BF16), grad)))
        for i, at in enumerate(range(0, count, step)):
            here = slice(first + at, first + at + step)
            for part in (0, 1):
                mixed_grad[here, columns(hp, 2 * HEAD, (part + 1) * width)] = jnp.where(
                    head_lanes(0), kept[i][part], kept[i + count // step][part]
                ).astype(BF16)
        for sub in (0, 1):
            key = mixed[rows, columns(hp, 2 * HEAD, width)]
            key_here = jnp.where(head_lanes(sub), key, jnp.zeros_like(key))
            query_grad = query_grad + dot_tn(logit_grads[sub, 0:count, 0:count], key_here)
        mixed_grad[rows, columns(hp, 2 * HEAD)] = (query_grad * SCALE).astype(BF16)
        tell(hp)
        return carry

    lax.fori_loop(0, HEADS // 2, pair, 0)


def backward_attention(
    members, sides, length, passages, queries, pass_grad, query_grad, project_out, mixed, attended, stats,
    attended_turned, project_in, pass_sum, query_sum, sums_pass, sums_query, shift_pass, shift_query,
    grad_out, turned_out, vectors, pass_out, query_out, *rest,
):
    sent = rest[0] if members else None
    (
        out_here, pass_here, query_here, mixed_here, attended_here, mixed_grad, turned,
        attended_grad, inner, logit_grads, mask, query_mask, across_here, in_here, pass_sum_here, query_sum_here, buffers,
        sems, out_sems,
    ) = rest[-19:]
    n_pass, width = passages.shape
    n_query = queries.shape[0]
    count = n_pass + n_query
    copies = fetch(
        [
            (project_out, out_here), (pass_grad, pass_here), (query_grad, query_here), (attended, attended_here),
            (mixed, mixed_here), (attended_turned, across_here), (project_in, in_here), (pass_sum, pass_sum_here),
            (query_sum, query_sum_here),
        ],
        sems,
    )
    query_mask[...] = same_slot(n_query, QLEN)
    mask[...] = same_slot(n_pass, length[0])
    turned[:, 0:n_pass] = passages[...].T
    turned[:, n_pass:count] = queries[...].T
    puts = fetch([(turned, turned_out)], out_sems)
    finish_all(copies[:3])
    attended_grad[0:n_pass, :] = dot_nt(pass_here[...], out_here[...]).astype(BF16)
    attended_grad[n_pass:count, :] = dot_nt(query_here[...], out_here[...]).astype(BF16)
    heads = 16
    owner = lax.broadcasted_iota(jnp.int32, (heads, width), 1) // HEAD
    spread = jnp.where(owner == lax.broadcasted_iota(jnp.int32, (heads, width), 0), 1.0, 0.0)
    copies[3].wait()
    for tile in tiles(count):
        product = attended_grad[tile, :].astype(F32) * attended_here[tile, :].astype(F32)
        levels = dot_nt(spread, product, HIGH)
        for head in range(HEADS):
            inner[head, :, tile] = levels[head : head + 1, :]
    copies[4].wait()
    nothing = lambda hp: None
    attend_backward(mixed_here, attended_grad, stats, inner, mixed_grad, logit_grads, n_pass, n_query, width, query_mask, nothing)
    attend_backward(mixed_here, attended_grad, stats, inner, mixed_grad, logit_grads, 0, n_pass, width, mask, nothing)
    puts += fetch([(mixed_grad, grad_out)], out_sems, 1)
    shifts = [row_sum(mixed_grad[:, first : first + width].astype(F32)) for first in (0, 2 * width)]
    whole = jnp.concatenate([sums_pass[...] + sums_query[...], *shifts, jnp.zeros((6, width), F32)])
    deep_shift = shift_pass[...] + shift_query[...]
    if members:
        shard = width // members
        lane = lax.broadcasted_iota(jnp.int32, (width, TILE), 1)
        source = lax.broadcasted_iota(jnp.int32, (width, TILE), 0)
        row = lax.broadcasted_iota(jnp.int32, (16, TILE), 0)
        for leaf in range(members):
            chosen = jnp.where((source == lane + leaf * shard) & (lane < shard), 1.0, 0.0)
            block = jnp.dot(whole, chosen, preferred_element_type=F32, precision=HIGH)
            for i in range(3):
                part = deep_shift[:, (3 * leaf + i) * TILE : (3 * leaf + i + 1) * TILE]
                block = jnp.where(row == 10 + i, part, block)
            vectors[leaf] = block
        finish_all(copies[5:6])
        core = 1 - sides[0]
        wide = width // 2
        for piece in range(3):

            def emit(leaf, side, row, part):
                buffers[piece, leaf, side, row : row + part.shape[0], :] = part

            narrow = pl.ds(pl.multiple_of(core * wide + piece * TILE, TILE), TILE)
            outer_leaves(
                members, turned, mixed_grad.at[:, pl.ds(pl.multiple_of(core * 3 * wide + piece * wide, TILE), wide)],
                across_here, pass_here.at[:, narrow], query_here.at[:, narrow], emit,
            )
            vector_leaves(members, piece, core, vectors, buffers.shape[3] - 8, emit)
            puts += fetch([(buffers.at[piece], sent.at[piece])], out_sems, 2 + piece)
        late = copies[6:]
    else:
        vectors[0:16, :] = whole
        for i in range(deep_shift.shape[1] // width):
            vectors[16 + i : 17 + i, :] = deep_shift[:, i * width : (i + 1) * width]
        late = copies[5:]
    finish_all(late)
    for first in range(0, width, BLOCK):
        cols = slice(first, first + BLOCK)
        weight = in_here[cols, :]
        pass_out[:, cols] = (dot_nt(mixed_grad[0:n_pass, :], weight) + pass_sum_here[:, cols]).astype(BF16)
        query_out[:, cols] = (dot_nt(mixed_grad[n_pass:count, :], weight) + query_sum_here[:, cols]).astype(BF16)
    finish_all(puts)


def inner_leaves(members, low_p, low_q, grad_p, grad_q, turn_p, turn_q, hid_p, hid_q, emit, tell):
    width = low_p.shape[0]
    shard = width // members
    for first in range(0, width, width // 2):
        rows = slice(first, first + width // 2)
        part = dot(low_p[rows, :], grad_p[...]) + dot(low_q[rows, :], grad_q[...])
        for at in range(0, width // 2, shard // 2):
            leaf, side = divmod((first + at) // (shard // 2), 2)
            for block in range(part.shape[1] // TILE):
                emit(leaf, side, block * (shard // 2), part[at : at + shard // 2, block * TILE : (block + 1) * TILE])
    base = (shard // 2) * (grad_p.shape[1] // TILE)
    tell(slice(0, base), 0)
    for leaf in range(0, members, 4):
        span = slice(leaf * TILE, (leaf + 4) * TILE)
        part = dot(turn_p[...], hid_p[:, span]) + dot(turn_q[...], hid_q[:, span])
        for i in range(4):
            for side in (0, 1):
                emit(leaf + i, side, base, part[side * (width // 4) : (side + 1) * (width // 4), i * TILE : (i + 1) * TILE])
    tell(slice(base, base + width // 4), 1)


def outer_leaves(members, turned, grad, attended, branch_p, branch_q, emit):
    width = turned.shape[0]
    n_pass = branch_p.shape[0]
    shard = width // members
    for first in range(0, width, width // 2):
        rows = slice(first, first + width // 2)
        parts = [
            dot(turned[rows, :], grad[...]),
            dot(attended[rows, 0:n_pass], branch_p[...]) + dot(attended[rows, n_pass:], branch_q[...]),
        ]
        for at in range(0, width // 2, shard // 2):
            leaf, side = divmod((first + at) // (shard // 2), 2)
            block = 0
            for part in parts:
                for lane in range(0, part.shape[1], TILE):
                    emit(leaf, side, block * (shard // 2), part[at : at + shard // 2, lane : lane + TILE])
                    block += 1


def side_of(bit_at, mine, leaf, side):
    index = 2 * leaf + side
    high, bit, rest = index >> (bit_at + 1), (index >> bit_at) & 1, index & ((1 << bit_at) - 1)
    return jnp.where(mine == bit, 0, 1), (high << bit_at) + rest


def inner_kept(
    members, piece, bit_at, sides, low_pass, low_query, grad_pass, grad_query, reduce_pass, reduce_query, hidden_pass, hidden_query,
    received, leaves, stays,
    low_p, low_q, grad_p, grad_q, turn_p, turn_q, hid_p, hid_q, came, both, sems, out_sems,
):
    width = low_pass.shape[0]
    spread = grad_pass.shape[1]
    third = spread // 6
    cols = pl.ds(pl.multiple_of(sides[0] * (spread // 2) + piece * third, TILE), third)
    half = pl.ds(pl.multiple_of(sides[0] * (width // 2), TILE), width // 2)
    base = (width // members // 2) * (third // TILE)
    spans = [slice(0, base), slice(base, base + width // 4)]
    early = fetch(
        [
            (low_pass, low_p), (low_query, low_q), (grad_pass.at[:, cols], grad_p), (grad_query.at[:, cols], grad_q),
            (received.at[:, :, spans[0], :], came.at[:, :, spans[0], :]),
        ],
        sems,
    )
    late = fetch(
        [
            (reduce_pass.at[half, :], turn_p), (reduce_query.at[half, :], turn_q),
            (hidden_pass.at[piece], hid_p), (hidden_query.at[piece], hid_q),
            (received.at[:, :, spans[1], :], came.at[:, :, spans[1], :]),
        ],
        sems, 5,
    )
    puts = []

    def emit(leaf, side, row, part):
        rows = slice(row, row + part.shape[0])
        both[*side_of(bit_at, sides[1], leaf, side), rows, :] = part + came[leaf, side, rows, :]

    def tell(rows, place):
        pairs = [(both.at[1, :, rows, :], leaves.at[:, rows, :]), (both.at[0, :, rows, :], stays.at[:, rows, :])]
        puts.extend(fetch(pairs, out_sems, 2 * place))
        if place == 0:
            finish_all(late)

    finish_all(early)
    inner_leaves(members, low_p, low_q, grad_p, grad_q, turn_p, turn_q, hid_p, hid_q, emit, tell)
    finish_all(puts)


def outer_kept(
    members, places, sides, turned, mixed_grad, attended, branch_pass, branch_query, vectors, received, *refs
):
    leaves, stays = refs[0:6:2], refs[1:6:2]
    rows_here, grad, attended_here, branch_p, branch_q, came, both, sems, out_sems = refs[6:]
    width = turned.shape[0]
    wide = width // 2
    cols = pl.ds(pl.multiple_of(sides[0] * 3 * wide, TILE), 3 * wide)
    narrow = pl.ds(pl.multiple_of(sides[0] * wide, TILE), wide)
    copies = fetch(
        [
            (turned, rows_here), (mixed_grad.at[:, cols], grad), (attended, attended_here),
            (branch_pass.at[:, narrow], branch_p), (branch_query.at[:, narrow], branch_q),
        ]
        + [(received.at[piece], came.at[piece]) for piece in range(3)],
        sems,
    )
    finish_all(copies[:5])
    puts = []
    for piece in range(3):
        copies[5 + piece].wait()

        def emit(leaf, side, row, part):
            rows = slice(row, row + part.shape[0])
            both[piece, *side_of(places[piece], sides[1 + piece], leaf, side), rows, :] = part + came[piece, leaf, side, rows, :]

        outer_leaves(
            members, rows_here, grad.at[:, piece * wide : (piece + 1) * wide], attended_here,
            branch_p.at[:, piece * TILE : (piece + 1) * TILE], branch_q.at[:, piece * TILE : (piece + 1) * TILE], emit,
        )
        vector_leaves(members, piece, sides[0], vectors, both.shape[3] - 8, emit)
        puts += fetch([(both.at[piece, 1], leaves[piece]), (both.at[piece, 0], stays[piece])], out_sems, 2 * piece)
    finish_all(puts)


def vector_leaves(members, piece, core, vectors, row, emit):
    for leaf in range(members):
        for side in (0, 1):
            if piece == 0:
                part = jnp.where(core == 0, vectors[leaf, 8 * side : 8 * side + 8, :], 0.0)
            else:
                part = jnp.zeros((8, TILE), F32)
            emit(leaf, side, row, part)


def finish_inner(sides, mine, near, other, beyond, expand, reduce):
    rows, wide = expand.shape
    half = rows // 2
    blocks = wide // 6 // TILE
    deep = reduce.shape[1] // 2
    for far, pair in enumerate(((mine, near), (other, beyond))):
        core = jnp.bitwise_xor(sides[0], far)
        for piece in range(3):
            for there, source in enumerate(pair):
                side = pl.multiple_of(jnp.bitwise_xor(sides[1], there) * half, 8)
                for block in range(blocks):
                    at = core * (wide // 2) + (piece * blocks + block) * TILE
                    expand[pl.ds(side, half), pl.ds(pl.multiple_of(at, TILE), TILE)] = source[
                        piece, block * half : (block + 1) * half, :
                    ]
            parts = [source[piece, blocks * half :, :] for source in pair]
            low = jnp.where(sides[1] == 0, parts[0], parts[1])
            high = jnp.where(sides[1] == 0, parts[1], parts[0])
            reduce[piece * TILE : (piece + 1) * TILE, pl.ds(pl.multiple_of(core * deep, TILE), deep)] = (
                jnp.concatenate([low, high]).T
            )


def finish_outer(sides, mine, near, other, beyond, project_in, project_out, gains, biases, term_weight, term_bias, expand_bias):
    rows, wide = project_in.shape
    half = rows // 2
    for far, pair in enumerate(((mine, near), (other, beyond))):
        core = jnp.bitwise_xor(sides[0], far)
        for there, source in enumerate(pair):
            side = pl.multiple_of(jnp.bitwise_xor(sides[1], there) * half, 8)
            for piece in range(3):
                for block in range(4):
                    part = source[piece, block * half : (block + 1) * half, :]
                    if block < 3:
                        at = core * (wide // 2) + (piece * 3 + block) * TILE
                        project_in[pl.ds(side, half), pl.ds(pl.multiple_of(at, TILE), TILE)] = part
                    else:
                        at = core * (wide // 6) + piece * TILE
                        project_out[pl.ds(side, half), pl.ds(pl.multiple_of(at, TILE), TILE)] = part
    at = mine.shape[1] - 8
    parts = [
        jnp.where(sides[0] == 0, a[0, at:, :], b[0, at:, :]) for a, b in ((mine, other), (near, beyond))
    ]
    low = jnp.where(sides[1] == 0, parts[0], parts[1])
    high = jnp.where(sides[1] == 0, parts[1], parts[0])
    gains[...] = low[0:2, :rows]
    biases[0:2, :] = high[0:2, :rows]
    biases[2:6, :] = low[2:6, :rows]
    term_weight[...] = low[6:7, :rows]
    term_bias[...] = low[7:8, 0:1]
    for i in range(expand_bias.shape[1] // TILE):
        expand_bias[:, i * TILE : (i + 1) * TILE] = high[2 + i : 3 + i, :]


def run(kernel, outs, kinds, scratch, args, after=(), aliases=None, limit=58):
    specs = {"s": IN_SMEM, "v": IN_VMEM, "h": IN_PLACE}
    shapes = [jax.ShapeDtypeStruct(dims, dtype) for _, dims, dtype in outs]
    given = [
        pltpu.with_memory_space_constraint(a, pltpu.HBM) if kind == "h" else a for a, kind in zip(args, kinds)
    ]
    many = len(outs) > 1
    known = len(args)

    def body(*refs):
        kernel(*refs[:known], *refs[known + len(after) :])

    return pl.pallas_call(
        body,
        out_shape=shapes if many else shapes[0],
        in_specs=[specs[kind] for kind in kinds] + [IN_PLACE] * len(after),
        out_specs=[specs[o[0]] for o in outs] if many else specs[outs[0][0]],
        scratch_shapes=scratch,
        input_output_aliases=aliases or {},
        compiler_params=pltpu.CompilerParams(vmem_limit_bytes=limit << 20),

    )(*given, *[pltpu.with_memory_space_constraint(a, pltpu.HBM) for a in after])


def contract_rows(left, right):
    return lax.dot_general(
        left, right, (((0,), (0,)), ((), ())), preferred_element_type=F32
    )


GROUP_FIRST = (("pb", 2), ("pa", 1))
ROW_FIRST = (("pa", 1), ("pb", 2))


def swap(value, axis, distance):
    return lax.ppermute(
        value, axis, [(i, i ^ distance) for i in range(lax.axis_size(axis))]
    )


def bit(axis, distance):
    return (lax.axis_index(axis) >> (distance.bit_length() - 1)) & 1


def pick(value, index, dim):
    return lax.dynamic_index_in_dim(value, index, dim, keepdims=False)


def group_gather(mine):
    distance = 1
    while distance < lax.axis_size("pa"):
        other = swap(mine, "pa", distance)
        mine = jnp.where(
            bit("pa", distance) == 0, jnp.concatenate([mine, other]), jnp.concatenate([other, mine])
        )
        distance *= 2
    return mine


def group_scatter(whole):
    distance = lax.axis_size("pa") // 2
    while distance:
        halves = whole.reshape((2, -1) + whole.shape[1:])
        mine = bit("pa", distance)
        whole = pick(halves, mine, 0) + swap(pick(halves, 1 - mine, 0), "pa", distance)
        distance //= 2
    return whole


def steps_of(order):
    steps = [(axis, distance) for axis, distance in order]
    distance = 2
    while distance < lax.axis_size("pa"):
        steps.append(("pa", distance))
        distance *= 2
    return steps


def tree_sum(send, keep, order):
    names = []
    distance = lax.axis_size("pa") // 2
    while distance:
        names.append(("pa", distance))
        distance //= 2
    names.append(("pb", 2))
    received = swap(send, "pb", 1)
    for axis, distance in steps_of(order):
        dim = names.index((axis, distance))
        names.pop(dim)
        mine = bit(axis, distance)
        send = pick(keep, 1 - mine, dim) + pick(received, 1 - mine, dim)
        keep = pick(keep, mine, dim) + pick(received, mine, dim)
        received = swap(send, axis, distance)
    mine = keep + received
    other = swap(mine, "pb", 2)
    high = bit("pb", 2)
    return jnp.where(high == 0, jnp.stack([mine, other]), jnp.stack([other, mine]))


def cut(matrix):
    bits = lax.axis_size("pa").bit_length() - 1
    rows = matrix.shape[0] >> (bits + 1)
    return matrix.reshape((2,) * (bits + 1) + (rows, matrix.shape[1]))


def summed_rows(left, right, order):
    core = bit("pb", 1)
    half = right.shape[1] // 2
    parts = [
        cut(contract_rows(left, lax.dynamic_slice_in_dim(right, side * half, half, axis=1)))
        for side in (1 - core, core)
    ]
    mine = tree_sum(parts[0], parts[1], order)
    mine = mine.reshape(-1, half)
    other = swap(mine, "pb", 1)
    return jnp.where(
        core == 0, jnp.concatenate([mine, other], 1), jnp.concatenate([other, mine], 1)
    )


def total_of_all(value):
    distance = 1
    while distance < lax.axis_size("pb"):
        value = value + swap(value, "pb", distance)
        distance *= 2
    distance = 1
    while distance < lax.axis_size("pa"):
        value = value + swap(value, "pa", distance)
        distance *= 2
    return value


LEAF_BITS = (("pa", 4), ("pa", 2), ("pa", 1), ("pb", 2))
PIECE_ORDERS = (
    (("pb", 2), ("pa", 1), ("pa", 2), ("pa", 4)),
    (("pa", 1), ("pa", 2), ("pb", 2), ("pa", 4)),
    (("pa", 2), ("pb", 2), ("pa", 1), ("pa", 4)),
)
PLACES = tuple(len(LEAF_BITS) - 1 - LEAF_BITS.index(order[0]) for order in PIECE_ORDERS)


def begun(parts):
    held = []
    for (leaving, staying), order in zip(parts, PIECE_ORDERS):
        rest = tuple(b for b in LEAF_BITS if b != order[0])
        held.append(([(staying, rest), (swap(leaving, *order[0]), rest)], (order[0],)))
    return held


def chosen(names, settled, current=None):
    return tuple(1 if name == current else 0 if name in settled else None for name in names)


def part_of(array, names, settled, current, rows):
    wants = chosen(names, settled, current)
    starts = [0 if want is None else bit(*name) ^ want for name, want in zip(names, wants)]
    sizes = [2 if want is None else 1 for want in wants]
    part = lax.dynamic_slice(array.reshape((2,) * len(names) + (rows, TILE)), starts + [0, 0], sizes + [rows, TILE])
    return part.reshape((2,) * wants.count(None) + (rows, TILE))


def onward(held, step, sent):
    moved = []
    for (terms, settled), order, leaving in zip(held, PIECE_ORDERS, sent):
        left = tuple(b for b in LEAF_BITS if b not in settled and b != order[step])
        moved.append((terms + [(swap(leaving, *order[step]), left)], settled + (order[step],)))
    return moved


def advance(held, step, rows):
    sent = []
    for (terms, settled), order in zip(held, PIECE_ORDERS):
        sent.append(sum(part_of(array, names, settled, order[step], rows) for array, names in terms))
    return onward(held, step, sent)


def fold(plans, through, joined, bits, *refs):
    count = sum(len(plan) for plan in plans)
    terms = refs[:count]
    outs = refs[count + through : count + through + (1 if joined else len(plans))]
    scratch = refs[count + through + len(outs) + through :]
    sems, out_sems = scratch[-2:]
    pairs = []
    at = 0
    for plan in plans:
        for wants in plan:
            index = tuple(
                slice(None) if want is None else jnp.bitwise_xor(bits[LEAF_BITS.index(name)], want) for name, want in wants
            )
            pairs.append((terms[at].at[index], scratch[at]))
            at += 1
    copies = fetch(pairs, sems)
    puts = []
    at = 0
    for i, plan in enumerate(plans):
        finish_all(copies[at : at + len(plan)])
        total = scratch[at][...]
        for k in range(1, len(plan)):
            total = total + scratch[at + k][...]
        scratch[at][...] = total
        puts += fetch([(scratch[at], outs[0].at[i] if joined else outs[i])], out_sems, i)
        at += len(plan)
    finish_all(puts)


def fold_by_kernel(held, step, rows, through=(), after=(), joined=False):
    plans = []
    args = []
    scratch = []
    outs = []
    for (terms, settled), order in zip(held, PIECE_ORDERS):
        plan = []
        for array, names in terms:
            wants = chosen(names, settled, order[step])
            plan.append(tuple(zip(names, wants)))
            args.append(array.reshape((2,) * len(names) + (rows, TILE)))
            dims = (2,) * wants.count(None) + (rows, TILE)
            scratch.append(pltpu.VMEM(dims, F32))
        plans.append(plan)
        outs.append(("h", dims, F32))
    if joined:
        outs = [("h", (len(plans), rows, TILE), F32)]
    bits = jnp.stack([bit(*name) for name in LEAF_BITS])
    done = run(
        partial(fold, plans, len(through), joined),
        outs + [("h", a.shape, a.dtype) for a in through],
        "s" + "h" * (len(args) + len(through)),
        scratch + [pltpu.SemaphoreType.DMA((len(args),)), pltpu.SemaphoreType.DMA((len(plans),))],
        (bits, *args, *through),
        after,
        {1 + len(args) + i: len(outs) + i for i in range(len(through))},
    )
    return done if len(outs) + len(through) > 1 else [done]


def advance_by_kernel(held, step, rows, through=(), after=()):
    done = fold_by_kernel(held, step, rows, through, after)
    return onward(held, step, done[:3]), done[3:]


def last_exchange(held, rows, through=()):
    step = len(LEAF_BITS) - 1
    name = PIECE_ORDERS[0][step]
    sent, *through = fold_by_kernel(held, step, rows, through, joined=True)
    came = swap(sent, *name)
    total = jnp.stack(
        [sum(part_of(array, names, settled + (name,), None, rows) for array, names in terms) for terms, settled in held]
    )
    return total + came, through


def on_device(
    passages, queries, passage_ids, query_ids, batch_length, query_batch, project_in, project_out, expand_weight,
    expand_bias, reduce_weight, norm_gains, biases, term_weight, term_bias, out_grad, score_grad,
):
    members = lax.axis_size("pa")
    member_index = lax.axis_index("pa")
    core = bit("pb", 1)
    local_batch = member_index // (members // BATCH_PB)
    length = lax.dynamic_slice_in_dim(
        batch_length, lax.axis_index("pb") * BATCH_PB + local_batch, 1, axis=0
    )
    n_pass, width = passages.shape
    n_query = queries.shape[0]
    count = n_pass + n_query
    deep = expand_weight.shape[1]
    slots = score_grad.shape[1]
    bias_row = expand_bias[None]
    term_row = term_weight[None]

    blocks = deep // (2 * BLOCK)
    by_three = (3, n_pass, deep // 3)
    weights = [pltpu.VMEM(expand_weight.shape, BF16), pltpu.VMEM(reduce_weight.shape, BF16)]

    def vmem(*dims, dtype=BF16):
        return pltpu.VMEM(dims, dtype)

    def sems(number):
        return pltpu.SemaphoreType.DMA((number,))

    (
        mixed, attended, attended_turned, stats, normed_one, inverse_one, low,
        hidden_query, slope_query, unit_query, scale_query, pre_query, known,
    ) = run(
        forward_one,
        [
            ("h", (count, 3 * width), BF16), ("h", (count, width), BF16),
            ("h", (width, count), BF16), ("v", (HEADS, 1, count), F32), ("h", (count, width), F32),
            ("v", (count, 1), F32), ("h", (count, width), BF16), ("h", (3, n_query, deep // 3), BF16),
            ("h", (n_query, deep), BF16), ("v", (n_query, width), F32), ("v", (n_query, 1), F32),
            ("v", (n_query, 1), F32), ("v", (1, 3, n_query), F32),
        ],
        "svvhhhhvvvvsvs",
        [
            vmem(*project_in.shape), vmem(*project_out.shape), *weights, vmem(count, 3 * width), vmem(count, width),
            vmem(width, count), vmem(count, width, dtype=F32), vmem(count, width), vmem(n_query, deep), vmem(n_query, deep),
            vmem(n_pass, n_pass, dtype=F32), vmem(n_query, n_query, dtype=F32), vmem(count, width, dtype=F32),
            sems(6), sems(6 + deep // TILE),
        ],
        (length, passages, queries, project_in, project_out, expand_weight, reduce_weight, bias_row, norm_gains,
         biases, term_row, term_bias, query_ids[None], query_batch),
    )
    known = group_gather(known)
    hidden, slope, unit_pass, scale_pass, pre_pass, passage_out = run(
        forward_two,
        [
            ("h", by_three, BF16), ("h", (n_pass, deep), BF16), ("h", (n_pass, width), F32),
            ("v", (n_pass, 1), F32), ("v", (n_pass, 1), F32), ("h", (n_pass, width), BF16),
        ],
        "hhhhvvvvs",
        [
            vmem(n_pass, width), vmem(n_pass, width, dtype=F32), *weights, vmem(n_pass, deep), vmem(n_pass, deep),
            vmem(n_pass, width, dtype=F32), vmem(n_pass, width), vmem(n_pass, width, dtype=F32),
            sems(3 + blocks), sems(deep // TILE + blocks + 2 * (n_pass // TILE)),
        ],
        (low, normed_one, expand_weight, reduce_weight, bias_row, norm_gains, biases, term_row, term_bias),
    )
    scores, pass_term_grad, query_part = run(
        match,
        [("v", score_grad.shape, F32), ("v", (n_pass, 1), F32), ("v", (members, 1, n_query), F32)],
        "svvvv",
        [],
        (jnp.concatenate([length, local_batch.reshape(1)]), known, score_grad, passage_ids[None], pre_pass),
    )
    query_term_grad = group_scatter(query_part)

    def back_outs(rows):
        return [
            ("h", (width, rows), BF16), ("h", (rows, deep), BF16), ("h", (width, rows), BF16),
            ("h", (rows, width), F32), ("h", (rows, width), BF16), ("v", (8, width), F32), ("v", (1, deep), F32),
        ]

    back_kinds = "vvhhvhhvhhhvvv"

    def back_scratch(rows):
        return [
            vmem(rows, width), vmem(rows, width, dtype=F32), vmem(rows, deep), vmem(rows, width, dtype=F32), vmem(rows, width),
            *weights, vmem(rows, deep), vmem(width, rows), vmem(width, rows), vmem(rows, width, dtype=F32), vmem(rows, width),
            vmem(rows, width, dtype=F32), vmem(rows, width),
            sems(3 + 2 * blocks + 2 * (rows // TILE)), sems(2 + blocks + 2 * (rows // TILE)),
        ]

    def back_args(term_grad, pre, unit, scale, slope_here):
        return (term_grad, pre, out_grad, unit, scale, slope_here, normed_one, inverse_one, low,
                expand_weight, reduce_weight, norm_gains, biases, term_row)

    rg_pass, eg_pass, low_pass, one_pass, bg_pass, sums_pass, shift_pass = run(
        partial(backward_rows, True, 0), back_outs(n_pass), back_kinds, back_scratch(n_pass),
        back_args(pass_term_grad, pre_pass, unit_pass, scale_pass, slope),
    )
    fits = deep // members == 3 * TILE
    shard = width // members
    sides = jnp.stack([core, *(bit(*order[0]) for order in PIECE_ORDERS)])
    leaf_rows = (deep // 6 // TILE * (shard // 2) + width // 4, 4 * (shard // 2) + 8)
    if fits:
        dims = (members, 2, leaf_rows[0], TILE)
        third = deep // 6
        (
            rg_query, eg_query, low_query, one_query, bg_query, sums_query, shift_query, *sent
        ) = run(
            partial(backward_query, members, n_pass),
            back_outs(n_query) + [("h", dims, F32)] * 3,
            "s" + back_kinds + "hhhhh",
            back_scratch(n_query)
            + [
                vmem(width, n_pass), vmem(n_pass, deep // 2), vmem(width // 2, n_pass), vmem(*by_three),
                vmem(3, n_query, deep // 3), vmem(3, *dims, dtype=F32), sems(5), sems(6),
            ],
            (sides,) + back_args(query_term_grad[0], pre_query, unit_query, scale_query, slope_query)
            + (low_pass, eg_pass, rg_pass, hidden, hidden_query),
        )
        came = [swap(part, "pb", 1) for part in sent]
        parts = []
        for piece, order in enumerate(PIECE_ORDERS):
            half = (leaf_rows[0], TILE)
            parts.append(
                run(
                    partial(inner_kept, members, piece, PLACES[piece]),
                    [("h", (members,) + half, F32)] * 2,
                    "s" + "h" * 9,
                    [
                        vmem(width, n_pass), vmem(width, n_query), vmem(n_pass, third), vmem(n_query, third),
                        vmem(width // 2, n_pass), vmem(width // 2, n_query), vmem(n_pass, deep // 3), vmem(n_query, deep // 3),
                        vmem(*dims, dtype=F32), vmem(2, members, *half, dtype=F32), sems(10), sems(4),
                    ],
                    (jnp.stack([core, bit(*order[0])]), low_pass, low_query, eg_pass, eg_query, rg_pass, rg_query, hidden,
                     hidden_query, came[piece]),
                )
            )
        inner = begun(parts)
        pins = tuple(leaving for leaving, _ in parts)
        extra = [("v", (members, 16, TILE), F32)]
        last = [("h", (3, members, 2, leaf_rows[1], TILE), F32)]
    else:
        rg_query, eg_query, low_query, one_query, bg_query, sums_query, shift_query = run(
            partial(backward_rows, False, n_pass), back_outs(n_query), back_kinds, back_scratch(n_query),
            back_args(query_term_grad[0], pre_query, unit_query, scale_query, slope_query),
        )
        pins = ()
        extra = [("v", (16 + deep // width, width), F32)]
        last = []
    mixed_grad, turned, vectors, passage_grad, query_grad, *sent = run(
        partial(backward_attention, members if fits else 0),
        [("h", (count, 3 * width), BF16), ("h", (width, count), BF16)]
        + extra
        + [("v", (n_pass, width), BF16), ("v", (n_query, width), BF16)]
        + last,
        "ssvvhhhhhv" + "hhhh" + "vvvv",
        [
            vmem(*project_out.shape), vmem(n_pass, width), vmem(n_query, width), vmem(count, 3 * width), vmem(count, width),
            vmem(count, 3 * width), vmem(width, count), vmem(count, width), vmem(HEADS, 1, count, dtype=F32),
            vmem(2, n_pass, n_pass), vmem(n_pass, n_pass, dtype=F32), vmem(n_query, n_query, dtype=F32),
            vmem(width, count), vmem(*project_in.shape), vmem(n_pass, width, dtype=F32), vmem(n_query, width, dtype=F32),
            vmem(*(last[0][1] if fits else (8, TILE)), dtype=F32), sems(9), sems(5),
        ],
        (sides, length, passages, queries, bg_pass, bg_query, project_out, mixed, attended, stats, attended_turned, project_in,
         one_pass, one_query, sums_pass, sums_query, shift_pass, shift_query),
        pins,
    )
    if fits:
        inner, sent = advance_by_kernel(inner, 1, leaf_rows[0], tuple(sent))
        half = (leaf_rows[1], TILE)
        dims = (3, members, 2) + half
        parts = run(
            partial(outer_kept, members, PLACES),
            [("h", (members,) + half, F32)] * 6,
            "s" + "h" * 5 + "vh",
            [
                vmem(width, count), vmem(count, 3 * width // 2), vmem(width, count), vmem(n_pass, width // 2),
                vmem(n_query, width // 2), vmem(*dims, dtype=F32), vmem(3, 2, members, *half, dtype=F32), sems(8), sems(6),
            ],
            (sides, turned, mixed_grad, attended_turned, bg_pass, bg_query, vectors, swap(sent[0], "pb", 1)),
        )
        inner, _ = advance_by_kernel(inner, 2, leaf_rows[0], after=tuple(parts[0:6:2]))
        inner_mine, late = last_exchange(inner, leaf_rows[0], (parts[2],))
        outer = begun([parts[0:2], (late[0], parts[3]), parts[4:6]])
        for step in (1, 2):
            outer = advance(outer, step, leaf_rows[1])
        outer_mine, _ = last_exchange(outer, leaf_rows[1])
        where = jnp.stack([core, bit("pb", 2)])

        def finish(kernel, mine, outs):
            near = swap(mine, "pb", 2)
            args = (where, mine, near, swap(mine, "pb", 1), swap(near, "pb", 1))
            return run(kernel, outs, "svvvv", [], args)

        expand_total, reduce_total = finish(
            finish_inner, inner_mine, [("v", (shard, deep), F32), ("v", (deep // members, width), F32)]
        )
        in_total, out_total, gains_grad, biases_grad, term_grad, bias_grad, expand_shift = finish(
            finish_outer, outer_mine,
            [
                ("v", (shard, 3 * width), F32), ("v", (shard, width), F32), ("v", (2, shard), F32), ("v", (6, shard), F32),
                ("v", (1, shard), F32), ("v", (1, 1), F32), ("v", (1, deep // members), F32),
            ],
        )
    else:
        in_order = [h.reshape(3, h.shape[1], -1, TILE).transpose(1, 2, 0, 3).reshape(-1, deep) for h in (hidden, hidden_query)]
        whole = [jnp.concatenate(pair, axis) for pair, axis in (
            (in_order, 0), ((rg_pass, rg_query), 1), ((eg_pass, eg_query), 0), ((bg_pass, bg_query), 0),
        )]
        reduce_total = summed_rows(whole[0], whole[1].T, ROW_FIRST)
        expand_total = summed_rows(low, whole[2], GROUP_FIRST)
        out_total = summed_rows(attended, whole[3], GROUP_FIRST)
        in_total = summed_rows(turned.T, mixed_grad, ROW_FIRST)
        vectors = total_of_all(vectors)
        mine = lax.dynamic_slice_in_dim(vectors[:10], member_index * shard, shard, axis=1)
        expand_shift = lax.dynamic_slice_in_dim(
            vectors[16:].reshape(-1), member_index * (deep // members), deep // members
        )
        gains_grad = mine[:2]
        biases_grad = jnp.concatenate([mine[8:10], mine[2:6]])
        term_grad = mine[6]
        bias_grad = mine[7, :1]
    return (
        scores,
        passage_out,
        passage_grad,
        query_grad,
        in_total,
        out_total,
        expand_total,
        expand_shift.reshape(-1),
        reduce_total,
        gains_grad,
        biases_grad,
        term_grad.reshape(-1),
        bias_grad.reshape(-1),
    )


def solution(mesh):
    return jax.shard_map(
        on_device,
        mesh=mesh,
        in_specs=(
            P(("pb", "pa"), None),
            P(("pb", "pa"), None),
            P(("pb", "pa")),
            P(("pb", "pa")),
            P(),
            P(("pb", "pa")),
            P(),
            P(),
            P(),
            P(),
            P(),
            P(),
            P(),
            P(),
            P(),
            P(("pb", "pa"), None),
            P("pb", "pa"),
        ),
        out_specs=(
            P("pb", "pa"),
            P(("pb", "pa"), None),
            P(("pb", "pa"), None),
            P(("pb", "pa"), None),
            P("pa", None),
            P("pa", None),
            P("pa", None),
            P("pa"),
            P("pa", None),
            P(None, "pa"),
            P(None, "pa"),
            P("pa"),
            P(),
        ),
        check_vma=False,
    )
```

```python
from functools import partial

import jax
import jax.numpy as jnp
from jax import lax
from jax.experimental import pallas as pl
from jax.experimental.pallas import tpu as pltpu
from jax.sharding import PartitionSpec as P

HEADS = 12
HEAD = 64
LONG = 512
QLEN = 32
BATCH_PB = 4

NEG = -1e30
HIGH = lax.Precision.HIGHEST
LN_EPS = 1e-12
SCALE = HEAD ** (-0.5)
BLOCK = 256
TILE = 128
F32 = jnp.float32
BF16 = jnp.bfloat16

IN_VMEM = pl.BlockSpec(memory_space=pltpu.VMEM)
IN_SMEM = pl.BlockSpec(memory_space=pltpu.SMEM)
IN_PLACE = pl.BlockSpec(memory_space=pl.ANY)


def shape(dims, dtype):
    return (tuple(dims), dtype)


def dot(left, right):
    return jnp.dot(left, right, preferred_element_type=F32)


def dot_nt(left, right, precision=None):
    return lax.dot_general(
        left, right, (((1,), (1,)), ((), ())), preferred_element_type=F32, precision=precision
    )


def dot_tn(left, right):
    return lax.dot_general(left, right, (((0,), (0,)), ((), ())), preferred_element_type=F32)


def columns(index, width, first=0):
    return pl.ds(pl.multiple_of(first + index * width, TILE), width)


def tiles(count):
    return [slice(first, first + TILE) for first in range(0, count, TILE)]


def row_sum(matrix):
    return jnp.sum(matrix, axis=0, keepdims=True)


def fetch(pairs, sems, first=0):
    copies = [
        pltpu.make_async_copy(source, target, sems.at[first + i]) for i, (source, target) in enumerate(pairs)
    ]
    for copy in copies:
        copy.start()
    return copies


def finish_all(copies):
    for copy in copies:
        copy.wait()


def norm_forward(total):
    centred = total - jnp.mean(total, axis=-1, keepdims=True)
    inverse = lax.rsqrt(jnp.mean(centred * centred, axis=-1, keepdims=True) + LN_EPS)
    return centred * inverse, inverse


def norm_backward(scaled, normed, inverse):
    centred = scaled - jnp.mean(scaled, axis=-1, keepdims=True)
    return inverse * (centred - normed * jnp.mean(scaled * normed, axis=-1, keepdims=True))


def head_lanes(sub):
    lane = lax.broadcasted_iota(jnp.int32, (1, 2 * HEAD), 1)
    return (lane // HEAD) == sub


def same_slot(count, length):
    rows = lax.broadcasted_iota(jnp.int32, (count, count), 0) // length
    cols = lax.broadcasted_iota(jnp.int32, (count, count), 1) // length
    return jnp.where(rows == cols, 0.0, NEG)


def attend(mixed, turned, stats, first, count, width, mask, unroll):
    rows = slice(first, first + count)

    def pair(hp, carry):
        key = mixed[rows, columns(hp, 2 * HEAD, width)]
        value = mixed[rows, columns(hp, 2 * HEAD, 2 * width)].T
        for sub in (0, 1):
            key_here = jnp.where(head_lanes(sub), key, jnp.zeros_like(key))
            logits = dot_nt(key_here, mixed[rows, columns(hp, 2 * HEAD)]) + mask[...]
            highest = jnp.max(logits, axis=0, keepdims=True)
            powers = jnp.exp(logits - highest)
            total = jnp.sum(powers, axis=0, keepdims=True)
            weights = (powers * (1.0 / total)).astype(BF16)
            out_rows = pl.ds(pl.multiple_of((2 * hp + sub) * HEAD, HEAD), HEAD)
            turned[out_rows, rows] = dot(value[sub * HEAD : (sub + 1) * HEAD], weights).astype(BF16)
            stats[2 * hp + sub, :, rows] = highest + jnp.log(total)
        return carry

    lax.fori_loop(0, HEADS // 2, pair, 0, unroll=unroll)


def grow(rows, first, count, expand, cols, expand_bias, hidden, slope):
    for at in range(0, count, min(BLOCK, count)):
        tile = slice(at, at + min(BLOCK, count))
        value = dot(rows[first + at : first + tile.stop, :], expand[:, cols]) + expand_bias[:, cols]
        lower = 0.5 + 0.5 * lax.erf(value * (0.5**0.5))
        hidden[tile, cols] = (value * lower).astype(BF16)
        density = jnp.exp(-0.5 * value * value) * 0.3989422804014327
        slope[tile, cols] = (lower + value * density).astype(BF16)


def by_piece(block, hidden, out):
    shard, piece = lax.div(block, 3), lax.rem(block, 3)
    return hidden.at[:, columns(block, TILE)], out.at[piece, :, columns(shard, TILE)]


def close_forward(total, normed_one, first, count, gains, biases, term_weight, term_bias, normed, inverse, pre, passage_out, tell):
    for i, tile in enumerate(tiles(count)):
        base = normed_one[first + tile.start : first + tile.stop, :] * gains[0:1, :] + biases[4:5, :]
        unit, scale = norm_forward(base + total[tile, :] + biases[3:4, :])
        normed[tile, :] = unit
        inverse[tile, :] = scale
        second = unit * gains[1:2, :] + biases[5:6, :]
        pre[tile, :] = jnp.sum(second * term_weight[...], axis=-1, keepdims=True) + term_bias[0]
        if passage_out is not None:
            passage_out[tile, :] = second.astype(BF16)
        tell(i, tile)


def softplus(value):
    return jnp.maximum(value, 0.0) + jnp.log1p(jnp.exp(-jnp.abs(value)))


def sigmoid(value):
    return 1.0 / (1.0 + jnp.exp(-value))


def forward_one(
    facts, lengths, passages, queries, project_in, project_out, expand, reduce, expand_bias, gains, biases,
    term_weight, term_bias, query_ids, query_batch,
    mixed_out, attended_out, turned_out, stats, normed_out, inverse_one, low_out,
    hidden_out, slope_out, normed_two, inverse_two, pre, known,
    in_here, out_here, expand_here, reduce_here, mixed, attended, turned, normed_one, low, hidden, slope,
    mask, query_mask, total, sems, out_sems,
):
    n_pass, width = passages.shape
    n_query = queries.shape[0]
    count = n_pass + n_query
    parts = [slice(i * width, (i + 1) * width) for i in range(3)]
    copies = fetch(
        [(project_in.at[:, part], in_here.at[:, part]) for part in parts]
        + [(project_out, out_here), (expand, expand_here), (reduce, reduce_here)],
        sems,
    )
    mask[...] = same_slot(n_pass, lengths[facts[BATCH]])
    query_mask[...] = same_slot(n_query, QLEN)
    for part in range(3):
        copies[part].wait()
        for source, first, rows in ((passages, 0, n_pass), (queries, n_pass, n_query)):
            value = dot(source[...], in_here[:, parts[part]])
            if part != 1:
                value = value + biases[part // 2 : part // 2 + 1, :]
            if part == 0:
                value = value * SCALE
            mixed[first : first + rows, parts[part]] = value.astype(BF16)
    puts = fetch([(mixed, mixed_out)], out_sems)
    attend(mixed, turned, stats, n_pass, n_query, width, query_mask, HEADS // 2)
    attend(mixed, turned, stats, 0, n_pass, width, mask, 3)
    attended[...] = turned[...].T
    puts += fetch([(turned, turned_out), (attended, attended_out)], out_sems, 1)
    copies[3].wait()
    total[...] = dot(attended[...], out_here[...])
    for tile in reversed(tiles(count)):
        source, at = (passages, tile.start) if tile.start < n_pass else (queries, tile.start - n_pass)
        unit, scale = norm_forward(source[at : at + TILE, :].astype(F32) + total[tile, :] + biases[2:3, :])
        normed_one[tile, :] = unit
        inverse_one[tile, :] = scale
        low[tile, :] = (unit * gains[0:1, :] + biases[4:5, :]).astype(BF16)
    puts += fetch([(normed_one, normed_out), (low, low_out)], out_sems, 3)
    copies[4].wait()
    wide = 2 * BLOCK

    def block(j, carry):
        grow(low, n_pass, n_query, expand_here, columns(j, wide), expand_bias, hidden, slope)
        return carry

    lax.fori_loop(0, expand.shape[1] // wide, block, 0, unroll=2)
    puts += fetch(
        [by_piece(i, hidden, hidden_out) for i in range(expand.shape[1] // TILE)] + [(slope, slope_out)], out_sems, 5
    )
    copies[5].wait()
    total[0:n_query, :] = dot(hidden[...], reduce_here[...])
    close_forward(
        total, normed_one, n_pass, n_query, gains, biases, term_weight, term_bias, normed_two, inverse_two, pre, None,
        lambda i, tile: None,
    )
    known[0, 0:1, :] = jnp.broadcast_to(softplus(pre[...]), (n_query, TILE)).T[0:1, :]
    known[0, 1:2, :] = query_ids[...].astype(F32)
    owner = lax.broadcasted_iota(jnp.int32, (1, n_query), 1) // QLEN
    tags = jnp.zeros((1, n_query), F32)
    for query in range(n_query // QLEN):
        tags = jnp.where(owner == query, query_batch[query].astype(F32), tags)
    known[0, 2:3, :] = tags
    finish_all(puts)


def forward_two(
    low, normed_one, expand, reduce, expand_bias, gains, biases, term_weight, term_bias,
    hidden_out, slope_out, normed_out, inverse_two, pre, passage_out,
    low_here, one_here, expand_here, reduce_here, hidden, slope, normed_two, second, total, sems, out_sems,
):
    count = second.shape[0]
    wide = 2 * BLOCK
    blocks = expand.shape[1] // wide
    rows = pl.ds(0, count)
    low_copy = fetch([(low.at[rows, :], low_here)], sems)[0]
    chunks = fetch([(expand.at[:, columns(j, wide)], expand_here.at[:, columns(j, wide)]) for j in range(blocks)], sems, 1)
    late = fetch([(reduce, reduce_here), (normed_one.at[rows, :], one_here)], sems, 1 + blocks)
    low_copy.wait()
    puts = []
    for j in range(blocks):
        chunks[j].wait()
        cols = columns(j, wide)
        grow(low_here, 0, count, expand_here, cols, expand_bias, hidden, slope)
        first = j * (wide // TILE)
        puts += fetch([by_piece(first + i, hidden, hidden_out) for i in range(wide // TILE)], out_sems, first)
        puts += fetch([(slope.at[:, cols], slope_out.at[:, cols])], out_sems, blocks * (wide // TILE) + j)
    late[0].wait()
    total[...] = dot(hidden[...], reduce_here[...])
    late[1].wait()
    base = blocks * (wide // TILE) + blocks

    def tell(i, tile):
        puts.extend(
            fetch([(normed_two.at[tile, :], normed_out.at[tile, :]), (second.at[tile, :], passage_out.at[tile, :])], out_sems, base + 2 * i)
        )

    close_forward(
        total, one_here, 0, count, gains, biases, term_weight, term_bias, normed_two, inverse_two, pre, second, tell
    )
    finish_all(puts)


def match(facts, lengths, known, score_grad, passage_ids, pre, scores, pass_grad, query_part):
    members, _, tokens = known.shape
    n_pass = passage_ids.shape[1]
    slots, queries = scores.shape
    per_query = queries // members
    together = min(members, 8)
    slot = lax.broadcasted_iota(jnp.int32, (n_pass, slots), 0) // lengths[facts[BATCH]]
    table = slot == lax.broadcasted_iota(jnp.int32, (n_pass, slots), 1)
    placed = jnp.where(table, softplus(pre[...]), 0.0).astype(BF16)
    who = lax.broadcasted_iota(jnp.int32, (queries, together * tokens), 0)
    token = lax.broadcasted_iota(jnp.int32, (queries, together * tokens), 1) // QLEN
    mine = jnp.broadcast_to(passage_ids[...].astype(F32), (8, n_pass)).T[:, 0:1]

    def several(c, carry):
        scored, placed_grads = carry
        first = c * together
        wide = jnp.concatenate([known[first + i] for i in range(together)], axis=1)
        matches = jnp.where(mine == wide[1:2, :], 1.0, 0.0).astype(BF16)
        per_token = dot_tn(placed, matches)
        masked = jnp.where(wide[2:3, :] == facts[BATCH_IN_GROUP].astype(F32), 1.0, 0.0)
        weighted = wide[0:1, :] * masked
        spread = jnp.where(who == token + first * per_query, 1.0, 0.0)
        grad = jnp.dot(score_grad[...], spread, preferred_element_type=F32, precision=HIGH)
        placed_grads = placed_grads + dot_nt(matches, (grad * weighted).astype(BF16))
        scored = scored + dot_nt(per_token * weighted, spread, HIGH)
        part = row_sum(grad * per_token) * masked
        for i in range(together):
            query_part[first + i] = part[:, i * tokens : (i + 1) * tokens]
        return scored, placed_grads

    carry = (jnp.zeros(scores.shape, F32), jnp.zeros((n_pass, slots), F32))
    if members == together:
        scored, placed_grads = several(0, carry)
    else:
        scored, placed_grads = lax.fori_loop(0, members // together, several, carry)
    scores[...] = scored
    pass_grad[...] = jnp.sum(jnp.where(table, placed_grads, 0.0), axis=1, keepdims=True)


def backward_rows(
    with_out, first, term_grad, pre, out_grad, normed_two, inverse_two, slope, normed_one, inverse_one, low_one, expand, reduce,
    gains, biases, term_weight,
    reduce_turned, expanded_grad, low_turned, sum_one, branch_grad, sums, expand_shift,
    grad_here, two_here, slope_here, one_here, low_here, expand_here, reduce_here, grown, turned, low_side, sum_here, branch_here,
    sum_two, reduce_out_grad, sems, out_sems, begin=lambda: None, then=lambda *made: [],
):
    count, width = branch_grad.shape
    deep = slope.shape[1]
    wide = 2 * BLOCK
    blocks = deep // wide
    here = pl.ds(first, count)
    early = [
        fetch(
            [(normed_two.at[tile, :], two_here.at[tile, :])]
            + ([(out_grad.at[tile, :], grad_here.at[tile, :])] if with_out else []),
            sems,
            2 * i,
        )
        for i, tile in enumerate(tiles(count))
    ]
    base = 2 * (count // TILE)
    chunks = [
        fetch(
            [
                (reduce.at[columns(j, wide), :], reduce_here.at[columns(j, wide), :]),
                (slope.at[:, columns(j, wide)], slope_here.at[:, columns(j, wide)]),
            ],
            sems,
            base + 2 * j,
        )
        for j in range(blocks)
    ]
    base += 2 * blocks
    late = fetch([(low_one.at[here, :], low_here), (expand, expand_here), (normed_one.at[here, :], one_here)], sems, base)
    begin()
    if not with_out:
        spread = jnp.broadcast_to(term_grad[...], (TILE, count)).T
    totals = [jnp.zeros((1, width), F32) for _ in range(8)]
    for i, tile in enumerate(tiles(count)):
        grad_in = term_grad[tile, :] if with_out else spread[:, 0:1]
        pre_grad = grad_in * sigmoid(pre[tile, :])
        finish_all(early[i])
        unit = two_here[tile, :]
        second_grad = pre_grad * term_weight[...]
        if with_out:
            second_grad = second_grad + grad_here[tile, :].astype(F32)
        back = norm_backward(second_grad * gains[1:2, :], unit, inverse_two[tile, :])
        rounded = back.astype(BF16)
        sum_two[tile, :] = back
        reduce_out_grad[tile, :] = rounded
        totals[1] = totals[1] + row_sum(second_grad * unit)
        totals[3] = totals[3] + row_sum(rounded.astype(F32))
        totals[5] = totals[5] + row_sum(second_grad)
        totals[6] = totals[6] + row_sum(pre_grad * (unit * gains[1:2, :] + biases[5:6, :]))
        totals[7] = totals[7] + row_sum(jnp.broadcast_to(pre_grad, (TILE, width)))
    turned[...] = reduce_out_grad[...].T
    puts = fetch([(turned, reduce_turned)], out_sems)
    for j in range(blocks):
        cols = columns(j, wide)
        finish_all(chunks[j])
        grad = dot_nt(reduce_out_grad[...], reduce_here[cols, :]) * slope_here[:, cols].astype(F32)
        rounded = grad.astype(BF16)
        grown[:, cols] = rounded
        expand_shift[:, cols] = row_sum(rounded.astype(F32))
        puts += fetch([(grown.at[:, cols], expanded_grad.at[:, cols])], out_sems, 1 + j)
    late[0].wait()
    low_side[...] = low_here[...].T
    puts += fetch([(low_side, low_turned)], out_sems, 1 + blocks)
    late[1].wait()
    sum_two[...] = sum_two[...] + dot_nt(grown[...], expand_here[...])
    late[2].wait()
    for i, tile in enumerate(tiles(count)):
        first_grad = sum_two[tile, :]
        unit = one_here[tile, :]
        back = norm_backward(first_grad * gains[0:1, :], unit, inverse_one[first + tile.start : first + tile.stop, :])
        rounded = back.astype(BF16)
        sum_here[tile, :] = back
        branch_here[tile, :] = rounded
        puts += fetch(
            [(sum_here.at[tile, :], sum_one.at[tile, :]), (branch_here.at[tile, :], branch_grad.at[tile, :])], out_sems, 2 + blocks + 2 * i
        )
        totals[0] = totals[0] + row_sum(first_grad * unit)
        totals[2] = totals[2] + row_sum(rounded.astype(F32))
        totals[4] = totals[4] + row_sum(first_grad)
    for i, total in enumerate(totals):
        sums[i : i + 1, :] = total
    puts += then(grown, turned, low_side)
    finish_all(puts)


def backward_query(members, first, sides, *refs):
    given, low_pass, grad_pass, reduce_pass, hidden_pass, hidden_query = refs[:14], *refs[14:19]
    made, sent = refs[19:26], refs[26:29]
    own, (low, grad, turn, hid_p, hid_q, buffers, sems, out_sems) = refs[29:45], refs[45:]
    core = 1 - sides[0]
    spread = grad_pass.shape[1]
    width = low_pass.shape[0]
    copies = []

    def begin():
        wide = pl.ds(pl.multiple_of(core * (spread // 2), TILE), spread // 2)
        half = pl.ds(pl.multiple_of(core * (width // 2), TILE), width // 2)
        pairs = [
            (low_pass, low), (grad_pass.at[:, wide], grad), (reduce_pass.at[half, :], turn),
            (hidden_pass, hid_p), (hidden_query, hid_q),
        ]
        copies.extend(fetch(pairs, sems))

    def then(grown, turned, low_side):
        finish_all(copies)
        puts = []
        for piece in range(3):

            def emit(leaf, side, row, part):
                buffers[piece, leaf, side, row : row + part.shape[0], :] = part

            def tell(rows, place):
                puts.extend(
                    fetch([(buffers.at[piece, :, :, rows, :], sent[piece].at[:, :, rows, :])], out_sems, 2 * piece + place)
                )

            third = spread // 6
            inner_leaves(
                members, low, low_side, grad.at[:, piece * third : (piece + 1) * third],
                grown.at[:, pl.ds(pl.multiple_of(core * (spread // 2) + piece * third, TILE), third)],
                turn, turned.at[pl.ds(pl.multiple_of(core * (width // 2), TILE), width // 2), :],
                hid_p.at[piece], hid_q.at[piece], emit, tell,
            )
        return puts

    backward_rows(False, first, *given, *made, *own, begin=begin, then=then)


def attend_backward(mixed, attended_grad, stats, inner, mixed_grad, logit_grads, first, count, width, mask, tell):
    rows = slice(first, first + count)
    step = min(BLOCK, count)

    def pair(hp, carry):
        query = mixed[rows, columns(hp, 2 * HEAD)]
        grad = attended_grad[rows, columns(hp, 2 * HEAD)]
        query_grad = jnp.zeros((count, 2 * HEAD), F32)
        kept = []
        for sub in (0, 1):
            lanes = head_lanes(sub)
            total = stats[2 * hp + sub, :, rows]
            level = inner[2 * hp + sub, :, rows]
            for at in range(0, count, step):
                tile = slice(at, at + step)
                here = slice(first + at, first + at + step)
                key = mixed[here, columns(hp, 2 * HEAD, width)]
                value = mixed[here, columns(hp, 2 * HEAD, 2 * width)]
                key_here = jnp.where(lanes, key, jnp.zeros_like(key))
                value_here = jnp.where(lanes, value, jnp.zeros_like(value))
                weights = jnp.exp(dot_nt(key_here, query) + (mask[tile, :] - total))
                logit_grad = (weights * (dot_nt(value_here, grad) - level)).astype(BF16)
                logit_grads[sub, tile, 0:count] = logit_grad
                kept.append((dot(logit_grad, query), dot(weights.astype(BF16), grad)))
        for i, at in enumerate(range(0, count, step)):
            here = slice(first + at, first + at + step)
            for part in (0, 1):
                mixed_grad[here, columns(hp, 2 * HEAD, (part + 1) * width)] = jnp.where(
                    head_lanes(0), kept[i][part], kept[i + count // step][part]
                ).astype(BF16)
        for sub in (0, 1):
            key = mixed[rows, columns(hp, 2 * HEAD, width)]
            key_here = jnp.where(head_lanes(sub), key, jnp.zeros_like(key))
            query_grad = query_grad + dot_tn(logit_grads[sub, 0:count, 0:count], key_here)
        mixed_grad[rows, columns(hp, 2 * HEAD)] = (query_grad * SCALE).astype(BF16)
        tell(hp)
        return carry

    lax.fori_loop(0, HEADS // 2, pair, 0)


def backward_attention(
    members, sides, lengths, passages, queries, pass_grad, query_grad, project_out, mixed, attended, stats,
    attended_turned, project_in, pass_sum, query_sum, sums_pass, sums_query, shift_pass, shift_query,
    grad_out, turned_out, vectors, pass_out, query_out, *rest,
):
    sent = rest[0] if members else None
    (
        out_here, pass_here, query_here, mixed_here, attended_here, mixed_grad, turned,
        attended_grad, inner, logit_grads, mask, query_mask, across_here, in_here, pass_sum_here, query_sum_here, buffers,
        sems, out_sems,
    ) = rest[-19:]
    n_pass, width = passages.shape
    n_query = queries.shape[0]
    count = n_pass + n_query
    copies = fetch(
        [
            (project_out, out_here), (pass_grad, pass_here), (query_grad, query_here), (attended, attended_here),
            (mixed, mixed_here), (attended_turned, across_here), (project_in, in_here), (pass_sum, pass_sum_here),
            (query_sum, query_sum_here),
        ],
        sems,
    )
    query_mask[...] = same_slot(n_query, QLEN)
    mask[...] = same_slot(n_pass, lengths[sides[BATCH]])
    turned[:, 0:n_pass] = passages[...].T
    turned[:, n_pass:count] = queries[...].T
    puts = fetch([(turned, turned_out)], out_sems)
    finish_all(copies[:3])
    attended_grad[0:n_pass, :] = dot_nt(pass_here[...], out_here[...]).astype(BF16)
    attended_grad[n_pass:count, :] = dot_nt(query_here[...], out_here[...]).astype(BF16)
    heads = 16
    owner = lax.broadcasted_iota(jnp.int32, (heads, width), 1) // HEAD
    spread = jnp.where(owner == lax.broadcasted_iota(jnp.int32, (heads, width), 0), 1.0, 0.0)
    copies[3].wait()
    for tile in tiles(count):
        product = attended_grad[tile, :].astype(F32) * attended_here[tile, :].astype(F32)
        levels = dot_nt(spread, product, HIGH)
        for head in range(HEADS):
            inner[head, :, tile] = levels[head : head + 1, :]
    copies[4].wait()
    nothing = lambda hp: None
    attend_backward(mixed_here, attended_grad, stats, inner, mixed_grad, logit_grads, n_pass, n_query, width, query_mask, nothing)
    attend_backward(mixed_here, attended_grad, stats, inner, mixed_grad, logit_grads, 0, n_pass, width, mask, nothing)
    puts += fetch([(mixed_grad, grad_out)], out_sems, 1)
    shifts = [row_sum(mixed_grad[:, first : first + width].astype(F32)) for first in (0, 2 * width)]
    whole = jnp.concatenate([sums_pass[...] + sums_query[...], *shifts, jnp.zeros((6, width), F32)])
    deep_shift = shift_pass[...] + shift_query[...]
    if members:
        shard = width // members
        lane = lax.broadcasted_iota(jnp.int32, (width, TILE), 1)
        source = lax.broadcasted_iota(jnp.int32, (width, TILE), 0)
        row = lax.broadcasted_iota(jnp.int32, (16, TILE), 0)
        for leaf in range(members):
            chosen = jnp.where((source == lane + leaf * shard) & (lane < shard), 1.0, 0.0)
            block = jnp.dot(whole, chosen, preferred_element_type=F32, precision=HIGH)
            for i in range(3):
                part = deep_shift[:, (3 * leaf + i) * TILE : (3 * leaf + i + 1) * TILE]
                block = jnp.where(row == 10 + i, part, block)
            vectors[leaf] = block
        finish_all(copies[5:6])
        core = 1 - sides[0]
        wide = width // 2
        for piece in range(3):

            def emit(leaf, side, row, part):
                buffers[piece, leaf, side, row : row + part.shape[0], :] = part

            narrow = pl.ds(pl.multiple_of(core * wide + piece * TILE, TILE), TILE)
            outer_leaves(
                members, turned, mixed_grad.at[:, pl.ds(pl.multiple_of(core * 3 * wide + piece * wide, TILE), wide)],
                across_here, pass_here.at[:, narrow], query_here.at[:, narrow], emit,
            )
            vector_leaves(members, piece, core, vectors, buffers.shape[3] - 8, emit)
            puts += fetch([(buffers.at[piece], sent.at[piece])], out_sems, 2 + piece)
        late = copies[6:]
    else:
        vectors[0:16, :] = whole
        for i in range(deep_shift.shape[1] // width):
            vectors[16 + i : 17 + i, :] = deep_shift[:, i * width : (i + 1) * width]
        late = copies[5:]
    finish_all(late)
    for first in range(0, width, BLOCK):
        cols = slice(first, first + BLOCK)
        weight = in_here[cols, :]
        pass_out[:, cols] = (dot_nt(mixed_grad[0:n_pass, :], weight) + pass_sum_here[:, cols]).astype(BF16)
        query_out[:, cols] = (dot_nt(mixed_grad[n_pass:count, :], weight) + query_sum_here[:, cols]).astype(BF16)
    finish_all(puts)


def inner_leaves(members, low_p, low_q, grad_p, grad_q, turn_p, turn_q, hid_p, hid_q, emit, tell):
    width = low_p.shape[0]
    shard = width // members
    for first in range(0, width, width // 2):
        rows = slice(first, first + width // 2)
        part = dot(low_p[rows, :], grad_p[...]) + dot(low_q[rows, :], grad_q[...])
        for at in range(0, width // 2, shard // 2):
            leaf, side = divmod((first + at) // (shard // 2), 2)
            for block in range(part.shape[1] // TILE):
                emit(leaf, side, block * (shard // 2), part[at : at + shard // 2, block * TILE : (block + 1) * TILE])
    base = (shard // 2) * (grad_p.shape[1] // TILE)
    tell(slice(0, base), 0)
    for leaf in range(0, members, 4):
        span = slice(leaf * TILE, (leaf + 4) * TILE)
        part = dot(turn_p[...], hid_p[:, span]) + dot(turn_q[...], hid_q[:, span])
        for i in range(4):
            for side in (0, 1):
                emit(leaf + i, side, base, part[side * (width // 4) : (side + 1) * (width // 4), i * TILE : (i + 1) * TILE])
    tell(slice(base, base + width // 4), 1)


def outer_leaves(members, turned, grad, attended, branch_p, branch_q, emit):
    width = turned.shape[0]
    n_pass = branch_p.shape[0]
    shard = width // members
    for first in range(0, width, width // 2):
        rows = slice(first, first + width // 2)
        parts = [
            dot(turned[rows, :], grad[...]),
            dot(attended[rows, 0:n_pass], branch_p[...]) + dot(attended[rows, n_pass:], branch_q[...]),
        ]
        for at in range(0, width // 2, shard // 2):
            leaf, side = divmod((first + at) // (shard // 2), 2)
            block = 0
            for part in parts:
                for lane in range(0, part.shape[1], TILE):
                    emit(leaf, side, block * (shard // 2), part[at : at + shard // 2, lane : lane + TILE])
                    block += 1


def side_of(bit_at, mine, leaf, side):
    index = 2 * leaf + side
    high, bit, rest = index >> (bit_at + 1), (index >> bit_at) & 1, index & ((1 << bit_at) - 1)
    return jnp.where(mine == bit, 0, 1), (high << bit_at) + rest


def inner_kept(
    members, piece, bit_at, sides, low_pass, low_query, grad_pass, grad_query, reduce_pass, reduce_query, hidden_pass, hidden_query,
    received, leaves, stays,
    low_p, low_q, grad_p, grad_q, turn_p, turn_q, hid_p, hid_q, came, both, sems, out_sems,
):
    width = low_pass.shape[0]
    spread = grad_pass.shape[1]
    third = spread // 6
    cols = pl.ds(pl.multiple_of(sides[0] * (spread // 2) + piece * third, TILE), third)
    half = pl.ds(pl.multiple_of(sides[0] * (width // 2), TILE), width // 2)
    base = (width // members // 2) * (third // TILE)
    spans = [slice(0, base), slice(base, base + width // 4)]
    early = fetch(
        [
            (low_pass, low_p), (low_query, low_q), (grad_pass.at[:, cols], grad_p), (grad_query.at[:, cols], grad_q),
            (received.at[:, :, spans[0], :], came.at[:, :, spans[0], :]),
        ],
        sems,
    )
    late = fetch(
        [
            (reduce_pass.at[half, :], turn_p), (reduce_query.at[half, :], turn_q),
            (hidden_pass.at[piece], hid_p), (hidden_query.at[piece], hid_q),
            (received.at[:, :, spans[1], :], came.at[:, :, spans[1], :]),
        ],
        sems, 5,
    )
    puts = []

    def emit(leaf, side, row, part):
        rows = slice(row, row + part.shape[0])
        both[*side_of(bit_at, sides[1 + piece], leaf, side), rows, :] = part + came[leaf, side, rows, :]

    def tell(rows, place):
        pairs = [(both.at[1, :, rows, :], leaves.at[:, rows, :]), (both.at[0, :, rows, :], stays.at[:, rows, :])]
        puts.extend(fetch(pairs, out_sems, 2 * place))
        if place == 0:
            finish_all(late)

    finish_all(early)
    inner_leaves(members, low_p, low_q, grad_p, grad_q, turn_p, turn_q, hid_p, hid_q, emit, tell)
    finish_all(puts)


def outer_kept(
    members, places, sides, turned, mixed_grad, attended, branch_pass, branch_query, vectors, received, *refs
):
    leaves, stays = refs[0:6:2], refs[1:6:2]
    rows_here, grad, attended_here, branch_p, branch_q, came, both, sems, out_sems = refs[6:]
    width = turned.shape[0]
    wide = width // 2
    cols = pl.ds(pl.multiple_of(sides[0] * 3 * wide, TILE), 3 * wide)
    narrow = pl.ds(pl.multiple_of(sides[0] * wide, TILE), wide)
    copies = fetch(
        [
            (turned, rows_here), (mixed_grad.at[:, cols], grad), (attended, attended_here),
            (branch_pass.at[:, narrow], branch_p), (branch_query.at[:, narrow], branch_q),
        ]
        + [(received.at[piece], came.at[piece]) for piece in range(3)],
        sems,
    )
    finish_all(copies[:5])
    puts = []
    for piece in range(3):
        copies[5 + piece].wait()

        def emit(leaf, side, row, part):
            rows = slice(row, row + part.shape[0])
            both[piece, *side_of(places[piece], sides[1 + piece], leaf, side), rows, :] = part + came[piece, leaf, side, rows, :]

        outer_leaves(
            members, rows_here, grad.at[:, piece * wide : (piece + 1) * wide], attended_here,
            branch_p.at[:, piece * TILE : (piece + 1) * TILE], branch_q.at[:, piece * TILE : (piece + 1) * TILE], emit,
        )
        vector_leaves(members, piece, sides[0], vectors, both.shape[3] - 8, emit)
        puts += fetch([(both.at[piece, 1], leaves[piece]), (both.at[piece, 0], stays[piece])], out_sems, 2 * piece)
    finish_all(puts)


def vector_leaves(members, piece, core, vectors, row, emit):
    for leaf in range(members):
        for side in (0, 1):
            if piece == 0:
                part = jnp.where(core == 0, vectors[leaf, 8 * side : 8 * side + 8, :], 0.0)
            else:
                part = jnp.zeros((8, TILE), F32)
            emit(leaf, side, row, part)


def finish_inner(sides, mine, near, other, beyond, expand, reduce):
    rows, wide = expand.shape
    half = rows // 2
    blocks = wide // 6 // TILE
    deep = reduce.shape[1] // 2
    for far, pair in enumerate(((mine, near), (other, beyond))):
        core = jnp.bitwise_xor(sides[0], far)
        for piece in range(3):
            for there, source in enumerate(pair):
                side = pl.multiple_of(jnp.bitwise_xor(sides[1], there) * half, 8)
                for block in range(blocks):
                    at = core * (wide // 2) + (piece * blocks + block) * TILE
                    expand[pl.ds(side, half), pl.ds(pl.multiple_of(at, TILE), TILE)] = source[
                        piece, block * half : (block + 1) * half, :
                    ]
            parts = [source[piece, blocks * half :, :] for source in pair]
            low = jnp.where(sides[1] == 0, parts[0], parts[1])
            high = jnp.where(sides[1] == 0, parts[1], parts[0])
            reduce[piece * TILE : (piece + 1) * TILE, pl.ds(pl.multiple_of(core * deep, TILE), deep)] = (
                jnp.concatenate([low, high]).T
            )


def finish_outer(sides, mine, near, other, beyond, project_in, project_out, gains, biases, term_weight, term_bias, expand_bias):
    rows, wide = project_in.shape
    half = rows // 2
    for far, pair in enumerate(((mine, near), (other, beyond))):
        core = jnp.bitwise_xor(sides[0], far)
        for there, source in enumerate(pair):
            side = pl.multiple_of(jnp.bitwise_xor(sides[1], there) * half, 8)
            for piece in range(3):
                for block in range(4):
                    part = source[piece, block * half : (block + 1) * half, :]
                    if block < 3:
                        at = core * (wide // 2) + (piece * 3 + block) * TILE
                        project_in[pl.ds(side, half), pl.ds(pl.multiple_of(at, TILE), TILE)] = part
                    else:
                        at = core * (wide // 6) + piece * TILE
                        project_out[pl.ds(side, half), pl.ds(pl.multiple_of(at, TILE), TILE)] = part
    at = mine.shape[1] - 8
    parts = [
        jnp.where(sides[0] == 0, a[0, at:, :], b[0, at:, :]) for a, b in ((mine, other), (near, beyond))
    ]
    low = jnp.where(sides[1] == 0, parts[0], parts[1])
    high = jnp.where(sides[1] == 0, parts[1], parts[0])
    gains[...] = low[0:2, :rows]
    biases[0:2, :] = high[0:2, :rows]
    biases[2:6, :] = low[2:6, :rows]
    term_weight[...] = low[6:7, :rows]
    term_bias[...] = low[7:8, 0:1]
    for i in range(expand_bias.shape[1] // TILE):
        expand_bias[:, i * TILE : (i + 1) * TILE] = high[2 + i : 3 + i, :]


def run(kernel, outs, kinds, scratch, args, after=(), aliases=None, limit=58):
    specs = {"s": IN_SMEM, "v": IN_VMEM, "h": IN_PLACE, "a": IN_PLACE}
    shapes = [
        pltpu.HBM(dims, dtype) if kind == "h" else jax.ShapeDtypeStruct(dims, dtype) for kind, dims, dtype in outs
    ]
    given = [
        pltpu.with_memory_space_constraint(a, pltpu.HBM) if kind == "h" else a for a, kind in zip(args, kinds)
    ]
    many = len(outs) > 1
    known = len(args)

    def body(*refs):
        kernel(*refs[:known], *refs[known + len(after) :])

    return pl.pallas_call(
        body,
        out_shape=shapes if many else shapes[0],
        in_specs=[specs[kind] for kind in kinds] + [IN_PLACE] * len(after),
        out_specs=[specs[o[0]] for o in outs] if many else specs[outs[0][0]],
        scratch_shapes=scratch,
        input_output_aliases=aliases or {},
        compiler_params=pltpu.CompilerParams(vmem_limit_bytes=limit << 20),

    )(*given, *after)


def contract_rows(left, right):
    return lax.dot_general(
        left, right, (((0,), (0,)), ((), ())), preferred_element_type=F32
    )


GROUP_FIRST = (("pb", 2), ("pa", 1))
ROW_FIRST = (("pa", 1), ("pb", 2))


def swap(value, axis, distance):
    return lax.ppermute(
        value, axis, [(i, i ^ distance) for i in range(lax.axis_size(axis))]
    )


def bit(axis, distance):
    return (lax.axis_index(axis) >> (distance.bit_length() - 1)) & 1


def pick(value, index, dim):
    return lax.dynamic_index_in_dim(value, index, dim, keepdims=False)


def group_gather(mine):
    distance = 1
    while distance < lax.axis_size("pa"):
        other = swap(mine, "pa", distance)
        mine = jnp.where(
            bit("pa", distance) == 0, jnp.concatenate([mine, other]), jnp.concatenate([other, mine])
        )
        distance *= 2
    return mine


def group_scatter(whole):
    distance = lax.axis_size("pa") // 2
    while distance:
        halves = whole.reshape((2, -1) + whole.shape[1:])
        mine = bit("pa", distance)
        whole = pick(halves, mine, 0) + swap(pick(halves, 1 - mine, 0), "pa", distance)
        distance //= 2
    return whole


def steps_of(order):
    steps = [(axis, distance) for axis, distance in order]
    distance = 2
    while distance < lax.axis_size("pa"):
        steps.append(("pa", distance))
        distance *= 2
    return steps


def tree_sum(send, keep, order):
    names = []
    distance = lax.axis_size("pa") // 2
    while distance:
        names.append(("pa", distance))
        distance //= 2
    names.append(("pb", 2))
    received = swap(send, "pb", 1)
    for axis, distance in steps_of(order):
        dim = names.index((axis, distance))
        names.pop(dim)
        mine = bit(axis, distance)
        send = pick(keep, 1 - mine, dim) + pick(received, 1 - mine, dim)
        keep = pick(keep, mine, dim) + pick(received, mine, dim)
        received = swap(send, axis, distance)
    mine = keep + received
    other = swap(mine, "pb", 2)
    high = bit("pb", 2)
    return jnp.where(high == 0, jnp.stack([mine, other]), jnp.stack([other, mine]))


def cut(matrix):
    bits = lax.axis_size("pa").bit_length() - 1
    rows = matrix.shape[0] >> (bits + 1)
    return matrix.reshape((2,) * (bits + 1) + (rows, matrix.shape[1]))


def summed_rows(left, right, order):
    core = bit("pb", 1)
    half = right.shape[1] // 2
    parts = [
        cut(contract_rows(left, lax.dynamic_slice_in_dim(right, side * half, half, axis=1)))
        for side in (1 - core, core)
    ]
    mine = tree_sum(parts[0], parts[1], order)
    mine = mine.reshape(-1, half)
    other = swap(mine, "pb", 1)
    return jnp.where(
        core == 0, jnp.concatenate([mine, other], 1), jnp.concatenate([other, mine], 1)
    )


def total_of_all(value):
    distance = 1
    while distance < lax.axis_size("pb"):
        value = value + swap(value, "pb", distance)
        distance *= 2
    distance = 1
    while distance < lax.axis_size("pa"):
        value = value + swap(value, "pa", distance)
        distance *= 2
    return value


BATCH_IN_GROUP, BATCH = 5, 6
LEAF_BITS = (("pa", 4), ("pa", 2), ("pa", 1), ("pb", 2))
PIECE_ORDERS = (
    (("pb", 2), ("pa", 1), ("pa", 2), ("pa", 4)),
    (("pa", 1), ("pa", 2), ("pb", 2), ("pa", 4)),
    (("pa", 2), ("pb", 2), ("pa", 1), ("pa", 4)),
)
PLACES = tuple(len(LEAF_BITS) - 1 - LEAF_BITS.index(order[0]) for order in PIECE_ORDERS)


def begun(parts):
    held = []
    for (leaving, staying), order in zip(parts, PIECE_ORDERS):
        rest = tuple(b for b in LEAF_BITS if b != order[0])
        held.append(([(staying, rest), (swap(leaving, *order[0]), rest)], (order[0],)))
    return held


def chosen(names, settled, current=None):
    return tuple(1 if name == current else 0 if name in settled else None for name in names)


def part_of(array, names, settled, current, rows):
    wants = chosen(names, settled, current)
    starts = [0 if want is None else bit(*name) ^ want for name, want in zip(names, wants)]
    sizes = [2 if want is None else 1 for want in wants]
    part = lax.dynamic_slice(array.reshape((2,) * len(names) + (rows, TILE)), starts + [0, 0], sizes + [rows, TILE])
    return part.reshape((2,) * wants.count(None) + (rows, TILE))


def onward(held, step, sent):
    moved = []
    for (terms, settled), order, leaving in zip(held, PIECE_ORDERS, sent):
        left = tuple(b for b in LEAF_BITS if b not in settled and b != order[step])
        moved.append((terms + [(swap(leaving, *order[step]), left)], settled + (order[step],)))
    return moved


def advance(held, step, rows):
    sent = []
    for (terms, settled), order in zip(held, PIECE_ORDERS):
        sent.append(sum(part_of(array, names, settled, order[step], rows) for array, names in terms))
    return onward(held, step, sent)


def fold(plans, through, joined, facts, *refs):
    count = sum(len(plan) for plan in plans)
    terms = refs[:count]
    outs = refs[count + through : count + through + (1 if joined else len(plans))]
    scratch = refs[count + through + len(outs) + through :]
    sems, out_sems = scratch[-2:]
    pairs = []
    at = 0
    for plan in plans:
        for wants in plan:
            index = tuple(
                slice(None) if want is None else jnp.bitwise_xor(facts[len(LEAF_BITS) - LEAF_BITS.index(name)], want) for name, want in wants
            )
            pairs.append((terms[at].at[index], scratch[at]))
            at += 1
    copies = fetch(pairs, sems)
    puts = []
    at = 0
    for i, plan in enumerate(plans):
        finish_all(copies[at : at + len(plan)])
        total = scratch[at][...]
        for k in range(1, len(plan)):
            total = total + scratch[at + k][...]
        scratch[at][...] = total
        puts += fetch([(scratch[at], outs[0].at[i] if joined else outs[i])], out_sems, i)
        at += len(plan)
    finish_all(puts)


def fold_by_kernel(facts, held, step, rows, through=(), after=(), joined=False):
    plans = []
    args = []
    scratch = []
    outs = []
    for (terms, settled), order in zip(held, PIECE_ORDERS):
        plan = []
        for array, names in terms:
            wants = chosen(names, settled, order[step])
            plan.append(tuple(zip(names, wants)))
            args.append(array.reshape((2,) * len(names) + (rows, TILE)))
            dims = (2,) * wants.count(None) + (rows, TILE)
            scratch.append(pltpu.VMEM(dims, F32))
        plans.append(plan)
        outs.append(("h", dims, F32))
    if joined:
        outs = [("h", (len(plans), rows, TILE), F32)]
    done = run(
        partial(fold, plans, len(through), joined),
        outs + [("h", a.shape, a.dtype) for a in through],
        "s" + "a" * len(args) + "h" * len(through),
        scratch + [pltpu.SemaphoreType.DMA((len(args),)), pltpu.SemaphoreType.DMA((len(plans),))],
        (facts, *args, *through),
        after,
        {1 + len(args) + i: len(outs) + i for i in range(len(through))},
        12,
    )
    return done if len(outs) + len(through) > 1 else [done]


def advance_by_kernel(facts, held, step, rows, through=(), after=()):
    done = fold_by_kernel(facts, held, step, rows, through, after)
    return onward(held, step, done[:3]), done[3:]


def last_exchange(facts, held, rows, through=()):
    step = len(LEAF_BITS) - 1
    name = PIECE_ORDERS[0][step]
    sent, *through = fold_by_kernel(facts, held, step, rows, through, joined=True)
    came = swap(sent, *name)
    total = jnp.stack(
        [sum(part_of(array, names, settled + (name,), None, rows) for array, names in terms) for terms, settled in held]
    )
    return total + came, through


def on_device(
    passages, queries, passage_ids, query_ids, batch_length, query_batch, project_in, project_out, expand_weight,
    expand_bias, reduce_weight, norm_gains, biases, term_weight, term_bias, out_grad, score_grad,
):
    members = lax.axis_size("pa")
    member_index = lax.axis_index("pa")
    local_batch = member_index // (members // BATCH_PB)
    facts = jnp.stack(
        [bit("pb", 1), *(bit(*name) for name in reversed(LEAF_BITS)), local_batch, lax.axis_index("pb") * BATCH_PB + local_batch]
    )
    n_pass, width = passages.shape
    n_query = queries.shape[0]
    count = n_pass + n_query
    deep = expand_weight.shape[1]
    slots = score_grad.shape[1]
    bias_row = expand_bias[None]
    term_row = term_weight[None]

    blocks = deep // (2 * BLOCK)
    by_three = (3, n_pass, deep // 3)
    weights = [pltpu.VMEM(expand_weight.shape, BF16), pltpu.VMEM(reduce_weight.shape, BF16)]

    def vmem(*dims, dtype=BF16):
        return pltpu.VMEM(dims, dtype)

    def sems(number):
        return pltpu.SemaphoreType.DMA((number,))

    (
        mixed, attended, attended_turned, stats, normed_one, inverse_one, low,
        hidden_query, slope_query, unit_query, scale_query, pre_query, known,
    ) = run(
        forward_one,
        [
            ("h", (count, 3 * width), BF16), ("h", (count, width), BF16),
            ("h", (width, count), BF16), ("v", (HEADS, 1, count), F32), ("h", (count, width), F32),
            ("v", (count, 1), F32), ("h", (count, width), BF16), ("h", (3, n_query, deep // 3), BF16),
            ("h", (n_query, deep), BF16), ("v", (n_query, width), F32), ("v", (n_query, 1), F32),
            ("v", (n_query, 1), F32), ("v", (1, 3, n_query), F32),
        ],
        "ssvvhhhhvvvvsvs",
        [
            vmem(*project_in.shape), vmem(*project_out.shape), *weights, vmem(count, 3 * width), vmem(count, width),
            vmem(width, count), vmem(count, width, dtype=F32), vmem(count, width), vmem(n_query, deep), vmem(n_query, deep),
            vmem(n_pass, n_pass, dtype=F32), vmem(n_query, n_query, dtype=F32), vmem(count, width, dtype=F32),
            sems(6), sems(6 + deep // TILE),
        ],
        (facts, batch_length, passages, queries, project_in, project_out, expand_weight, reduce_weight, bias_row, norm_gains,
         biases, term_row, term_bias, query_ids[None], query_batch),
    )
    known = group_gather(known)
    hidden, slope, unit_pass, scale_pass, pre_pass, passage_out = run(
        forward_two,
        [
            ("h", by_three, BF16), ("h", (n_pass, deep), BF16), ("h", (n_pass, width), F32),
            ("v", (n_pass, 1), F32), ("v", (n_pass, 1), F32), ("h", (n_pass, width), BF16),
        ],
        "hhhhvvvvs",
        [
            vmem(n_pass, width), vmem(n_pass, width, dtype=F32), *weights, vmem(n_pass, deep), vmem(n_pass, deep),
            vmem(n_pass, width, dtype=F32), vmem(n_pass, width), vmem(n_pass, width, dtype=F32),
            sems(3 + blocks), sems(deep // TILE + blocks + 2 * (n_pass // TILE)),
        ],
        (low, normed_one, expand_weight, reduce_weight, bias_row, norm_gains, biases, term_row, term_bias),
    )
    scores, pass_term_grad, query_part = run(
        match,
        [("v", score_grad.shape[::-1], F32), ("v", (n_pass, 1), F32), ("v", (members, 1, n_query), F32)],
        "ssvvvv",
        [],
        (facts, batch_length, known, score_grad.T, passage_ids[None], pre_pass),
    )
    query_term_grad = group_scatter(query_part)

    def back_outs(rows):
        return [
            ("h", (width, rows), BF16), ("h", (rows, deep), BF16), ("h", (width, rows), BF16),
            ("h", (rows, width), F32), ("h", (rows, width), BF16), ("v", (8, width), F32), ("v", (1, deep), F32),
        ]

    back_kinds = "vvhhvhhvhhhvvv"

    def back_scratch(rows):
        return [
            vmem(rows, width), vmem(rows, width, dtype=F32), vmem(rows, deep), vmem(rows, width, dtype=F32), vmem(rows, width),
            *weights, vmem(rows, deep), vmem(width, rows), vmem(width, rows), vmem(rows, width, dtype=F32), vmem(rows, width),
            vmem(rows, width, dtype=F32), vmem(rows, width),
            sems(3 + 2 * blocks + 2 * (rows // TILE)), sems(2 + blocks + 2 * (rows // TILE)),
        ]

    def back_args(term_grad, pre, unit, scale, slope_here):
        return (term_grad, pre, out_grad, unit, scale, slope_here, normed_one, inverse_one, low,
                expand_weight, reduce_weight, norm_gains, biases, term_row)

    rg_pass, eg_pass, low_pass, one_pass, bg_pass, sums_pass, shift_pass = run(
        partial(backward_rows, True, 0), back_outs(n_pass), back_kinds, back_scratch(n_pass),
        back_args(pass_term_grad, pre_pass, unit_pass, scale_pass, slope),
    )
    fits = deep // members == 3 * TILE
    shard = width // members
    leaf_rows = (deep // 6 // TILE * (shard // 2) + width // 4, 4 * (shard // 2) + 8)
    if fits:
        dims = (members, 2, leaf_rows[0], TILE)
        third = deep // 6
        (
            rg_query, eg_query, low_query, one_query, bg_query, sums_query, shift_query, *sent
        ) = run(
            partial(backward_query, members, n_pass),
            back_outs(n_query) + [("h", dims, F32)] * 3,
            "s" + back_kinds + "hhhhh",
            back_scratch(n_query)
            + [
                vmem(width, n_pass), vmem(n_pass, deep // 2), vmem(width // 2, n_pass), vmem(*by_three),
                vmem(3, n_query, deep // 3), vmem(3, *dims, dtype=F32), sems(5), sems(6),
            ],
            (facts,) + back_args(query_term_grad[0], pre_query, unit_query, scale_query, slope_query)
            + (low_pass, eg_pass, rg_pass, hidden, hidden_query),
        )
        came = [swap(part, "pb", 1) for part in sent]
        parts = []
        for piece, order in enumerate(PIECE_ORDERS):
            half = (leaf_rows[0], TILE)
            parts.append(
                run(
                    partial(inner_kept, members, piece, PLACES[piece]),
                    [("h", (members,) + half, F32)] * 2,
                    "s" + "h" * 8 + "a",
                    [
                        vmem(width, n_pass), vmem(width, n_query), vmem(n_pass, third), vmem(n_query, third),
                        vmem(width // 2, n_pass), vmem(width // 2, n_query), vmem(n_pass, deep // 3), vmem(n_query, deep // 3),
                        vmem(*dims, dtype=F32), vmem(2, members, *half, dtype=F32), sems(10), sems(4),
                    ],
                    (facts, low_pass, low_query, eg_pass, eg_query, rg_pass, rg_query, hidden,
                     hidden_query, came[piece]),
                    limit=18,
                )
            )
        inner = begun(parts)
        pins = tuple(leaving for leaving, _ in parts)
        extra = [("v", (members, 16, TILE), F32)]
        last = [("h", (3, members, 2, leaf_rows[1], TILE), F32)]
    else:
        rg_query, eg_query, low_query, one_query, bg_query, sums_query, shift_query = run(
            partial(backward_rows, False, n_pass), back_outs(n_query), back_kinds, back_scratch(n_query),
            back_args(query_term_grad[0], pre_query, unit_query, scale_query, slope_query),
        )
        pins = ()
        extra = [("v", (16 + deep // width, width), F32)]
        last = []
    mixed_grad, turned, vectors, passage_grad, query_grad, *sent = run(
        partial(backward_attention, members if fits else 0),
        [("h", (count, 3 * width), BF16), ("h", (width, count), BF16)]
        + extra
        + [("v", (n_pass, width), BF16), ("v", (n_query, width), BF16)]
        + last,
        "ssvvhhhhhv" + "hhhh" + "vvvv",
        [
            vmem(*project_out.shape), vmem(n_pass, width), vmem(n_query, width), vmem(count, 3 * width), vmem(count, width),
            vmem(count, 3 * width), vmem(width, count), vmem(count, width), vmem(HEADS, 1, count, dtype=F32),
            vmem(2, n_pass, n_pass), vmem(n_pass, n_pass, dtype=F32), vmem(n_query, n_query, dtype=F32),
            vmem(width, count), vmem(*project_in.shape), vmem(n_pass, width, dtype=F32), vmem(n_query, width, dtype=F32),
            vmem(*(last[0][1] if fits else (8, TILE)), dtype=F32), sems(9), sems(5),
        ],
        (facts, batch_length, passages, queries, bg_pass, bg_query, project_out, mixed, attended, stats, attended_turned, project_in,
         one_pass, one_query, sums_pass, sums_query, shift_pass, shift_query),
        pins,
    )
    if fits:
        inner, sent = advance_by_kernel(facts, inner, 1, leaf_rows[0], tuple(sent))
        half = (leaf_rows[1], TILE)
        dims = (3, members, 2) + half
        parts = run(
            partial(outer_kept, members, PLACES),
            [("h", (members,) + half, F32)] * 6,
            "s" + "h" * 5 + "va",
            [
                vmem(width, count), vmem(count, 3 * width // 2), vmem(width, count), vmem(n_pass, width // 2),
                vmem(n_query, width // 2), vmem(*dims, dtype=F32), vmem(3, 2, members, *half, dtype=F32), sems(8), sems(6),
            ],
            (facts, turned, mixed_grad, attended_turned, bg_pass, bg_query, vectors, swap(sent[0], "pb", 1)),
            limit=24,
        )
        inner, _ = advance_by_kernel(facts, inner, 2, leaf_rows[0], after=tuple(parts[0:6:2]))
        inner_mine, late = last_exchange(facts, inner, leaf_rows[0], (parts[2],))
        outer = begun([parts[0:2], (late[0], parts[3]), parts[4:6]])
        for step in (1, 2):
            outer = advance(outer, step, leaf_rows[1])
        outer_mine, _ = last_exchange(facts, outer, leaf_rows[1])

        def finish(kernel, mine, outs):
            near = swap(mine, "pb", 2)
            args = (facts, mine, near, swap(mine, "pb", 1), swap(near, "pb", 1))
            return run(kernel, outs, "svvvv", [], args, limit=12)

        expand_total, reduce_total = finish(
            finish_inner, inner_mine, [("v", (shard, deep), F32), ("v", (deep // members, width), F32)]
        )
        in_total, out_total, gains_grad, biases_grad, term_grad, bias_grad, expand_shift = finish(
            finish_outer, outer_mine,
            [
                ("v", (shard, 3 * width), F32), ("v", (shard, width), F32), ("v", (2, shard), F32), ("v", (6, shard), F32),
                ("v", (1, shard), F32), ("v", (1, 1), F32), ("v", (1, deep // members), F32),
            ],
        )
    else:
        in_order = [h.reshape(3, h.shape[1], -1, TILE).transpose(1, 2, 0, 3).reshape(-1, deep) for h in (hidden, hidden_query)]
        whole = [jnp.concatenate(pair, axis) for pair, axis in (
            (in_order, 0), ((rg_pass, rg_query), 1), ((eg_pass, eg_query), 0), ((bg_pass, bg_query), 0),
        )]
        reduce_total = summed_rows(whole[0], whole[1].T, ROW_FIRST)
        expand_total = summed_rows(low, whole[2], GROUP_FIRST)
        out_total = summed_rows(attended, whole[3], GROUP_FIRST)
        in_total = summed_rows(turned.T, mixed_grad, ROW_FIRST)
        vectors = total_of_all(vectors)
        mine = lax.dynamic_slice_in_dim(vectors[:10], member_index * shard, shard, axis=1)
        expand_shift = lax.dynamic_slice_in_dim(
            vectors[16:].reshape(-1), member_index * (deep // members), deep // members
        )
        gains_grad = mine[:2]
        biases_grad = jnp.concatenate([mine[8:10], mine[2:6]])
        term_grad = mine[6]
        bias_grad = mine[7, :1]
    return (
        scores.T,
        passage_out,
        passage_grad,
        query_grad,
        in_total,
        out_total,
        expand_total,
        expand_shift.reshape(-1),
        reduce_total,
        gains_grad,
        biases_grad,
        term_grad.reshape(-1),
        bias_grad.reshape(-1),
    )


def solution(mesh):
    return jax.shard_map(
        on_device,
        mesh=mesh,
        in_specs=(
            P(("pb", "pa"), None),
            P(("pb", "pa"), None),
            P(("pb", "pa")),
            P(("pb", "pa")),
            P(),
            P(("pb", "pa")),
            P(),
            P(),
            P(),
            P(),
            P(),
            P(),
            P(),
            P(),
            P(),
            P(("pb", "pa"), None),
            P("pb", "pa"),
        ),
        out_specs=(
            P("pb", "pa"),
            P(("pb", "pa"), None),
            P(("pb", "pa"), None),
            P(("pb", "pa"), None),
            P("pa", None),
            P("pa", None),
            P("pa", None),
            P("pa"),
            P("pa", None),
            P(None, "pa"),
            P(None, "pa"),
            P("pa"),
            P(),
        ),
        check_vma=False,
    )
```

```python
from functools import partial

import jax
import jax.numpy as jnp
from jax import lax
from jax.experimental import pallas as pl
from jax.experimental.pallas import tpu as pltpu
from jax.sharding import PartitionSpec as P

HEADS = 12
HEAD = 64
LONG = 512
QLEN = 32
BATCH_PB = 4

NEG = -1e30
HIGH = lax.Precision.HIGHEST
LN_EPS = 1e-12
SCALE = HEAD ** (-0.5)
BLOCK = 256
TILE = 128
F32 = jnp.float32
BF16 = jnp.bfloat16

IN_VMEM = pl.BlockSpec(memory_space=pltpu.VMEM)
IN_SMEM = pl.BlockSpec(memory_space=pltpu.SMEM)
IN_PLACE = pl.BlockSpec(memory_space=pl.ANY)


def shape(dims, dtype):
    return (tuple(dims), dtype)


def dot(left, right):
    return jnp.dot(left, right, preferred_element_type=F32)


def dot_nt(left, right, precision=None):
    return lax.dot_general(
        left, right, (((1,), (1,)), ((), ())), preferred_element_type=F32, precision=precision
    )


def dot_tn(left, right):
    return lax.dot_general(left, right, (((0,), (0,)), ((), ())), preferred_element_type=F32)


def columns(index, width, first=0):
    return pl.ds(pl.multiple_of(first + index * width, TILE), width)


def tiles(count):
    return [slice(first, first + TILE) for first in range(0, count, TILE)]


def row_sum(matrix):
    return jnp.sum(matrix, axis=0, keepdims=True)


def fetch(pairs, sems, first=0):
    copies = [
        pltpu.make_async_copy(source, target, sems.at[first + i]) for i, (source, target) in enumerate(pairs)
    ]
    for copy in copies:
        copy.start()
    return copies


def finish_all(copies):
    for copy in copies:
        copy.wait()


def norm_forward(total):
    centred = total - jnp.mean(total, axis=-1, keepdims=True)
    inverse = lax.rsqrt(jnp.mean(centred * centred, axis=-1, keepdims=True) + LN_EPS)
    return centred * inverse, inverse


def norm_backward(scaled, normed, inverse):
    centred = scaled - jnp.mean(scaled, axis=-1, keepdims=True)
    return inverse * (centred - normed * jnp.mean(scaled * normed, axis=-1, keepdims=True))


def head_lanes(sub):
    lane = lax.broadcasted_iota(jnp.int32, (1, 2 * HEAD), 1)
    return (lane // HEAD) == sub


def same_slot(count, length):
    rows = lax.broadcasted_iota(jnp.int32, (count, count), 0) // length
    cols = lax.broadcasted_iota(jnp.int32, (count, count), 1) // length
    return jnp.where(rows == cols, 0.0, NEG)


def attend(mixed, turned, stats, first, count, width, mask, unroll):
    rows = slice(first, first + count)

    def pair(hp, carry):
        key = mixed[rows, columns(hp, 2 * HEAD, width)]
        value = mixed[rows, columns(hp, 2 * HEAD, 2 * width)].T
        for sub in (0, 1):
            key_here = jnp.where(head_lanes(sub), key, jnp.zeros_like(key))
            logits = dot_nt(key_here, mixed[rows, columns(hp, 2 * HEAD)]) + mask[...]
            highest = jnp.max(logits, axis=0, keepdims=True)
            powers = jnp.exp(logits - highest)
            total = jnp.sum(powers, axis=0, keepdims=True)
            weights = (powers * (1.0 / total)).astype(BF16)
            out_rows = pl.ds(pl.multiple_of((2 * hp + sub) * HEAD, HEAD), HEAD)
            turned[out_rows, rows] = dot(value[sub * HEAD : (sub + 1) * HEAD], weights).astype(BF16)
            stats[2 * hp + sub, :, rows] = highest + jnp.log(total)
        return carry

    lax.fori_loop(0, HEADS // 2, pair, 0, unroll=unroll)


def grow(rows, first, count, expand, cols, expand_bias, hidden, slope):
    for at in range(0, count, min(BLOCK, count)):
        tile = slice(at, at + min(BLOCK, count))
        value = dot(rows[first + at : first + tile.stop, :], expand[:, cols]) + expand_bias[:, cols]
        lower = 0.5 + 0.5 * lax.erf(value * (0.5**0.5))
        hidden[tile, cols] = (value * lower).astype(BF16)
        density = jnp.exp(-0.5 * value * value) * 0.3989422804014327
        slope[tile, cols] = (lower + value * density).astype(BF16)


def by_piece(block, hidden, out):
    shard, piece = lax.div(block, 3), lax.rem(block, 3)
    return hidden.at[:, columns(block, TILE)], out.at[piece, :, columns(shard, TILE)]


def close_forward(total, normed_one, first, count, at, gains, biases, term_weight, term_bias, normed, inverse, pre, passage_out, tell):
    for i, tile in enumerate(tiles(count)):
        base = normed_one[first + tile.start : first + tile.stop, :] * gains[0:1, :] + biases[4:5, :]
        unit, scale = norm_forward(base + total[at + tile.start : at + tile.stop, :] + biases[3:4, :])
        normed[tile, :] = unit
        inverse[tile, :] = scale
        second = unit * gains[1:2, :] + biases[5:6, :]
        pre[tile, :] = jnp.sum(second * term_weight[...], axis=-1, keepdims=True) + term_bias[0]
        if passage_out is not None:
            passage_out[tile, :] = second.astype(BF16)
        tell(i, tile)


def softplus(value):
    return jnp.maximum(value, 0.0) + jnp.log1p(jnp.exp(-jnp.abs(value)))


def sigmoid(value):
    return 1.0 / (1.0 + jnp.exp(-value))


def forward_layer(
    facts, lengths, passages, queries, project_in, project_out, expand, reduce, expand_bias, gains, biases,
    term_weight, term_bias, query_ids, query_batch, score_grad, passage_ids,
    mixed_out, attended_out, turned_out, stats, normed_out, inverse_one, low_out,
    hidden_query_out, slope_query_out, unit_query, scale_query, pre_query,
    hidden_out, slope_out, unit_out, scale_pass, pre_pass, passage_out, known,
    in_here, out_here, expand_here, reduce_here, mixed, attended, turned, normed_one, low, hidden_query, slope_query,
    hidden, slope, unit_pass, second, mask, query_mask, total, sems, out_sems,
):
    n_pass, width = passages.shape
    n_query = queries.shape[0]
    count = n_pass + n_query
    parts = [slice(i * width, (i + 1) * width) for i in range(3)]
    copies = fetch(
        [(project_in.at[:, part], in_here.at[:, part]) for part in parts]
        + [(project_out, out_here), (expand, expand_here), (reduce, reduce_here)],
        sems,
    )
    mask[...] = same_slot(n_pass, lengths[facts[BATCH]])
    query_mask[...] = same_slot(n_query, QLEN)
    for part in range(3):
        copies[part].wait()
        for source, first, rows in ((passages, 0, n_pass), (queries, n_pass, n_query)):
            value = dot(source[...], in_here[:, parts[part]])
            if part != 1:
                value = value + biases[part // 2 : part // 2 + 1, :]
            if part == 0:
                value = value * SCALE
            mixed[first : first + rows, parts[part]] = value.astype(BF16)
    puts = fetch([(mixed, mixed_out)], out_sems)
    attend(mixed, turned, stats, n_pass, n_query, width, query_mask, HEADS // 2)
    attend(mixed, turned, stats, 0, n_pass, width, mask, 3)
    attended[...] = turned[...].T
    puts += fetch([(turned, turned_out), (attended, attended_out)], out_sems, 1)
    copies[3].wait()
    total[...] = dot(attended[...], out_here[...])
    for tile in reversed(tiles(count)):
        source, at = (passages, tile.start) if tile.start < n_pass else (queries, tile.start - n_pass)
        unit, scale = norm_forward(source[at : at + TILE, :].astype(F32) + total[tile, :] + biases[2:3, :])
        normed_one[tile, :] = unit
        inverse_one[tile, :] = scale
        low[tile, :] = (unit * gains[0:1, :] + biases[4:5, :]).astype(BF16)
    puts += fetch([(normed_one, normed_out), (low, low_out)], out_sems, 3)
    copies[4].wait()
    wide = 2 * BLOCK
    per = wide // TILE
    blocks = expand.shape[1] // wide
    at = 5
    for j in range(blocks):
        cols = columns(j, wide)
        grow(low, 0, n_pass, expand_here, cols, expand_bias, hidden, slope)
        grow(low, n_pass, n_query, expand_here, cols, expand_bias, hidden_query, slope_query)
        pairs = [(slope.at[:, cols], slope_out.at[:, cols]), (slope_query.at[:, cols], slope_query_out.at[:, cols])]
        for i in range(j * per, (j + 1) * per):
            pairs += [by_piece(i, hidden, hidden_out), by_piece(i, hidden_query, hidden_query_out)]
        puts += fetch(pairs, out_sems, at)
        at += len(pairs)
    copies[5].wait()
    total[0:n_pass, :] = dot(hidden[...], reduce_here[...])
    total[n_pass:count, :] = dot(hidden_query[...], reduce_here[...])

    def tell(i, tile):
        pairs = [(unit_pass.at[tile, :], unit_out.at[tile, :]), (second.at[tile, :], passage_out.at[tile, :])]
        puts.extend(fetch(pairs, out_sems, at + 2 * i))

    close = (gains, biases, term_weight, term_bias)
    close_forward(total, normed_one, 0, n_pass, 0, *close, unit_pass, scale_pass, pre_pass, second, tell)
    close_forward(
        total, normed_one, n_pass, n_query, n_pass, *close, unit_query, scale_query, pre_query, None, lambda i, tile: None
    )
    known[...] = jnp.zeros_like(known)
    known[0, 0:1, :] = jnp.broadcast_to(softplus(pre_query[...]), (n_query, TILE)).T[0:1, :]
    known[0, 1:2, :] = query_ids[...].astype(F32)
    owner = lax.broadcasted_iota(jnp.int32, (1, n_query), 1) // QLEN
    tags = jnp.zeros((1, n_query), F32)
    for query in range(n_query // QLEN):
        tags = jnp.where(owner == query, query_batch[query].astype(F32), tags)
    known[0, 2:3, :] = tags
    slots, number = score_grad.shape
    row = 3
    for first in range(0, number, TILE):
        size = min(TILE, number - first)
        known[0, row : row + slots, 0:size] = score_grad[:, first : first + size]
        row += slots
    terms = jnp.broadcast_to(softplus(pre_pass[...]), (n_pass, TILE)).T[0:1, :]
    for source in (terms, passage_ids[...].astype(F32)):
        for tile in tiles(n_pass):
            known[0, row : row + 1, :] = source[:, tile]
            row += 1
    finish_all(puts)


def match(facts, lengths, known, score_grad, passage_ids, pre, scores, pass_grad, query_grad):
    members, _, tokens = known.shape
    n_pass = passage_ids.shape[1]
    slots, queries = scores.shape
    per_query = queries // members
    together = min(members, 8)
    slot = lax.broadcasted_iota(jnp.int32, (n_pass, slots), 0) // lengths[facts[BATCH]]
    table = slot == lax.broadcasted_iota(jnp.int32, (n_pass, slots), 1)
    placed = jnp.where(table, softplus(pre[...]), 0.0).astype(BF16)
    who = lax.broadcasted_iota(jnp.int32, (queries, together * tokens), 0)
    token = lax.broadcasted_iota(jnp.int32, (queries, together * tokens), 1) // QLEN
    mine = jnp.broadcast_to(passage_ids[...].astype(F32), (8, n_pass)).T[:, 0:1]

    def several(c, carry):
        scored, placed_grads = carry
        first = c * together
        wide = jnp.concatenate([known[first + i, 0:3, :] for i in range(together)], axis=1)
        matches = jnp.where(mine == wide[1:2, :], 1.0, 0.0).astype(BF16)
        per_token = dot_tn(placed, matches)
        masked = jnp.where(wide[2:3, :] == facts[BATCH_IN_GROUP].astype(F32), 1.0, 0.0)
        weighted = wide[0:1, :] * masked
        spread = jnp.where(who == token + first * per_query, 1.0, 0.0)
        grad = jnp.dot(score_grad[...], spread, preferred_element_type=F32, precision=HIGH)
        placed_grads = placed_grads + dot_nt(matches, (grad * weighted).astype(BF16))
        scored = scored + dot_nt(per_token * weighted, spread, HIGH)
        return scored, placed_grads

    carry = (jnp.zeros(scores.shape, F32), jnp.zeros((n_pass, slots), F32))
    if members == together:
        scored, placed_grads = several(0, carry)
    else:
        scored, placed_grads = lax.fori_loop(0, members // together, several, carry)
    scores[...] = scored
    pass_grad[...] = jnp.sum(jnp.where(table, placed_grads, 0.0), axis=1, keepdims=True)
    me = facts[MEMBER]
    own = known[me, 0:3, :]
    ids = jnp.broadcast_to(own[1:2, :], (TILE, tokens)).T[:, 0:1]
    chunks = -(-queries // TILE)
    who = lax.broadcasted_iota(jnp.int32, (TILE, tokens), 0)
    token = lax.broadcasted_iota(jnp.int32, (TILE, tokens), 1) // QLEN + me * per_query
    spreads = [jnp.where(who + i * TILE == token, 1.0, 0.0) for i in range(chunks)]
    place = lax.broadcasted_iota(jnp.int32, (slots, n_pass), 1)
    slot = lax.broadcasted_iota(jnp.int32, (slots, n_pass), 0)
    per_batch = members // BATCH_PB
    first_batch = facts[BATCH] - facts[BATCH_IN_GROUP]

    def against(n, total):
        batch = lax.div(n, per_batch)
        row = 3
        grad = jnp.zeros((slots, tokens), F32)
        for spread in spreads:
            part = known[n, row : row + slots, :]
            grad = grad + jnp.dot(part, spread, preferred_element_type=F32, precision=HIGH)
            row += slots
        wide = []
        for _ in range(2):
            rows = [known[n, row + i : row + i + 1, :] for i in range(n_pass // TILE)]
            wide.append(jnp.concatenate(rows, axis=1))
            row += n_pass // TILE
        placed = jnp.where(lax.div(place, lengths[first_batch + batch]) == slot, wide[0], 0.0).astype(BF16)
        matches = jnp.where(ids == wide[1], 1.0, 0.0).astype(BF16)
        part = row_sum(grad * dot_nt(placed, matches))
        return total + jnp.where(own[2:3, :] == batch.astype(F32), part, 0.0)

    query_grad[...] = lax.fori_loop(
        0, members, against, jnp.zeros((1, tokens), F32), unroll=min(members, 8)
    )


def backward_rows(
    with_out, first, term_grad, pre, out_grad, normed_two, inverse_two, slope, normed_one, inverse_one, low_one, expand, reduce,
    gains, biases, term_weight,
    reduce_turned, expanded_grad, low_turned, sum_one, branch_grad, sums, expand_shift,
    grad_here, two_here, slope_here, one_here, low_here, expand_here, reduce_here, grown, turned, low_side, sum_here, branch_here,
    sum_two, reduce_out_grad, sems, out_sems, begin=lambda: None, load=True,
):
    count, width = branch_grad.shape
    deep = slope.shape[1]
    wide = 2 * BLOCK
    blocks = deep // wide
    here = pl.ds(first, count)
    early = [
        fetch(
            [(normed_two.at[tile, :], two_here.at[tile, :])]
            + ([(out_grad.at[tile, :], grad_here.at[tile, :])] if with_out else []),
            sems,
            2 * i,
        )
        for i, tile in enumerate(tiles(count))
    ]
    base = 2 * (count // TILE)
    chunks = [
        fetch(
            [(slope.at[:, columns(j, wide)], slope_here.at[:, columns(j, wide)])]
            + ([(reduce.at[columns(j, wide), :], reduce_here.at[columns(j, wide), :])] if load else []),
            sems,
            base + 2 * j,
        )
        for j in range(blocks)
    ]
    base += 2 * blocks
    late = fetch(
        [(low_one.at[here, :], low_here), (normed_one.at[here, :], one_here)] + ([(expand, expand_here)] if load else []), sems, base
    )
    begin()
    if not with_out:
        spread = jnp.broadcast_to(term_grad[...], (TILE, count)).T
    totals = [jnp.zeros((1, width), F32) for _ in range(8)]
    for i, tile in enumerate(tiles(count)):
        grad_in = term_grad[tile, :] if with_out else spread[:, 0:1]
        pre_grad = grad_in * sigmoid(pre[tile, :])
        finish_all(early[i])
        unit = two_here[tile, :]
        second_grad = pre_grad * term_weight[...]
        if with_out:
            second_grad = second_grad + grad_here[tile, :].astype(F32)
        back = norm_backward(second_grad * gains[1:2, :], unit, inverse_two[tile, :])
        rounded = back.astype(BF16)
        sum_two[tile, :] = back
        reduce_out_grad[tile, :] = rounded
        totals[1] = totals[1] + row_sum(second_grad * unit)
        totals[3] = totals[3] + row_sum(rounded.astype(F32))
        totals[5] = totals[5] + row_sum(second_grad)
        totals[6] = totals[6] + row_sum(pre_grad * (unit * gains[1:2, :] + biases[5:6, :]))
        totals[7] = totals[7] + row_sum(jnp.broadcast_to(pre_grad, (TILE, width)))
    turned[...] = reduce_out_grad[...].T
    puts = fetch([(turned, reduce_turned)], out_sems)
    for j in range(blocks):
        cols = columns(j, wide)
        finish_all(chunks[j])
        grad = dot_nt(reduce_out_grad[...], reduce_here[cols, :]) * slope_here[:, cols].astype(F32)
        rounded = grad.astype(BF16)
        grown[:, cols] = rounded
        expand_shift[:, cols] = row_sum(rounded.astype(F32))
        puts += fetch([(grown.at[:, cols], expanded_grad.at[:, cols])], out_sems, 1 + j)
    late[0].wait()
    low_side[...] = low_here[...].T
    puts += fetch([(low_side, low_turned)], out_sems, 1 + blocks)
    finish_all(late[1:])
    sum_two[...] = sum_two[...] + dot_nt(grown[...], expand_here[...])
    for i, tile in enumerate(tiles(count)):
        first_grad = sum_two[tile, :]
        unit = one_here[tile, :]
        back = norm_backward(first_grad * gains[0:1, :], unit, inverse_one[first + tile.start : first + tile.stop, :])
        rounded = back.astype(BF16)
        sum_here[tile, :] = back
        branch_here[tile, :] = rounded
        puts += fetch(
            [(sum_here.at[tile, :], sum_one.at[tile, :]), (branch_here.at[tile, :], branch_grad.at[tile, :])], out_sems, 2 + blocks + 2 * i
        )
        totals[0] = totals[0] + row_sum(first_grad * unit)
        totals[2] = totals[2] + row_sum(rounded.astype(F32))
        totals[4] = totals[4] + row_sum(first_grad)
    for i, total in enumerate(totals):
        sums[i : i + 1, :] = total
    return puts


def backward_alone(with_out, first, *refs):
    finish_all(backward_rows(with_out, first, *refs))


def backward_layer(members, facts, lengths, known, score_grad, passage_ids, *refs):
    pre, normed_two, inverse_two, slope, hidden_pass, hidden_query = refs[13:19]
    pass_out, query_out, sent, scores = refs[19:26], refs[26:33], refs[33:36], refs[36]
    pass_own, query_own, (hid_p, hid_q, buffers, sems, out_sems, pass_term, query_term) = refs[37:53], refs[53:67], refs[67:]
    pass_in = (pass_term,) + refs[:13]
    expand_here, reduce_here, grown_p, turned_p, low_p = pass_own[5:10]
    grown_q, turned_q, low_q = query_own[5:8]
    query_in = (query_term, pre, pass_in[2], normed_two, inverse_two, slope) + pass_in[6:]
    copies = []

    def begin():
        copies.extend(fetch([(hidden_pass, hid_p), (hidden_query, hid_q)], sems))
        match(facts, lengths, known, score_grad, passage_ids, pass_in[1], scores, pass_term, query_term)

    puts = backward_rows(True, 0, *pass_in, *pass_out, *pass_own, begin=begin)
    puts += backward_rows(
        False, grown_p.shape[0], *query_in, *query_out, *query_own[:5], expand_here, reduce_here, *query_own[5:], load=False
    )
    finish_all(copies)
    core = 1 - facts[0]
    spread = grown_p.shape[1]
    width = low_p.shape[0]
    third = spread // 6
    half = pl.ds(pl.multiple_of(core * (width // 2), TILE), width // 2)
    for piece in range(3):

        def emit(leaf, side, row, part):
            buffers[piece, leaf, side, row : row + part.shape[0], :] = part

        def tell(rows, place):
            puts.extend(
                fetch([(buffers.at[piece, :, :, rows, :], sent[piece].at[:, :, rows, :])], out_sems, 2 * piece + place)
            )

        cols = pl.ds(pl.multiple_of(core * (spread // 2) + piece * third, TILE), third)
        inner_leaves(
            members, low_p, low_q, grown_p.at[:, cols], grown_q.at[:, cols], turned_p.at[half, :], turned_q.at[half, :],
            hid_p.at[piece], hid_q.at[piece], emit, tell,
        )
    finish_all(puts)


def attend_backward(mixed, attended_grad, stats, inner, mixed_grad, logit_grads, first, count, width, mask, tell):
    rows = slice(first, first + count)
    step = min(BLOCK, count)

    def pair(hp, carry):
        query = mixed[rows, columns(hp, 2 * HEAD)]
        grad = attended_grad[rows, columns(hp, 2 * HEAD)]
        query_grad = jnp.zeros((count, 2 * HEAD), F32)
        kept = []
        for sub in (0, 1):
            lanes = head_lanes(sub)
            total = stats[2 * hp + sub, :, rows]
            level = inner[2 * hp + sub, :, rows]
            for at in range(0, count, step):
                tile = slice(at, at + step)
                here = slice(first + at, first + at + step)
                key = mixed[here, columns(hp, 2 * HEAD, width)]
                value = mixed[here, columns(hp, 2 * HEAD, 2 * width)]
                key_here = jnp.where(lanes, key, jnp.zeros_like(key))
                value_here = jnp.where(lanes, value, jnp.zeros_like(value))
                weights = jnp.exp(dot_nt(key_here, query) + (mask[tile, :] - total))
                logit_grad = (weights * (dot_nt(value_here, grad) - level)).astype(BF16)
                logit_grads[sub, tile, 0:count] = logit_grad
                kept.append((dot(logit_grad, query), dot(weights.astype(BF16), grad)))
        for i, at in enumerate(range(0, count, step)):
            here = slice(first + at, first + at + step)
            for part in (0, 1):
                mixed_grad[here, columns(hp, 2 * HEAD, (part + 1) * width)] = jnp.where(
                    head_lanes(0), kept[i][part], kept[i + count // step][part]
                ).astype(BF16)
        for sub in (0, 1):
            key = mixed[rows, columns(hp, 2 * HEAD, width)]
            key_here = jnp.where(head_lanes(sub), key, jnp.zeros_like(key))
            query_grad = query_grad + dot_tn(logit_grads[sub, 0:count, 0:count], key_here)
        mixed_grad[rows, columns(hp, 2 * HEAD)] = (query_grad * SCALE).astype(BF16)
        tell(hp)
        return carry

    lax.fori_loop(0, HEADS // 2, pair, 0)


def backward_attention(
    members, sides, lengths, passages, queries, pass_grad, query_grad, project_out, mixed, attended, stats,
    attended_turned, project_in, pass_sum, query_sum, sums_pass, sums_query, shift_pass, shift_query,
    grad_out, turned_out, vectors, pass_out, query_out, *rest,
):
    sent = rest[0] if members else None
    (
        out_here, pass_here, query_here, mixed_here, attended_here, mixed_grad, turned,
        attended_grad, inner, logit_grads, mask, query_mask, across_here, in_here, pass_sum_here, query_sum_here, buffers,
        sems, out_sems,
    ) = rest[-19:]
    n_pass, width = passages.shape
    n_query = queries.shape[0]
    count = n_pass + n_query
    copies = fetch(
        [
            (project_out, out_here), (pass_grad, pass_here), (query_grad, query_here), (attended, attended_here),
            (mixed, mixed_here), (attended_turned, across_here), (project_in, in_here), (pass_sum, pass_sum_here),
            (query_sum, query_sum_here),
        ],
        sems,
    )
    query_mask[...] = same_slot(n_query, QLEN)
    mask[...] = same_slot(n_pass, lengths[sides[BATCH]])
    turned[:, 0:n_pass] = passages[...].T
    turned[:, n_pass:count] = queries[...].T
    puts = fetch([(turned, turned_out)], out_sems)
    finish_all(copies[:3])
    attended_grad[0:n_pass, :] = dot_nt(pass_here[...], out_here[...]).astype(BF16)
    attended_grad[n_pass:count, :] = dot_nt(query_here[...], out_here[...]).astype(BF16)
    heads = 16
    owner = lax.broadcasted_iota(jnp.int32, (heads, width), 1) // HEAD
    spread = jnp.where(owner == lax.broadcasted_iota(jnp.int32, (heads, width), 0), 1.0, 0.0)
    copies[3].wait()
    for tile in tiles(count):
        product = attended_grad[tile, :].astype(F32) * attended_here[tile, :].astype(F32)
        levels = dot_nt(spread, product, HIGH)
        for head in range(HEADS):
            inner[head, :, tile] = levels[head : head + 1, :]
    copies[4].wait()
    nothing = lambda hp: None
    attend_backward(mixed_here, attended_grad, stats, inner, mixed_grad, logit_grads, n_pass, n_query, width, query_mask, nothing)
    attend_backward(mixed_here, attended_grad, stats, inner, mixed_grad, logit_grads, 0, n_pass, width, mask, nothing)
    puts += fetch([(mixed_grad, grad_out)], out_sems, 1)
    shifts = [row_sum(mixed_grad[:, first : first + width].astype(F32)) for first in (0, 2 * width)]
    whole = jnp.concatenate([sums_pass[...] + sums_query[...], *shifts, jnp.zeros((6, width), F32)])
    deep_shift = shift_pass[...] + shift_query[...]
    if members:
        shard = width // members
        lane = lax.broadcasted_iota(jnp.int32, (width, TILE), 1)
        source = lax.broadcasted_iota(jnp.int32, (width, TILE), 0)
        row = lax.broadcasted_iota(jnp.int32, (16, TILE), 0)
        for leaf in range(members):
            chosen = jnp.where((source == lane + leaf * shard) & (lane < shard), 1.0, 0.0)
            block = jnp.dot(whole, chosen, preferred_element_type=F32, precision=HIGH)
            for i in range(3):
                part = deep_shift[:, (3 * leaf + i) * TILE : (3 * leaf + i + 1) * TILE]
                block = jnp.where(row == 10 + i, part, block)
            vectors[leaf] = block
        finish_all(copies[5:6])
        core = 1 - sides[0]
        wide = width // 2
        for piece in range(3):

            def emit(leaf, side, row, part):
                buffers[piece, leaf, side, row : row + part.shape[0], :] = part

            narrow = pl.ds(pl.multiple_of(core * wide + piece * TILE, TILE), TILE)
            outer_leaves(
                members, turned, mixed_grad.at[:, pl.ds(pl.multiple_of(core * 3 * wide + piece * wide, TILE), wide)],
                across_here, pass_here.at[:, narrow], query_here.at[:, narrow], emit,
            )
            vector_leaves(members, piece, core, vectors, buffers.shape[3] - 8, emit)
            puts += fetch([(buffers.at[piece], sent.at[piece])], out_sems, 2 + piece)
        late = copies[6:]
    else:
        vectors[0:16, :] = whole
        for i in range(deep_shift.shape[1] // width):
            vectors[16 + i : 17 + i, :] = deep_shift[:, i * width : (i + 1) * width]
        late = copies[5:]
    finish_all(late)
    for first in range(0, width, BLOCK):
        cols = slice(first, first + BLOCK)
        weight = in_here[cols, :]
        pass_out[:, cols] = (dot_nt(mixed_grad[0:n_pass, :], weight) + pass_sum_here[:, cols]).astype(BF16)
        query_out[:, cols] = (dot_nt(mixed_grad[n_pass:count, :], weight) + query_sum_here[:, cols]).astype(BF16)
    finish_all(puts)


def inner_leaves(members, low_p, low_q, grad_p, grad_q, turn_p, turn_q, hid_p, hid_q, emit, tell):
    width = low_p.shape[0]
    shard = width // members
    for first in range(0, width, width // 2):
        rows = slice(first, first + width // 2)
        part = dot(low_p[rows, :], grad_p[...]) + dot(low_q[rows, :], grad_q[...])
        for at in range(0, width // 2, shard // 2):
            leaf, side = divmod((first + at) // (shard // 2), 2)
            for block in range(part.shape[1] // TILE):
                emit(leaf, side, block * (shard // 2), part[at : at + shard // 2, block * TILE : (block + 1) * TILE])
    base = (shard // 2) * (grad_p.shape[1] // TILE)
    tell(slice(0, base), 0)
    for leaf in range(0, members, 4):
        span = slice(leaf * TILE, (leaf + 4) * TILE)
        part = dot(turn_p[...], hid_p[:, span]) + dot(turn_q[...], hid_q[:, span])
        for i in range(4):
            for side in (0, 1):
                emit(leaf + i, side, base, part[side * (width // 4) : (side + 1) * (width // 4), i * TILE : (i + 1) * TILE])
    tell(slice(base, base + width // 4), 1)


def outer_leaves(members, turned, grad, attended, branch_p, branch_q, emit):
    width = turned.shape[0]
    n_pass = branch_p.shape[0]
    shard = width // members
    for first in range(0, width, width // 2):
        rows = slice(first, first + width // 2)
        parts = [
            dot(turned[rows, :], grad[...]),
            dot(attended[rows, 0:n_pass], branch_p[...]) + dot(attended[rows, n_pass:], branch_q[...]),
        ]
        for at in range(0, width // 2, shard // 2):
            leaf, side = divmod((first + at) // (shard // 2), 2)
            block = 0
            for part in parts:
                for lane in range(0, part.shape[1], TILE):
                    emit(leaf, side, block * (shard // 2), part[at : at + shard // 2, lane : lane + TILE])
                    block += 1


def side_of(bit_at, mine, leaf, side):
    index = 2 * leaf + side
    high, bit, rest = index >> (bit_at + 1), (index >> bit_at) & 1, index & ((1 << bit_at) - 1)
    return jnp.where(mine == bit, 0, 1), (high << bit_at) + rest


def inner_kept(
    members, piece, bit_at, sides, low_pass, low_query, grad_pass, grad_query, reduce_pass, reduce_query, hidden_pass, hidden_query,
    received, leaves, stays,
    low_p, low_q, grad_p, grad_q, turn_p, turn_q, hid_p, hid_q, came, both, sems, out_sems,
):
    width = low_pass.shape[0]
    spread = grad_pass.shape[1]
    third = spread // 6
    cols = pl.ds(pl.multiple_of(sides[0] * (spread // 2) + piece * third, TILE), third)
    half = pl.ds(pl.multiple_of(sides[0] * (width // 2), TILE), width // 2)
    base = (width // members // 2) * (third // TILE)
    spans = [slice(0, base), slice(base, base + width // 4)]
    early = fetch(
        [
            (low_pass, low_p), (low_query, low_q), (grad_pass.at[:, cols], grad_p), (grad_query.at[:, cols], grad_q),
            (received.at[:, :, spans[0], :], came.at[:, :, spans[0], :]),
        ],
        sems,
    )
    late = fetch(
        [
            (reduce_pass.at[half, :], turn_p), (reduce_query.at[half, :], turn_q),
            (hidden_pass.at[piece], hid_p), (hidden_query.at[piece], hid_q),
            (received.at[:, :, spans[1], :], came.at[:, :, spans[1], :]),
        ],
        sems, 5,
    )
    puts = []

    def emit(leaf, side, row, part):
        rows = slice(row, row + part.shape[0])
        both[*side_of(bit_at, sides[1 + piece], leaf, side), rows, :] = part + came[leaf, side, rows, :]

    def tell(rows, place):
        pairs = [(both.at[1, :, rows, :], leaves.at[:, rows, :]), (both.at[0, :, rows, :], stays.at[:, rows, :])]
        puts.extend(fetch(pairs, out_sems, 2 * place))
        if place == 0:
            finish_all(late)

    finish_all(early)
    inner_leaves(members, low_p, low_q, grad_p, grad_q, turn_p, turn_q, hid_p, hid_q, emit, tell)
    finish_all(puts)


def outer_kept(
    members, places, sides, turned, mixed_grad, attended, branch_pass, branch_query, vectors, received, *refs
):
    leaves, stays = refs[0:6:2], refs[1:6:2]
    rows_here, grad, attended_here, branch_p, branch_q, came, both, sems, out_sems = refs[6:]
    width = turned.shape[0]
    wide = width // 2
    cols = pl.ds(pl.multiple_of(sides[0] * 3 * wide, TILE), 3 * wide)
    narrow = pl.ds(pl.multiple_of(sides[0] * wide, TILE), wide)
    copies = fetch(
        [
            (turned, rows_here), (mixed_grad.at[:, cols], grad), (attended, attended_here),
            (branch_pass.at[:, narrow], branch_p), (branch_query.at[:, narrow], branch_q),
        ]
        + [(received.at[piece], came.at[piece]) for piece in range(3)],
        sems,
    )
    finish_all(copies[:5])
    puts = []
    for piece in range(3):
        copies[5 + piece].wait()

        def emit(leaf, side, row, part):
            rows = slice(row, row + part.shape[0])
            both[piece, *side_of(places[piece], sides[1 + piece], leaf, side), rows, :] = part + came[piece, leaf, side, rows, :]

        outer_leaves(
            members, rows_here, grad.at[:, piece * wide : (piece + 1) * wide], attended_here,
            branch_p.at[:, piece * TILE : (piece + 1) * TILE], branch_q.at[:, piece * TILE : (piece + 1) * TILE], emit,
        )
        vector_leaves(members, piece, sides[0], vectors, both.shape[3] - 8, emit)
        puts += fetch([(both.at[piece, 1], leaves[piece]), (both.at[piece, 0], stays[piece])], out_sems, 2 * piece)
    finish_all(puts)


def vector_leaves(members, piece, core, vectors, row, emit):
    for leaf in range(members):
        for side in (0, 1):
            if piece == 0:
                part = jnp.where(core == 0, vectors[leaf, 8 * side : 8 * side + 8, :], 0.0)
            else:
                part = jnp.zeros((8, TILE), F32)
            emit(leaf, side, row, part)


def finish_inner(sides, mine, near, other, beyond, expand, reduce):
    rows, wide = expand.shape
    half = rows // 2
    blocks = wide // 6 // TILE
    deep = reduce.shape[1] // 2
    for far, pair in enumerate(((mine, near), (other, beyond))):
        core = jnp.bitwise_xor(sides[0], far)
        for piece in range(3):
            for there, source in enumerate(pair):
                side = pl.multiple_of(jnp.bitwise_xor(sides[1], there) * half, 8)
                for block in range(blocks):
                    at = core * (wide // 2) + (piece * blocks + block) * TILE
                    expand[pl.ds(side, half), pl.ds(pl.multiple_of(at, TILE), TILE)] = source[
                        piece, block * half : (block + 1) * half, :
                    ]
            parts = [source[piece, blocks * half :, :] for source in pair]
            low = jnp.where(sides[1] == 0, parts[0], parts[1])
            high = jnp.where(sides[1] == 0, parts[1], parts[0])
            reduce[piece * TILE : (piece + 1) * TILE, pl.ds(pl.multiple_of(core * deep, TILE), deep)] = (
                jnp.concatenate([low, high]).T
            )


def finish_outer(sides, mine, near, other, beyond, project_in, project_out, gains, biases, term_weight, term_bias, expand_bias):
    rows, wide = project_in.shape
    half = rows // 2
    for far, pair in enumerate(((mine, near), (other, beyond))):
        core = jnp.bitwise_xor(sides[0], far)
        for there, source in enumerate(pair):
            side = pl.multiple_of(jnp.bitwise_xor(sides[1], there) * half, 8)
            for piece in range(3):
                for block in range(4):
                    part = source[piece, block * half : (block + 1) * half, :]
                    if block < 3:
                        at = core * (wide // 2) + (piece * 3 + block) * TILE
                        project_in[pl.ds(side, half), pl.ds(pl.multiple_of(at, TILE), TILE)] = part
                    else:
                        at = core * (wide // 6) + piece * TILE
                        project_out[pl.ds(side, half), pl.ds(pl.multiple_of(at, TILE), TILE)] = part
    at = mine.shape[1] - 8
    parts = [
        jnp.where(sides[0] == 0, a[0, at:, :], b[0, at:, :]) for a, b in ((mine, other), (near, beyond))
    ]
    low = jnp.where(sides[1] == 0, parts[0], parts[1])
    high = jnp.where(sides[1] == 0, parts[1], parts[0])
    gains[...] = low[0:2, :rows]
    biases[0:2, :] = high[0:2, :rows]
    biases[2:6, :] = low[2:6, :rows]
    term_weight[...] = low[6:7, :rows]
    term_bias[...] = low[7:8, 0:1]
    for i in range(expand_bias.shape[1] // TILE):
        expand_bias[:, i * TILE : (i + 1) * TILE] = high[2 + i : 3 + i, :]


def run(kernel, outs, kinds, scratch, args, after=(), aliases=None, limit=58):
    specs = {"s": IN_SMEM, "v": IN_VMEM, "h": IN_PLACE, "a": IN_PLACE}
    shapes = [
        pltpu.HBM(dims, dtype) if kind == "h" else jax.ShapeDtypeStruct(dims, dtype) for kind, dims, dtype in outs
    ]
    given = [
        pltpu.with_memory_space_constraint(a, pltpu.HBM) if kind == "h" else a for a, kind in zip(args, kinds)
    ]
    many = len(outs) > 1
    known = len(args)

    def body(*refs):
        kernel(*refs[:known], *refs[known + len(after) :])

    return pl.pallas_call(
        body,
        out_shape=shapes if many else shapes[0],
        in_specs=[specs[kind] for kind in kinds] + [IN_PLACE] * len(after),
        out_specs=[specs[o[0]] for o in outs] if many else specs[outs[0][0]],
        scratch_shapes=scratch,
        input_output_aliases=aliases or {},
        compiler_params=pltpu.CompilerParams(vmem_limit_bytes=limit << 20),

    )(*given, *after)


def contract_rows(left, right):
    return lax.dot_general(
        left, right, (((0,), (0,)), ((), ())), preferred_element_type=F32
    )


GROUP_FIRST = (("pb", 2), ("pa", 1))
ROW_FIRST = (("pa", 1), ("pb", 2))


def swap(value, axis, distance):
    return lax.ppermute(
        value, axis, [(i, i ^ distance) for i in range(lax.axis_size(axis))]
    )


def bit(axis, distance):
    return (lax.axis_index(axis) >> (distance.bit_length() - 1)) & 1


def pick(value, index, dim):
    return lax.dynamic_index_in_dim(value, index, dim, keepdims=False)


def group_gather(mine):
    distance = 1
    while distance < lax.axis_size("pa"):
        other = swap(mine, "pa", distance)
        mine = jnp.where(
            bit("pa", distance) == 0, jnp.concatenate([mine, other]), jnp.concatenate([other, mine])
        )
        distance *= 2
    return mine


def steps_of(order):
    steps = [(axis, distance) for axis, distance in order]
    distance = 2
    while distance < lax.axis_size("pa"):
        steps.append(("pa", distance))
        distance *= 2
    return steps


def tree_sum(send, keep, order):
    names = []
    distance = lax.axis_size("pa") // 2
    while distance:
        names.append(("pa", distance))
        distance //= 2
    names.append(("pb", 2))
    received = swap(send, "pb", 1)
    for axis, distance in steps_of(order):
        dim = names.index((axis, distance))
        names.pop(dim)
        mine = bit(axis, distance)
        send = pick(keep, 1 - mine, dim) + pick(received, 1 - mine, dim)
        keep = pick(keep, mine, dim) + pick(received, mine, dim)
        received = swap(send, axis, distance)
    mine = keep + received
    other = swap(mine, "pb", 2)
    high = bit("pb", 2)
    return jnp.where(high == 0, jnp.stack([mine, other]), jnp.stack([other, mine]))


def cut(matrix):
    bits = lax.axis_size("pa").bit_length() - 1
    rows = matrix.shape[0] >> (bits + 1)
    return matrix.reshape((2,) * (bits + 1) + (rows, matrix.shape[1]))


def summed_rows(left, right, order):
    core = bit("pb", 1)
    half = right.shape[1] // 2
    parts = [
        cut(contract_rows(left, lax.dynamic_slice_in_dim(right, side * half, half, axis=1)))
        for side in (1 - core, core)
    ]
    mine = tree_sum(parts[0], parts[1], order)
    mine = mine.reshape(-1, half)
    other = swap(mine, "pb", 1)
    return jnp.where(
        core == 0, jnp.concatenate([mine, other], 1), jnp.concatenate([other, mine], 1)
    )


def total_of_all(value):
    distance = 1
    while distance < lax.axis_size("pb"):
        value = value + swap(value, "pb", distance)
        distance *= 2
    distance = 1
    while distance < lax.axis_size("pa"):
        value = value + swap(value, "pa", distance)
        distance *= 2
    return value


BATCH_IN_GROUP, BATCH, MEMBER = 5, 6, 7
LEAF_BITS = (("pa", 4), ("pa", 2), ("pa", 1), ("pb", 2))
PIECE_ORDERS = (
    (("pb", 2), ("pa", 1), ("pa", 2), ("pa", 4)),
    (("pa", 1), ("pa", 2), ("pb", 2), ("pa", 4)),
    (("pa", 2), ("pb", 2), ("pa", 1), ("pa", 4)),
)
PLACES = tuple(len(LEAF_BITS) - 1 - LEAF_BITS.index(order[0]) for order in PIECE_ORDERS)


def begun(parts):
    held = []
    for (leaving, staying), order in zip(parts, PIECE_ORDERS):
        rest = tuple(b for b in LEAF_BITS if b != order[0])
        held.append(([(staying, rest), (swap(leaving, *order[0]), rest)], (order[0],)))
    return held


def chosen(names, settled, current=None):
    return tuple(1 if name == current else 0 if name in settled else None for name in names)


def part_of(array, names, settled, current, rows):
    wants = chosen(names, settled, current)
    starts = [0 if want is None else bit(*name) ^ want for name, want in zip(names, wants)]
    sizes = [2 if want is None else 1 for want in wants]
    part = lax.dynamic_slice(array.reshape((2,) * len(names) + (rows, TILE)), starts + [0, 0], sizes + [rows, TILE])
    return part.reshape((2,) * wants.count(None) + (rows, TILE))


def onward(held, step, sent):
    moved = []
    for (terms, settled), order, leaving in zip(held, PIECE_ORDERS, sent):
        left = tuple(b for b in LEAF_BITS if b not in settled and b != order[step])
        moved.append((terms + [(swap(leaving, *order[step]), left)], settled + (order[step],)))
    return moved


def advance(held, step, rows):
    sent = []
    for (terms, settled), order in zip(held, PIECE_ORDERS):
        sent.append(sum(part_of(array, names, settled, order[step], rows) for array, names in terms))
    return onward(held, step, sent)


def fold(plans, through, joined, facts, *refs):
    count = sum(len(plan) for plan in plans)
    terms = refs[:count]
    outs = refs[count + through : count + through + (1 if joined else len(plans))]
    scratch = refs[count + through + len(outs) + through :]
    sems, out_sems = scratch[-2:]
    pairs = []
    at = 0
    for plan in plans:
        for wants in plan:
            index = tuple(
                slice(None) if want is None else jnp.bitwise_xor(facts[len(LEAF_BITS) - LEAF_BITS.index(name)], want) for name, want in wants
            )
            pairs.append((terms[at].at[index], scratch[at]))
            at += 1
    copies = fetch(pairs, sems)
    puts = []
    at = 0
    for i, plan in enumerate(plans):
        finish_all(copies[at : at + len(plan)])
        total = scratch[at][...]
        for k in range(1, len(plan)):
            total = total + scratch[at + k][...]
        scratch[at][...] = total
        puts += fetch([(scratch[at], outs[0].at[i] if joined else outs[i])], out_sems, i)
        at += len(plan)
    finish_all(puts)


def fold_by_kernel(facts, held, step, rows, through=(), after=(), joined=False):
    plans = []
    args = []
    scratch = []
    outs = []
    for (terms, settled), order in zip(held, PIECE_ORDERS):
        plan = []
        for array, names in terms:
            wants = chosen(names, settled, order[step])
            plan.append(tuple(zip(names, wants)))
            args.append(array.reshape((2,) * len(names) + (rows, TILE)))
            dims = (2,) * wants.count(None) + (rows, TILE)
            scratch.append(pltpu.VMEM(dims, F32))
        plans.append(plan)
        outs.append(("h", dims, F32))
    if joined:
        outs = [("h", (len(plans), rows, TILE), F32)]
    done = run(
        partial(fold, plans, len(through), joined),
        outs + [("h", a.shape, a.dtype) for a in through],
        "s" + "a" * len(args) + "h" * len(through),
        scratch + [pltpu.SemaphoreType.DMA((len(args),)), pltpu.SemaphoreType.DMA((len(plans),))],
        (facts, *args, *through),
        after,
        {1 + len(args) + i: len(outs) + i for i in range(len(through))},
        12,
    )
    return done if len(outs) + len(through) > 1 else [done]


def advance_by_kernel(facts, held, step, rows, through=(), after=()):
    done = fold_by_kernel(facts, held, step, rows, through, after)
    return onward(held, step, done[:3]), done[3:]


def last_exchange(facts, held, rows, through=()):
    step = len(LEAF_BITS) - 1
    name = PIECE_ORDERS[0][step]
    sent, *through = fold_by_kernel(facts, held, step, rows, through, joined=True)
    came = swap(sent, *name)
    total = jnp.stack(
        [sum(part_of(array, names, settled + (name,), None, rows) for array, names in terms) for terms, settled in held]
    )
    return total + came, through


def on_device(
    passages, queries, passage_ids, query_ids, batch_length, query_batch, project_in, project_out, expand_weight,
    expand_bias, reduce_weight, norm_gains, biases, term_weight, term_bias, out_grad, score_grad,
):
    members = lax.axis_size("pa")
    member_index = lax.axis_index("pa")
    local_batch = member_index // (members // BATCH_PB)
    facts = jnp.stack(
        [
            bit("pb", 1), *(bit(*name) for name in reversed(LEAF_BITS)), local_batch,
            lax.axis_index("pb") * BATCH_PB + local_batch, member_index,
        ]
    )
    n_pass, width = passages.shape
    n_query = queries.shape[0]
    count = n_pass + n_query
    deep = expand_weight.shape[1]
    slots = score_grad.shape[1]
    bias_row = expand_bias[None]
    term_row = term_weight[None]

    blocks = deep // (2 * BLOCK)
    by_three = (3, n_pass, deep // 3)
    weights = [pltpu.VMEM(expand_weight.shape, BF16), pltpu.VMEM(reduce_weight.shape, BF16)]

    def vmem(*dims, dtype=BF16):
        return pltpu.VMEM(dims, dtype)

    def sems(number):
        return pltpu.SemaphoreType.DMA((number,))

    known_rows = 3 + slots * (-(-score_grad.shape[0] // TILE)) + 2 * (n_pass // TILE)
    (
        mixed, attended, attended_turned, stats, normed_one, inverse_one, low,
        hidden_query, slope_query, unit_query, scale_query, pre_query,
        hidden, slope, unit_pass, scale_pass, pre_pass, passage_out, known,
    ) = run(
        forward_layer,
        [
            ("h", (count, 3 * width), BF16), ("h", (count, width), BF16),
            ("h", (width, count), BF16), ("v", (HEADS, 1, count), F32), ("h", (count, width), F32),
            ("v", (count, 1), F32), ("h", (count, width), BF16), ("h", (3, n_query, deep // 3), BF16),
            ("h", (n_query, deep), BF16), ("v", (n_query, width), F32), ("v", (n_query, 1), F32), ("v", (n_query, 1), F32),
            ("h", by_three, BF16), ("h", (n_pass, deep), BF16), ("h", (n_pass, width), F32),
            ("v", (n_pass, 1), F32), ("v", (n_pass, 1), F32), ("h", (n_pass, width), BF16),
            ("v", (1, known_rows, TILE), F32),
        ],
        "ssvvhhhhvvvvsvsvv",
        [
            vmem(*project_in.shape), vmem(*project_out.shape), *weights, vmem(count, 3 * width), vmem(count, width),
            vmem(width, count), vmem(count, width, dtype=F32), vmem(count, width), vmem(n_query, deep), vmem(n_query, deep),
            vmem(n_pass, deep), vmem(n_pass, deep), vmem(n_pass, width, dtype=F32), vmem(n_pass, width),
            vmem(n_pass, n_pass, dtype=F32), vmem(n_query, n_query, dtype=F32), vmem(count, width, dtype=F32),
            sems(6), sems(5 + 2 * blocks + 2 * (deep // TILE) + 2 * (n_pass // TILE)),
        ],
        (facts, batch_length, passages, queries, project_in, project_out, expand_weight, reduce_weight, bias_row, norm_gains,
         biases, term_row, term_bias, query_ids[None], query_batch, score_grad.T, passage_ids[None]),
    )
    known = group_gather(known)
    def back_outs(rows):
        return [
            ("h", (width, rows), BF16), ("h", (rows, deep), BF16), ("h", (width, rows), BF16),
            ("h", (rows, width), F32), ("h", (rows, width), BF16), ("v", (8, width), F32), ("v", (1, deep), F32),
        ]

    back_kinds = "vvhhvhhvhhhvvv"

    def back_scratch(rows):
        return [
            vmem(rows, width), vmem(rows, width, dtype=F32), vmem(rows, deep), vmem(rows, width, dtype=F32), vmem(rows, width),
            *weights, vmem(rows, deep), vmem(width, rows), vmem(width, rows), vmem(rows, width, dtype=F32), vmem(rows, width),
            vmem(rows, width, dtype=F32), vmem(rows, width),
            sems(3 + 2 * blocks + 2 * (rows // TILE)), sems(2 + blocks + 2 * (rows // TILE)),
        ]

    def back_args(term_grad, pre, unit, scale, slope_here):
        return (term_grad, pre, out_grad, unit, scale, slope_here, normed_one, inverse_one, low,
                expand_weight, reduce_weight, norm_gains, biases, term_row)

    fits = deep // members == 3 * TILE
    shard = width // members
    leaf_rows = (deep // 6 // TILE * (shard // 2) + width // 4, 4 * (shard // 2) + 8)
    if fits:
        dims = (members, 2, leaf_rows[0], TILE)
        third = deep // 6
        pass_scratch, query_scratch = back_scratch(n_pass), back_scratch(n_query)
        (
            rg_pass, eg_pass, low_pass, one_pass, bg_pass, sums_pass, shift_pass,
            rg_query, eg_query, low_query, one_query, bg_query, sums_query, shift_query, *sent, scores
        ) = run(
            partial(backward_layer, members),
            back_outs(n_pass) + back_outs(n_query) + [("h", dims, F32)] * 3 + [("v", score_grad.shape[::-1], F32)],
            "ssvvv" + back_kinds[1:] + "vhvhhh",
            pass_scratch + query_scratch[:5] + query_scratch[7:]
            + [vmem(*by_three), vmem(3, n_query, deep // 3), vmem(3, *dims, dtype=F32), sems(2), sems(6), vmem(n_pass, 1, dtype=F32),
               vmem(1, n_query, dtype=F32)],
            (facts, batch_length, known, score_grad.T, passage_ids[None])
            + back_args(None, pre_pass, unit_pass, scale_pass, slope)[1:]
            + (pre_query, unit_query, scale_query, slope_query, hidden, hidden_query),
        )
        came = [swap(part, "pb", 1) for part in sent]
        parts = []
        for piece, order in enumerate(PIECE_ORDERS):
            half = (leaf_rows[0], TILE)
            parts.append(
                run(
                    partial(inner_kept, members, piece, PLACES[piece]),
                    [("h", (members,) + half, F32)] * 2,
                    "s" + "h" * 8 + "a",
                    [
                        vmem(width, n_pass), vmem(width, n_query), vmem(n_pass, third), vmem(n_query, third),
                        vmem(width // 2, n_pass), vmem(width // 2, n_query), vmem(n_pass, deep // 3), vmem(n_query, deep // 3),
                        vmem(*dims, dtype=F32), vmem(2, members, *half, dtype=F32), sems(10), sems(4),
                    ],
                    (facts, low_pass, low_query, eg_pass, eg_query, rg_pass, rg_query, hidden,
                     hidden_query, came[piece]),
                    limit=18,
                )
            )
        inner = begun(parts)
        pins = tuple(leaving for leaving, _ in parts)
        extra = [("v", (members, 16, TILE), F32)]
        last = [("h", (3, members, 2, leaf_rows[1], TILE), F32)]
    else:
        scores, pass_term_grad, query_term_grad = run(
            match,
            [("v", score_grad.shape[::-1], F32), ("v", (n_pass, 1), F32), ("v", (1, n_query), F32)],
            "ssvvvv",
            [],
            (facts, batch_length, known, score_grad.T, passage_ids[None], pre_pass),
        )
        rg_pass, eg_pass, low_pass, one_pass, bg_pass, sums_pass, shift_pass = run(
            partial(backward_alone, True, 0), back_outs(n_pass), back_kinds, back_scratch(n_pass),
            back_args(pass_term_grad, pre_pass, unit_pass, scale_pass, slope),
        )
        rg_query, eg_query, low_query, one_query, bg_query, sums_query, shift_query = run(
            partial(backward_alone, False, n_pass), back_outs(n_query), back_kinds, back_scratch(n_query),
            back_args(query_term_grad, pre_query, unit_query, scale_query, slope_query),
        )
        pins = ()
        extra = [("v", (16 + deep // width, width), F32)]
        last = []
    mixed_grad, turned, vectors, passage_grad, query_grad, *sent = run(
        partial(backward_attention, members if fits else 0),
        [("h", (count, 3 * width), BF16), ("h", (width, count), BF16)]
        + extra
        + [("v", (n_pass, width), BF16), ("v", (n_query, width), BF16)]
        + last,
        "ssvvhhhhhv" + "hhhh" + "vvvv",
        [
            vmem(*project_out.shape), vmem(n_pass, width), vmem(n_query, width), vmem(count, 3 * width), vmem(count, width),
            vmem(count, 3 * width), vmem(width, count), vmem(count, width), vmem(HEADS, 1, count, dtype=F32),
            vmem(2, n_pass, n_pass), vmem(n_pass, n_pass, dtype=F32), vmem(n_query, n_query, dtype=F32),
            vmem(width, count), vmem(*project_in.shape), vmem(n_pass, width, dtype=F32), vmem(n_query, width, dtype=F32),
            vmem(*(last[0][1] if fits else (8, TILE)), dtype=F32), sems(9), sems(5),
        ],
        (facts, batch_length, passages, queries, bg_pass, bg_query, project_out, mixed, attended, stats, attended_turned, project_in,
         one_pass, one_query, sums_pass, sums_query, shift_pass, shift_query),
        pins,
    )
    if fits:
        inner, sent = advance_by_kernel(facts, inner, 1, leaf_rows[0], tuple(sent))
        half = (leaf_rows[1], TILE)
        dims = (3, members, 2) + half
        parts = run(
            partial(outer_kept, members, PLACES),
            [("h", (members,) + half, F32)] * 6,
            "s" + "h" * 5 + "va",
            [
                vmem(width, count), vmem(count, 3 * width // 2), vmem(width, count), vmem(n_pass, width // 2),
                vmem(n_query, width // 2), vmem(*dims, dtype=F32), vmem(3, 2, members, *half, dtype=F32), sems(8), sems(6),
            ],
            (facts, turned, mixed_grad, attended_turned, bg_pass, bg_query, vectors, swap(sent[0], "pb", 1)),
            limit=24,
        )
        inner, _ = advance_by_kernel(facts, inner, 2, leaf_rows[0], after=tuple(parts[0:6:2]))
        inner_mine, late = last_exchange(facts, inner, leaf_rows[0], (parts[2],))
        outer = begun([parts[0:2], (late[0], parts[3]), parts[4:6]])
        for step in (1, 2):
            outer = advance(outer, step, leaf_rows[1])
        outer_mine, _ = last_exchange(facts, outer, leaf_rows[1])

        def finish(kernel, mine, outs):
            near = swap(mine, "pb", 2)
            args = (facts, mine, near, swap(mine, "pb", 1), swap(near, "pb", 1))
            return run(kernel, outs, "svvvv", [], args, limit=12)

        expand_total, reduce_total = finish(
            finish_inner, inner_mine, [("v", (shard, deep), F32), ("v", (deep // members, width), F32)]
        )
        in_total, out_total, gains_grad, biases_grad, term_grad, bias_grad, expand_shift = finish(
            finish_outer, outer_mine,
            [
                ("v", (shard, 3 * width), F32), ("v", (shard, width), F32), ("v", (2, shard), F32), ("v", (6, shard), F32),
                ("v", (1, shard), F32), ("v", (1, 1), F32), ("v", (1, deep // members), F32),
            ],
        )
    else:
        in_order = [h.reshape(3, h.shape[1], -1, TILE).transpose(1, 2, 0, 3).reshape(-1, deep) for h in (hidden, hidden_query)]
        whole = [jnp.concatenate(pair, axis) for pair, axis in (
            (in_order, 0), ((rg_pass, rg_query), 1), ((eg_pass, eg_query), 0), ((bg_pass, bg_query), 0),
        )]
        reduce_total = summed_rows(whole[0], whole[1].T, ROW_FIRST)
        expand_total = summed_rows(low, whole[2], GROUP_FIRST)
        out_total = summed_rows(attended, whole[3], GROUP_FIRST)
        in_total = summed_rows(turned.T, mixed_grad, ROW_FIRST)
        vectors = total_of_all(vectors)
        mine = lax.dynamic_slice_in_dim(vectors[:10], member_index * shard, shard, axis=1)
        expand_shift = lax.dynamic_slice_in_dim(
            vectors[16:].reshape(-1), member_index * (deep // members), deep // members
        )
        gains_grad = mine[:2]
        biases_grad = jnp.concatenate([mine[8:10], mine[2:6]])
        term_grad = mine[6]
        bias_grad = mine[7, :1]
    return (
        scores.T,
        passage_out,
        passage_grad,
        query_grad,
        in_total,
        out_total,
        expand_total,
        expand_shift.reshape(-1),
        reduce_total,
        gains_grad,
        biases_grad,
        term_grad.reshape(-1),
        bias_grad.reshape(-1),
    )


def solution(mesh):
    return jax.shard_map(
        on_device,
        mesh=mesh,
        in_specs=(
            P(("pb", "pa"), None),
            P(("pb", "pa"), None),
            P(("pb", "pa")),
            P(("pb", "pa")),
            P(),
            P(("pb", "pa")),
            P(),
            P(),
            P(),
            P(),
            P(),
            P(),
            P(),
            P(),
            P(),
            P(("pb", "pa"), None),
            P("pb", "pa"),
        ),
        out_specs=(
            P("pb", "pa"),
            P(("pb", "pa"), None),
            P(("pb", "pa"), None),
            P(("pb", "pa"), None),
            P("pa", None),
            P("pa", None),
            P("pa", None),
            P("pa"),
            P("pa", None),
            P(None, "pa"),
            P(None, "pa"),
            P("pa"),
            P(),
        ),
        check_vma=False,
    )
```

```python
from functools import partial

import jax
import jax.numpy as jnp
from jax import lax
from jax.experimental import pallas as pl
from jax.experimental.pallas import tpu as pltpu
from jax.sharding import PartitionSpec as P

HEADS = 12
HEAD = 64
LONG = 512
QLEN = 32
BATCH_PB = 4

NEG = -1e30
HIGH = lax.Precision.HIGHEST
LN_EPS = 1e-12
SCALE = HEAD ** (-0.5)
BLOCK = 256
TILE = 128
F32 = jnp.float32
BF16 = jnp.bfloat16

IN_VMEM = pl.BlockSpec(memory_space=pltpu.VMEM)
IN_SMEM = pl.BlockSpec(memory_space=pltpu.SMEM)
IN_PLACE = pl.BlockSpec(memory_space=pl.ANY)


def shape(dims, dtype):
    return (tuple(dims), dtype)


def dot(left, right):
    return jnp.dot(left, right, preferred_element_type=F32)


def dot_nt(left, right, precision=None):
    return lax.dot_general(
        left, right, (((1,), (1,)), ((), ())), preferred_element_type=F32, precision=precision
    )


def dot_tn(left, right):
    return lax.dot_general(left, right, (((0,), (0,)), ((), ())), preferred_element_type=F32)


def columns(index, width, first=0):
    return pl.ds(pl.multiple_of(first + index * width, TILE), width)


def tiles(count):
    return [slice(first, first + TILE) for first in range(0, count, TILE)]


def row_sum(matrix):
    return jnp.sum(matrix, axis=0, keepdims=True)


def fetch(pairs, sems, first=0):
    copies = [
        pltpu.make_async_copy(source, target, sems.at[first + i]) for i, (source, target) in enumerate(pairs)
    ]
    for copy in copies:
        copy.start()
    return copies


def finish_all(copies):
    for copy in copies:
        copy.wait()


def norm_forward(total):
    centred = total - jnp.mean(total, axis=-1, keepdims=True)
    inverse = lax.rsqrt(jnp.mean(centred * centred, axis=-1, keepdims=True) + LN_EPS)
    return centred * inverse, inverse


def norm_backward(scaled, normed, inverse):
    centred = scaled - jnp.mean(scaled, axis=-1, keepdims=True)
    return inverse * (centred - normed * jnp.mean(scaled * normed, axis=-1, keepdims=True))


def head_lanes(sub):
    lane = lax.broadcasted_iota(jnp.int32, (1, 2 * HEAD), 1)
    return (lane // HEAD) == sub


def same_slot(count, length):
    rows = lax.broadcasted_iota(jnp.int32, (count, count), 0) // length
    cols = lax.broadcasted_iota(jnp.int32, (count, count), 1) // length
    return jnp.where(rows == cols, 0.0, NEG)


def attend(mixed, turned, stats, first, count, width, mask, unroll):
    rows = slice(first, first + count)

    def pair(hp, carry):
        key = mixed[rows, columns(hp, 2 * HEAD, width)]
        value = mixed[rows, columns(hp, 2 * HEAD, 2 * width)].T
        for sub in (0, 1):
            key_here = jnp.where(head_lanes(sub), key, jnp.zeros_like(key))
            logits = dot_nt(key_here, mixed[rows, columns(hp, 2 * HEAD)]) + mask[...]
            highest = jnp.max(logits, axis=0, keepdims=True)
            powers = jnp.exp(logits - highest)
            total = jnp.sum(powers, axis=0, keepdims=True)
            weights = (powers * (1.0 / total)).astype(BF16)
            out_rows = pl.ds(pl.multiple_of((2 * hp + sub) * HEAD, HEAD), HEAD)
            turned[out_rows, rows] = dot(value[sub * HEAD : (sub + 1) * HEAD], weights).astype(BF16)
            stats[2 * hp + sub, :, rows] = highest + jnp.log(total)
        return carry

    lax.fori_loop(0, HEADS // 2, pair, 0, unroll=unroll)


def grow(rows, first, count, expand, cols, expand_bias, hidden, slope):
    for at in range(0, count, min(BLOCK, count)):
        tile = slice(at, at + min(BLOCK, count))
        value = dot(rows[first + at : first + tile.stop, :], expand[:, cols]) + expand_bias[:, cols]
        lower = 0.5 + 0.5 * lax.erf(value * (0.5**0.5))
        hidden[tile, cols] = (value * lower).astype(BF16)
        density = jnp.exp(-0.5 * value * value) * 0.3989422804014327
        slope[tile, cols] = (lower + value * density).astype(BF16)


def by_piece(block, hidden, out):
    shard, piece = lax.div(block, 3), lax.rem(block, 3)
    return hidden.at[:, columns(block, TILE)], out.at[piece, :, columns(shard, TILE)]


def close_forward(total, normed_one, first, count, at, gains, biases, term_weight, term_bias, normed, inverse, pre, passage_out, tell):
    for i, tile in enumerate(tiles(count)):
        base = normed_one[first + tile.start : first + tile.stop, :] * gains[0:1, :] + biases[4:5, :]
        unit, scale = norm_forward(base + total[at + tile.start : at + tile.stop, :] + biases[3:4, :])
        normed[tile, :] = unit
        inverse[tile, :] = scale
        second = unit * gains[1:2, :] + biases[5:6, :]
        pre[tile, :] = jnp.sum(second * term_weight[...], axis=-1, keepdims=True) + term_bias[0]
        if passage_out is not None:
            passage_out[tile, :] = second.astype(BF16)
        tell(i, tile)


def softplus(value):
    return jnp.maximum(value, 0.0) + jnp.log1p(jnp.exp(-jnp.abs(value)))


def sigmoid(value):
    return 1.0 / (1.0 + jnp.exp(-value))


def forward_layer(
    facts, lengths, passages, queries, project_in, project_out, expand, reduce, expand_bias, gains, biases,
    term_weight, term_bias, query_ids, query_batch, score_grad, passage_ids,
    mixed_out, attended_out, turned_out, stats, normed_out, inverse_one, low_out,
    hidden_query_out, slope_query_out, unit_query, scale_query, pre_query,
    hidden_out, slope_out, unit_out, scale_pass, pre_pass, passage_out, known,
    in_here, out_here, expand_here, reduce_here, mixed, attended, turned, normed_one, low, hidden_query, slope_query,
    hidden, slope, unit_pass, second, mask, query_mask, total, sems, out_sems,
):
    n_pass, width = passages.shape
    n_query = queries.shape[0]
    count = n_pass + n_query
    parts = [slice(i * width, (i + 1) * width) for i in range(3)]
    copies = fetch(
        [(project_in.at[:, part], in_here.at[:, part]) for part in parts]
        + [(project_out, out_here), (expand, expand_here), (reduce, reduce_here)],
        sems,
    )
    mask[...] = same_slot(n_pass, lengths[facts[BATCH]])
    query_mask[...] = same_slot(n_query, QLEN)
    for part in range(3):
        copies[part].wait()
        for source, first, rows in ((passages, 0, n_pass), (queries, n_pass, n_query)):
            value = dot(source[...], in_here[:, parts[part]])
            if part != 1:
                value = value + biases[part // 2 : part // 2 + 1, :]
            if part == 0:
                value = value * SCALE
            mixed[first : first + rows, parts[part]] = value.astype(BF16)
    puts = fetch([(mixed, mixed_out)], out_sems)
    attend(mixed, turned, stats, n_pass, n_query, width, query_mask, HEADS // 2)
    attend(mixed, turned, stats, 0, n_pass, width, mask, 3)
    attended[...] = turned[...].T
    puts += fetch([(turned, turned_out), (attended, attended_out)], out_sems, 1)
    copies[3].wait()
    total[...] = dot(attended[...], out_here[...])
    for tile in reversed(tiles(count)):
        source, at = (passages, tile.start) if tile.start < n_pass else (queries, tile.start - n_pass)
        unit, scale = norm_forward(source[at : at + TILE, :].astype(F32) + total[tile, :] + biases[2:3, :])
        normed_one[tile, :] = unit
        inverse_one[tile, :] = scale
        low[tile, :] = (unit * gains[0:1, :] + biases[4:5, :]).astype(BF16)
    puts += fetch([(normed_one, normed_out), (low, low_out)], out_sems, 3)
    copies[4].wait()
    wide = 2 * BLOCK
    per = wide // TILE
    blocks = expand.shape[1] // wide
    at = 5
    for j in range(blocks):
        cols = columns(j, wide)
        grow(low, 0, n_pass, expand_here, cols, expand_bias, hidden, slope)
        grow(low, n_pass, n_query, expand_here, cols, expand_bias, hidden_query, slope_query)
        pairs = [(slope.at[:, cols], slope_out.at[:, cols]), (slope_query.at[:, cols], slope_query_out.at[:, cols])]
        for i in range(j * per, (j + 1) * per):
            pairs += [by_piece(i, hidden, hidden_out), by_piece(i, hidden_query, hidden_query_out)]
        puts += fetch(pairs, out_sems, at)
        at += len(pairs)
    copies[5].wait()
    total[0:n_pass, :] = dot(hidden[...], reduce_here[...])
    total[n_pass:count, :] = dot(hidden_query[...], reduce_here[...])

    def tell(i, tile):
        pairs = [(unit_pass.at[tile, :], unit_out.at[tile, :]), (second.at[tile, :], passage_out.at[tile, :])]
        puts.extend(fetch(pairs, out_sems, at + 2 * i))

    close = (gains, biases, term_weight, term_bias)
    close_forward(total, normed_one, 0, n_pass, 0, *close, unit_pass, scale_pass, pre_pass, second, tell)
    close_forward(
        total, normed_one, n_pass, n_query, n_pass, *close, unit_query, scale_query, pre_query, None, lambda i, tile: None
    )
    known[...] = jnp.zeros_like(known)
    known[0, 0:1, :] = jnp.broadcast_to(softplus(pre_query[...]), (n_query, TILE)).T[0:1, :]
    known[0, 1:2, :] = query_ids[...].astype(F32)
    owner = lax.broadcasted_iota(jnp.int32, (1, n_query), 1) // QLEN
    tags = jnp.zeros((1, n_query), F32)
    for query in range(n_query // QLEN):
        tags = jnp.where(owner == query, query_batch[query].astype(F32), tags)
    known[0, 2:3, :] = tags
    slots, number = score_grad.shape
    row = 3
    for first in range(0, number, TILE):
        size = min(TILE, number - first)
        known[0, row : row + slots, 0:size] = score_grad[:, first : first + size]
        row += slots
    terms = jnp.broadcast_to(softplus(pre_pass[...]), (n_pass, TILE)).T[0:1, :]
    for source in (terms, passage_ids[...].astype(F32)):
        for tile in tiles(n_pass):
            known[0, row : row + 1, :] = source[:, tile]
            row += 1
    finish_all(puts)


def match(facts, lengths, known, score_grad, passage_ids, pre, scores, pass_grad, query_grad):
    members, _, tokens = known.shape
    n_pass = passage_ids.shape[1]
    slots, queries = scores.shape
    per_query = queries // members
    together = min(members, 8)
    slot = lax.broadcasted_iota(jnp.int32, (n_pass, slots), 0) // lengths[facts[BATCH]]
    table = slot == lax.broadcasted_iota(jnp.int32, (n_pass, slots), 1)
    placed = jnp.where(table, softplus(pre[...]), 0.0).astype(BF16)
    who = lax.broadcasted_iota(jnp.int32, (queries, together * tokens), 0)
    token = lax.broadcasted_iota(jnp.int32, (queries, together * tokens), 1) // QLEN
    mine = jnp.broadcast_to(passage_ids[...].astype(F32), (8, n_pass)).T[:, 0:1]

    def several(c, carry):
        scored, placed_grads = carry
        first = c * together
        wide = jnp.concatenate([known[first + i, 0:3, :] for i in range(together)], axis=1)
        matches = jnp.where(mine == wide[1:2, :], 1.0, 0.0).astype(BF16)
        per_token = dot_tn(placed, matches)
        masked = jnp.where(wide[2:3, :] == facts[BATCH_IN_GROUP].astype(F32), 1.0, 0.0)
        weighted = wide[0:1, :] * masked
        spread = jnp.where(who == token + first * per_query, 1.0, 0.0)
        grad = jnp.dot(score_grad[...], spread, preferred_element_type=F32, precision=HIGH)
        placed_grads = placed_grads + dot_nt(matches, (grad * weighted).astype(BF16))
        scored = scored + dot_nt(per_token * weighted, spread, HIGH)
        return scored, placed_grads

    carry = (jnp.zeros(scores.shape, F32), jnp.zeros((n_pass, slots), F32))
    if members == together:
        scored, placed_grads = several(0, carry)
    else:
        scored, placed_grads = lax.fori_loop(0, members // together, several, carry)
    scores[...] = scored
    pass_grad[...] = jnp.sum(jnp.where(table, placed_grads, 0.0), axis=1, keepdims=True)
    me = facts[MEMBER]
    own = known[me, 0:3, :]
    ids = jnp.broadcast_to(own[1:2, :], (TILE, tokens)).T[:, 0:1]
    chunks = -(-queries // TILE)
    who = lax.broadcasted_iota(jnp.int32, (TILE, tokens), 0)
    token = lax.broadcasted_iota(jnp.int32, (TILE, tokens), 1) // QLEN + me * per_query
    spreads = [jnp.where(who + i * TILE == token, 1.0, 0.0) for i in range(chunks)]
    place = lax.broadcasted_iota(jnp.int32, (slots, n_pass), 1)
    slot = lax.broadcasted_iota(jnp.int32, (slots, n_pass), 0)
    per_batch = members // BATCH_PB
    first_batch = facts[BATCH] - facts[BATCH_IN_GROUP]

    def against(n, total):
        batch = lax.div(n, per_batch)
        row = 3
        grad = jnp.zeros((slots, tokens), F32)
        for spread in spreads:
            part = known[n, row : row + slots, :]
            grad = grad + jnp.dot(part, spread, preferred_element_type=F32, precision=HIGH)
            row += slots
        wide = []
        for _ in range(2):
            rows = [known[n, row + i : row + i + 1, :] for i in range(n_pass // TILE)]
            wide.append(jnp.concatenate(rows, axis=1))
            row += n_pass // TILE
        placed = jnp.where(lax.div(place, lengths[first_batch + batch]) == slot, wide[0], 0.0).astype(BF16)
        matches = jnp.where(ids == wide[1], 1.0, 0.0).astype(BF16)
        part = row_sum(grad * dot_nt(placed, matches))
        return total + jnp.where(own[2:3, :] == batch.astype(F32), part, 0.0)

    query_grad[...] = lax.fori_loop(
        0, members, against, jnp.zeros((1, tokens), F32), unroll=min(members, 8)
    )


def backward_rows(
    with_out, first, term_grad, pre, out_grad, normed_two, inverse_two, slope, normed_one, inverse_one, low_one, expand, reduce,
    gains, biases, term_weight,
    reduce_turned, expanded_grad, low_turned, sum_one, branch_grad, sums, expand_shift,
    grad_here, two_here, slope_here, one_here, low_here, expand_here, reduce_here, grown, turned, low_side, sum_here, branch_here,
    sum_two, reduce_out_grad, sems, out_sems, load=True,
):
    count, width = branch_grad.shape
    deep = slope.shape[1]
    wide = 2 * BLOCK
    blocks = deep // wide
    here = pl.ds(first, count)
    early = [
        fetch(
            [(normed_two.at[tile, :], two_here.at[tile, :])]
            + ([(out_grad.at[tile, :], grad_here.at[tile, :])] if with_out else []),
            sems,
            2 * i,
        )
        for i, tile in enumerate(tiles(count))
    ]
    base = 2 * (count // TILE)
    chunks = [
        fetch(
            [(slope.at[:, columns(j, wide)], slope_here.at[:, columns(j, wide)])]
            + ([(reduce.at[columns(j, wide), :], reduce_here.at[columns(j, wide), :])] if load else []),
            sems,
            base + 2 * j,
        )
        for j in range(blocks)
    ]
    base += 2 * blocks
    late = fetch(
        [(low_one.at[here, :], low_here), (normed_one.at[here, :], one_here)] + ([(expand, expand_here)] if load else []), sems, base
    )
    yield
    if not with_out:
        spread = jnp.broadcast_to(term_grad[...], (TILE, count)).T
    totals = [jnp.zeros((1, width), F32) for _ in range(8)]
    for i, tile in enumerate(tiles(count)):
        grad_in = term_grad[tile, :] if with_out else spread[:, 0:1]
        pre_grad = grad_in * sigmoid(pre[tile, :])
        finish_all(early[i])
        unit = two_here[tile, :]
        second_grad = pre_grad * term_weight[...]
        if with_out:
            second_grad = second_grad + grad_here[tile, :].astype(F32)
        back = norm_backward(second_grad * gains[1:2, :], unit, inverse_two[tile, :])
        rounded = back.astype(BF16)
        sum_two[tile, :] = back
        reduce_out_grad[tile, :] = rounded
        totals[1] = totals[1] + row_sum(second_grad * unit)
        totals[3] = totals[3] + row_sum(rounded.astype(F32))
        totals[5] = totals[5] + row_sum(second_grad)
        totals[6] = totals[6] + row_sum(pre_grad * (unit * gains[1:2, :] + biases[5:6, :]))
        totals[7] = totals[7] + row_sum(jnp.broadcast_to(pre_grad, (TILE, width)))
    turned[...] = reduce_out_grad[...].T
    puts = fetch([(turned, reduce_turned)], out_sems)
    for j in range(blocks):
        cols = columns(j, wide)
        finish_all(chunks[j])
        grad = dot_nt(reduce_out_grad[...], reduce_here[cols, :]) * slope_here[:, cols].astype(F32)
        rounded = grad.astype(BF16)
        grown[:, cols] = rounded
        expand_shift[:, cols] = row_sum(rounded.astype(F32))
        puts += fetch([(grown.at[:, cols], expanded_grad.at[:, cols])], out_sems, 1 + j)
    late[0].wait()
    low_side[...] = low_here[...].T
    puts += fetch([(low_side, low_turned)], out_sems, 1 + blocks)
    finish_all(late[1:])
    sum_two[...] = sum_two[...] + dot_nt(grown[...], expand_here[...])
    for i, tile in enumerate(tiles(count)):
        first_grad = sum_two[tile, :]
        unit = one_here[tile, :]
        back = norm_backward(first_grad * gains[0:1, :], unit, inverse_one[first + tile.start : first + tile.stop, :])
        rounded = back.astype(BF16)
        sum_here[tile, :] = back
        branch_here[tile, :] = rounded
        puts += fetch(
            [(sum_here.at[tile, :], sum_one.at[tile, :]), (branch_here.at[tile, :], branch_grad.at[tile, :])], out_sems, 2 + blocks + 2 * i
        )
        totals[0] = totals[0] + row_sum(first_grad * unit)
        totals[2] = totals[2] + row_sum(rounded.astype(F32))
        totals[4] = totals[4] + row_sum(first_grad)
    for i, total in enumerate(totals):
        sums[i : i + 1, :] = total
    return puts


def completed(rows):
    try:
        next(rows)
    except StopIteration as done:
        return done.value


def backward_alone(with_out, first, *refs):
    rows = backward_rows(with_out, first, *refs)
    next(rows)
    finish_all(completed(rows))


def backward_layer(members, facts, lengths, known, score_grad, passage_ids, *refs):
    pre, normed_two, inverse_two, slope, hidden_pass, hidden_query = refs[13:19]
    pass_out, query_out, sent, scores = refs[19:26], refs[26:33], refs[33:36], refs[36]
    pass_own, query_own, (hid_p, hid_q, buffers, sems, out_sems, pass_term, query_term) = refs[37:53], refs[53:67], refs[67:]
    pass_in = (pass_term,) + refs[:13]
    expand_here, reduce_here, grown_p, turned_p, low_p = pass_own[5:10]
    grown_q, turned_q, low_q = query_own[5:8]
    query_in = (query_term, pre, pass_in[2], normed_two, inverse_two, slope) + pass_in[6:]
    pass_rows = backward_rows(True, 0, *pass_in, *pass_out, *pass_own)
    query_rows = backward_rows(
        False, grown_p.shape[0], *query_in, *query_out, *query_own[:5], expand_here, reduce_here, *query_own[5:], load=False
    )
    next(pass_rows)
    next(query_rows)
    copies = fetch([(hidden_pass, hid_p), (hidden_query, hid_q)], sems)
    match(facts, lengths, known, score_grad, passage_ids, pass_in[1], scores, pass_term, query_term)
    puts = completed(pass_rows) + completed(query_rows)
    finish_all(copies)
    core = 1 - facts[0]
    spread = grown_p.shape[1]
    width = low_p.shape[0]
    third = spread // 6
    half = pl.ds(pl.multiple_of(core * (width // 2), TILE), width // 2)
    for piece in range(3):

        def emit(leaf, side, row, part):
            buffers[piece, leaf, side, row : row + part.shape[0], :] = part

        def tell(rows, place):
            puts.extend(
                fetch([(buffers.at[piece, :, :, rows, :], sent[piece].at[:, :, rows, :])], out_sems, 2 * piece + place)
            )

        cols = pl.ds(pl.multiple_of(core * (spread // 2) + piece * third, TILE), third)
        inner_leaves(
            members, low_p, low_q, grown_p.at[:, cols], grown_q.at[:, cols], turned_p.at[half, :], turned_q.at[half, :],
            hid_p.at[piece], hid_q.at[piece], emit, tell,
        )
    finish_all(puts)


def attend_backward(mixed, attended_grad, stats, inner, mixed_grad, logit_grads, first, count, width, mask, tell):
    rows = slice(first, first + count)
    step = min(BLOCK, count)

    def pair(hp, carry):
        query = mixed[rows, columns(hp, 2 * HEAD)]
        grad = attended_grad[rows, columns(hp, 2 * HEAD)]
        query_grad = jnp.zeros((count, 2 * HEAD), F32)
        kept = []
        for sub in (0, 1):
            lanes = head_lanes(sub)
            total = stats[2 * hp + sub, :, rows]
            level = inner[2 * hp + sub, :, rows]
            for at in range(0, count, step):
                tile = slice(at, at + step)
                here = slice(first + at, first + at + step)
                key = mixed[here, columns(hp, 2 * HEAD, width)]
                value = mixed[here, columns(hp, 2 * HEAD, 2 * width)]
                key_here = jnp.where(lanes, key, jnp.zeros_like(key))
                value_here = jnp.where(lanes, value, jnp.zeros_like(value))
                weights = jnp.exp(dot_nt(key_here, query) + (mask[tile, :] - total))
                logit_grad = (weights * (dot_nt(value_here, grad) - level)).astype(BF16)
                logit_grads[sub, tile, 0:count] = logit_grad
                kept.append((dot(logit_grad, query), dot(weights.astype(BF16), grad)))
        for i, at in enumerate(range(0, count, step)):
            here = slice(first + at, first + at + step)
            for part in (0, 1):
                mixed_grad[here, columns(hp, 2 * HEAD, (part + 1) * width)] = jnp.where(
                    head_lanes(0), kept[i][part], kept[i + count // step][part]
                ).astype(BF16)
        for sub in (0, 1):
            key = mixed[rows, columns(hp, 2 * HEAD, width)]
            key_here = jnp.where(head_lanes(sub), key, jnp.zeros_like(key))
            query_grad = query_grad + dot_tn(logit_grads[sub, 0:count, 0:count], key_here)
        mixed_grad[rows, columns(hp, 2 * HEAD)] = (query_grad * SCALE).astype(BF16)
        tell(hp)
        return carry

    lax.fori_loop(0, HEADS // 2, pair, 0)


def backward_attention(
    members, sides, lengths, passages, queries, pass_grad, query_grad, project_out, mixed, attended, stats,
    attended_turned, project_in, pass_sum, query_sum, sums_pass, sums_query, shift_pass, shift_query,
    grad_out, turned_out, vectors, pass_out, query_out, *rest,
):
    sent = rest[0] if members else None
    (
        out_here, pass_here, query_here, mixed_here, attended_here, mixed_grad, turned,
        attended_grad, inner, logit_grads, mask, query_mask, across_here, in_here, pass_sum_here, query_sum_here, buffers,
        sems, out_sems,
    ) = rest[-19:]
    n_pass, width = passages.shape
    n_query = queries.shape[0]
    count = n_pass + n_query
    copies = fetch(
        [
            (project_out, out_here), (pass_grad, pass_here), (query_grad, query_here), (attended, attended_here),
            (mixed, mixed_here), (attended_turned, across_here), (project_in, in_here), (pass_sum, pass_sum_here),
            (query_sum, query_sum_here),
        ],
        sems,
    )
    query_mask[...] = same_slot(n_query, QLEN)
    mask[...] = same_slot(n_pass, lengths[sides[BATCH]])
    turned[:, 0:n_pass] = passages[...].T
    turned[:, n_pass:count] = queries[...].T
    puts = fetch([(turned, turned_out)], out_sems)
    finish_all(copies[:3])
    attended_grad[0:n_pass, :] = dot_nt(pass_here[...], out_here[...]).astype(BF16)
    attended_grad[n_pass:count, :] = dot_nt(query_here[...], out_here[...]).astype(BF16)
    heads = 16
    owner = lax.broadcasted_iota(jnp.int32, (heads, width), 1) // HEAD
    spread = jnp.where(owner == lax.broadcasted_iota(jnp.int32, (heads, width), 0), 1.0, 0.0)
    copies[3].wait()
    for tile in tiles(count):
        product = attended_grad[tile, :].astype(F32) * attended_here[tile, :].astype(F32)
        levels = dot_nt(spread, product, HIGH)
        for head in range(HEADS):
            inner[head, :, tile] = levels[head : head + 1, :]
    copies[4].wait()
    nothing = lambda hp: None
    attend_backward(mixed_here, attended_grad, stats, inner, mixed_grad, logit_grads, n_pass, n_query, width, query_mask, nothing)
    attend_backward(mixed_here, attended_grad, stats, inner, mixed_grad, logit_grads, 0, n_pass, width, mask, nothing)
    puts += fetch([(mixed_grad, grad_out)], out_sems, 1)
    shifts = [row_sum(mixed_grad[:, first : first + width].astype(F32)) for first in (0, 2 * width)]
    whole = jnp.concatenate([sums_pass[...] + sums_query[...], *shifts, jnp.zeros((6, width), F32)])
    deep_shift = shift_pass[...] + shift_query[...]
    if members:
        shard = width // members
        lane = lax.broadcasted_iota(jnp.int32, (width, TILE), 1)
        source = lax.broadcasted_iota(jnp.int32, (width, TILE), 0)
        row = lax.broadcasted_iota(jnp.int32, (16, TILE), 0)
        for leaf in range(members):
            chosen = jnp.where((source == lane + leaf * shard) & (lane < shard), 1.0, 0.0)
            block = jnp.dot(whole, chosen, preferred_element_type=F32, precision=HIGH)
            for i in range(3):
                part = deep_shift[:, (3 * leaf + i) * TILE : (3 * leaf + i + 1) * TILE]
                block = jnp.where(row == 10 + i, part, block)
            vectors[leaf] = block
        finish_all(copies[5:6])
        core = 1 - sides[0]
        wide = width // 2
        for piece in range(3):

            def emit(leaf, side, row, part):
                buffers[piece, leaf, side, row : row + part.shape[0], :] = part

            narrow = pl.ds(pl.multiple_of(core * wide + piece * TILE, TILE), TILE)
            outer_leaves(
                members, turned, mixed_grad.at[:, pl.ds(pl.multiple_of(core * 3 * wide + piece * wide, TILE), wide)],
                across_here, pass_here.at[:, narrow], query_here.at[:, narrow], emit,
            )
            vector_leaves(members, piece, core, vectors, buffers.shape[3] - 8, emit)
            puts += fetch([(buffers.at[piece], sent.at[piece])], out_sems, 2 + piece)
        late = copies[6:]
    else:
        vectors[0:16, :] = whole
        for i in range(deep_shift.shape[1] // width):
            vectors[16 + i : 17 + i, :] = deep_shift[:, i * width : (i + 1) * width]
        late = copies[5:]
    finish_all(late)
    for first in range(0, width, BLOCK):
        cols = slice(first, first + BLOCK)
        weight = in_here[cols, :]
        pass_out[:, cols] = (dot_nt(mixed_grad[0:n_pass, :], weight) + pass_sum_here[:, cols]).astype(BF16)
        query_out[:, cols] = (dot_nt(mixed_grad[n_pass:count, :], weight) + query_sum_here[:, cols]).astype(BF16)
    finish_all(puts)


def inner_leaves(members, low_p, low_q, grad_p, grad_q, turn_p, turn_q, hid_p, hid_q, emit, tell):
    width = low_p.shape[0]
    shard = width // members
    for first in range(0, width, width // 2):
        rows = slice(first, first + width // 2)
        part = dot(low_p[rows, :], grad_p[...]) + dot(low_q[rows, :], grad_q[...])
        for at in range(0, width // 2, shard // 2):
            leaf, side = divmod((first + at) // (shard // 2), 2)
            for block in range(part.shape[1] // TILE):
                emit(leaf, side, block * (shard // 2), part[at : at + shard // 2, block * TILE : (block + 1) * TILE])
    base = (shard // 2) * (grad_p.shape[1] // TILE)
    tell(slice(0, base), 0)
    for leaf in range(0, members, 4):
        span = slice(leaf * TILE, (leaf + 4) * TILE)
        part = dot(turn_p[...], hid_p[:, span]) + dot(turn_q[...], hid_q[:, span])
        for i in range(4):
            for side in (0, 1):
                emit(leaf + i, side, base, part[side * (width // 4) : (side + 1) * (width // 4), i * TILE : (i + 1) * TILE])
    tell(slice(base, base + width // 4), 1)


def outer_leaves(members, turned, grad, attended, branch_p, branch_q, emit):
    width = turned.shape[0]
    n_pass = branch_p.shape[0]
    shard = width // members
    for first in range(0, width, width // 2):
        rows = slice(first, first + width // 2)
        parts = [
            dot(turned[rows, :], grad[...]),
            dot(attended[rows, 0:n_pass], branch_p[...]) + dot(attended[rows, n_pass:], branch_q[...]),
        ]
        for at in range(0, width // 2, shard // 2):
            leaf, side = divmod((first + at) // (shard // 2), 2)
            block = 0
            for part in parts:
                for lane in range(0, part.shape[1], TILE):
                    emit(leaf, side, block * (shard // 2), part[at : at + shard // 2, lane : lane + TILE])
                    block += 1


def side_of(bit_at, mine, leaf, side):
    index = 2 * leaf + side
    high, bit, rest = index >> (bit_at + 1), (index >> bit_at) & 1, index & ((1 << bit_at) - 1)
    return jnp.where(mine == bit, 0, 1), (high << bit_at) + rest


def inner_kept(
    members, piece, bit_at, sides, low_pass, low_query, grad_pass, grad_query, reduce_pass, reduce_query, hidden_pass, hidden_query,
    received, leaves, stays,
    low_p, low_q, grad_p, grad_q, turn_p, turn_q, hid_p, hid_q, came, both, sems, out_sems,
):
    width = low_pass.shape[0]
    spread = grad_pass.shape[1]
    third = spread // 6
    cols = pl.ds(pl.multiple_of(sides[0] * (spread // 2) + piece * third, TILE), third)
    half = pl.ds(pl.multiple_of(sides[0] * (width // 2), TILE), width // 2)
    base = (width // members // 2) * (third // TILE)
    spans = [slice(0, base), slice(base, base + width // 4)]
    early = fetch(
        [
            (low_pass, low_p), (low_query, low_q), (grad_pass.at[:, cols], grad_p), (grad_query.at[:, cols], grad_q),
            (received.at[:, :, spans[0], :], came.at[:, :, spans[0], :]),
        ],
        sems,
    )
    late = fetch(
        [
            (reduce_pass.at[half, :], turn_p), (reduce_query.at[half, :], turn_q),
            (hidden_pass.at[piece], hid_p), (hidden_query.at[piece], hid_q),
            (received.at[:, :, spans[1], :], came.at[:, :, spans[1], :]),
        ],
        sems, 5,
    )
    puts = []

    def emit(leaf, side, row, part):
        rows = slice(row, row + part.shape[0])
        both[*side_of(bit_at, sides[1 + piece], leaf, side), rows, :] = part + came[leaf, side, rows, :]

    def tell(rows, place):
        pairs = [(both.at[1, :, rows, :], leaves.at[:, rows, :]), (both.at[0, :, rows, :], stays.at[:, rows, :])]
        puts.extend(fetch(pairs, out_sems, 2 * place))
        if place == 0:
            finish_all(late)

    finish_all(early)
    inner_leaves(members, low_p, low_q, grad_p, grad_q, turn_p, turn_q, hid_p, hid_q, emit, tell)
    finish_all(puts)


def outer_kept(
    members, places, sides, turned, mixed_grad, attended, branch_pass, branch_query, vectors, received, *refs
):
    leaves, stays = refs[0:6:2], refs[1:6:2]
    rows_here, grad, attended_here, branch_p, branch_q, came, both, sems, out_sems = refs[6:]
    width = turned.shape[0]
    wide = width // 2
    cols = pl.ds(pl.multiple_of(sides[0] * 3 * wide, TILE), 3 * wide)
    narrow = pl.ds(pl.multiple_of(sides[0] * wide, TILE), wide)
    copies = fetch(
        [
            (turned, rows_here), (mixed_grad.at[:, cols], grad), (attended, attended_here),
            (branch_pass.at[:, narrow], branch_p), (branch_query.at[:, narrow], branch_q),
        ]
        + [(received.at[piece], came.at[piece]) for piece in range(3)],
        sems,
    )
    finish_all(copies[:5])
    puts = []
    for piece in range(3):
        copies[5 + piece].wait()

        def emit(leaf, side, row, part):
            rows = slice(row, row + part.shape[0])
            both[piece, *side_of(places[piece], sides[1 + piece], leaf, side), rows, :] = part + came[piece, leaf, side, rows, :]

        outer_leaves(
            members, rows_here, grad.at[:, piece * wide : (piece + 1) * wide], attended_here,
            branch_p.at[:, piece * TILE : (piece + 1) * TILE], branch_q.at[:, piece * TILE : (piece + 1) * TILE], emit,
        )
        vector_leaves(members, piece, sides[0], vectors, both.shape[3] - 8, emit)
        puts += fetch([(both.at[piece, 1], leaves[piece]), (both.at[piece, 0], stays[piece])], out_sems, 2 * piece)
    finish_all(puts)


def vector_leaves(members, piece, core, vectors, row, emit):
    for leaf in range(members):
        for side in (0, 1):
            if piece == 0:
                part = jnp.where(core == 0, vectors[leaf, 8 * side : 8 * side + 8, :], 0.0)
            else:
                part = jnp.zeros((8, TILE), F32)
            emit(leaf, side, row, part)


def finish_inner(sides, mine, near, other, beyond, expand, reduce):
    rows, wide = expand.shape
    half = rows // 2
    blocks = wide // 6 // TILE
    deep = reduce.shape[1] // 2
    for far, pair in enumerate(((mine, near), (other, beyond))):
        core = jnp.bitwise_xor(sides[0], far)
        for piece in range(3):
            for there, source in enumerate(pair):
                side = pl.multiple_of(jnp.bitwise_xor(sides[1], there) * half, 8)
                for block in range(blocks):
                    at = core * (wide // 2) + (piece * blocks + block) * TILE
                    expand[pl.ds(side, half), pl.ds(pl.multiple_of(at, TILE), TILE)] = source[
                        piece, block * half : (block + 1) * half, :
                    ]
            parts = [source[piece, blocks * half :, :] for source in pair]
            low = jnp.where(sides[1] == 0, parts[0], parts[1])
            high = jnp.where(sides[1] == 0, parts[1], parts[0])
            reduce[piece * TILE : (piece + 1) * TILE, pl.ds(pl.multiple_of(core * deep, TILE), deep)] = (
                jnp.concatenate([low, high]).T
            )


def finish_outer(sides, mine, near, other, beyond, project_in, project_out, gains, biases, term_weight, term_bias, expand_bias):
    rows, wide = project_in.shape
    half = rows // 2
    for far, pair in enumerate(((mine, near), (other, beyond))):
        core = jnp.bitwise_xor(sides[0], far)
        for there, source in enumerate(pair):
            side = pl.multiple_of(jnp.bitwise_xor(sides[1], there) * half, 8)
            for piece in range(3):
                for block in range(4):
                    part = source[piece, block * half : (block + 1) * half, :]
                    if block < 3:
                        at = core * (wide // 2) + (piece * 3 + block) * TILE
                        project_in[pl.ds(side, half), pl.ds(pl.multiple_of(at, TILE), TILE)] = part
                    else:
                        at = core * (wide // 6) + piece * TILE
                        project_out[pl.ds(side, half), pl.ds(pl.multiple_of(at, TILE), TILE)] = part
    at = mine.shape[1] - 8
    parts = [
        jnp.where(sides[0] == 0, a[0, at:, :], b[0, at:, :]) for a, b in ((mine, other), (near, beyond))
    ]
    low = jnp.where(sides[1] == 0, parts[0], parts[1])
    high = jnp.where(sides[1] == 0, parts[1], parts[0])
    gains[...] = low[0:2, :rows]
    biases[0:2, :] = high[0:2, :rows]
    biases[2:6, :] = low[2:6, :rows]
    term_weight[...] = low[6:7, :rows]
    term_bias[...] = low[7:8, 0:1]
    for i in range(expand_bias.shape[1] // TILE):
        expand_bias[:, i * TILE : (i + 1) * TILE] = high[2 + i : 3 + i, :]


def run(kernel, outs, kinds, scratch, args, after=(), aliases=None, limit=58):
    specs = {"s": IN_SMEM, "v": IN_VMEM, "h": IN_PLACE, "a": IN_PLACE}
    shapes = [
        pltpu.HBM(dims, dtype) if kind == "h" else jax.ShapeDtypeStruct(dims, dtype) for kind, dims, dtype in outs
    ]
    given = [
        pltpu.with_memory_space_constraint(a, pltpu.HBM) if kind == "h" else a for a, kind in zip(args, kinds)
    ]
    many = len(outs) > 1
    known = len(args)

    def body(*refs):
        kernel(*refs[:known], *refs[known + len(after) :])

    return pl.pallas_call(
        body,
        out_shape=shapes if many else shapes[0],
        in_specs=[specs[kind] for kind in kinds] + [IN_PLACE] * len(after),
        out_specs=[specs[o[0]] for o in outs] if many else specs[outs[0][0]],
        scratch_shapes=scratch,
        input_output_aliases=aliases or {},
        compiler_params=pltpu.CompilerParams(vmem_limit_bytes=limit << 20),

    )(*given, *[pltpu.with_memory_space_constraint(a, pltpu.HBM) for a in after])


def contract_rows(left, right):
    return lax.dot_general(
        left, right, (((0,), (0,)), ((), ())), preferred_element_type=F32
    )


GROUP_FIRST = (("pb", 2), ("pa", 1))
ROW_FIRST = (("pa", 1), ("pb", 2))


def swap(value, axis, distance):
    return lax.ppermute(
        value, axis, [(i, i ^ distance) for i in range(lax.axis_size(axis))]
    )


def bit(axis, distance):
    return (lax.axis_index(axis) >> (distance.bit_length() - 1)) & 1


def pick(value, index, dim):
    return lax.dynamic_index_in_dim(value, index, dim, keepdims=False)


def group_gather(mine):
    distance = 1
    while distance < lax.axis_size("pa"):
        other = swap(mine, "pa", distance)
        mine = jnp.where(
            bit("pa", distance) == 0, jnp.concatenate([mine, other]), jnp.concatenate([other, mine])
        )
        distance *= 2
    return mine


def steps_of(order):
    steps = [(axis, distance) for axis, distance in order]
    distance = 2
    while distance < lax.axis_size("pa"):
        steps.append(("pa", distance))
        distance *= 2
    return steps


def tree_sum(send, keep, order):
    names = []
    distance = lax.axis_size("pa") // 2
    while distance:
        names.append(("pa", distance))
        distance //= 2
    names.append(("pb", 2))
    received = swap(send, "pb", 1)
    for axis, distance in steps_of(order):
        dim = names.index((axis, distance))
        names.pop(dim)
        mine = bit(axis, distance)
        send = pick(keep, 1 - mine, dim) + pick(received, 1 - mine, dim)
        keep = pick(keep, mine, dim) + pick(received, mine, dim)
        received = swap(send, axis, distance)
    mine = keep + received
    other = swap(mine, "pb", 2)
    high = bit("pb", 2)
    return jnp.where(high == 0, jnp.stack([mine, other]), jnp.stack([other, mine]))


def cut(matrix):
    bits = lax.axis_size("pa").bit_length() - 1
    rows = matrix.shape[0] >> (bits + 1)
    return matrix.reshape((2,) * (bits + 1) + (rows, matrix.shape[1]))


def summed_rows(left, right, order):
    core = bit("pb", 1)
    half = right.shape[1] // 2
    parts = [
        cut(contract_rows(left, lax.dynamic_slice_in_dim(right, side * half, half, axis=1)))
        for side in (1 - core, core)
    ]
    mine = tree_sum(parts[0], parts[1], order)
    mine = mine.reshape(-1, half)
    other = swap(mine, "pb", 1)
    return jnp.where(
        core == 0, jnp.concatenate([mine, other], 1), jnp.concatenate([other, mine], 1)
    )


def total_of_all(value):
    distance = 1
    while distance < lax.axis_size("pb"):
        value = value + swap(value, "pb", distance)
        distance *= 2
    distance = 1
    while distance < lax.axis_size("pa"):
        value = value + swap(value, "pa", distance)
        distance *= 2
    return value


BATCH_IN_GROUP, BATCH, MEMBER = 5, 6, 7
LEAF_BITS = (("pa", 4), ("pa", 2), ("pa", 1), ("pb", 2))
PIECE_ORDERS = (
    (("pb", 2), ("pa", 1), ("pa", 2), ("pa", 4)),
    (("pa", 1), ("pa", 2), ("pb", 2), ("pa", 4)),
    (("pa", 2), ("pb", 2), ("pa", 1), ("pa", 4)),
)
PLACES = tuple(len(LEAF_BITS) - 1 - LEAF_BITS.index(order[0]) for order in PIECE_ORDERS)


def begun(parts):
    held = []
    for (leaving, staying), order in zip(parts, PIECE_ORDERS):
        rest = tuple(b for b in LEAF_BITS if b != order[0])
        held.append(([(staying, rest), (swap(leaving, *order[0]), rest)], (order[0],)))
    return held


def chosen(names, settled, current=None):
    return tuple(1 if name == current else 0 if name in settled else None for name in names)


def part_of(array, names, settled, current, rows):
    wants = chosen(names, settled, current)
    starts = [0 if want is None else bit(*name) ^ want for name, want in zip(names, wants)]
    sizes = [2 if want is None else 1 for want in wants]
    part = lax.dynamic_slice(array.reshape((2,) * len(names) + (rows, TILE)), starts + [0, 0], sizes + [rows, TILE])
    return part.reshape((2,) * wants.count(None) + (rows, TILE))


def onward(held, step, sent):
    moved = []
    for (terms, settled), order, leaving in zip(held, PIECE_ORDERS, sent):
        left = tuple(b for b in LEAF_BITS if b not in settled and b != order[step])
        moved.append((terms + [(swap(leaving, *order[step]), left)], settled + (order[step],)))
    return moved


def advance(held, step, rows):
    sent = []
    for (terms, settled), order in zip(held, PIECE_ORDERS):
        sent.append(sum(part_of(array, names, settled, order[step], rows) for array, names in terms))
    return onward(held, step, sent)


def fold(plans, through, joined, facts, *refs):
    count = sum(len(plan) for plan in plans)
    terms = refs[:count]
    outs = refs[count + through : count + through + (1 if joined else len(plans))]
    scratch = refs[count + through + len(outs) + through :]
    sems, out_sems = scratch[-2:]
    pairs = []
    at = 0
    for plan in plans:
        for wants in plan:
            index = tuple(
                slice(None) if want is None else jnp.bitwise_xor(facts[len(LEAF_BITS) - LEAF_BITS.index(name)], want) for name, want in wants
            )
            pairs.append((terms[at].at[index], scratch[at]))
            at += 1
    copies = fetch(pairs, sems)
    puts = []
    at = 0
    for i, plan in enumerate(plans):
        finish_all(copies[at : at + len(plan)])
        total = scratch[at][...]
        for k in range(1, len(plan)):
            total = total + scratch[at + k][...]
        scratch[at][...] = total
        puts += fetch([(scratch[at], outs[0].at[i] if joined else outs[i])], out_sems, i)
        at += len(plan)
    finish_all(puts)


def fold_by_kernel(facts, held, step, rows, through=(), after=(), joined=False):
    plans = []
    args = []
    kinds = ""
    scratch = []
    outs = []
    for (terms, settled), order in zip(held, PIECE_ORDERS):
        plan = []
        for array, names in terms:
            wants = chosen(names, settled, order[step])
            plan.append(tuple(zip(names, wants)))
            args.append(array.reshape((2,) * len(names) + (rows, TILE)))
            kinds += "a" if plan[1:] else "h"
            dims = (2,) * wants.count(None) + (rows, TILE)
            scratch.append(pltpu.VMEM(dims, F32))
        plans.append(plan)
        outs.append(("h", dims, F32))
    if joined:
        outs = [("h", (len(plans), rows, TILE), F32)]
    done = run(
        partial(fold, plans, len(through), joined),
        outs + [("h", a.shape, a.dtype) for a in through],
        "s" + kinds + "h" * len(through),
        scratch + [pltpu.SemaphoreType.DMA((len(args),)), pltpu.SemaphoreType.DMA((len(plans),))],
        (facts, *args, *through),
        after,
        {1 + len(args) + i: len(outs) + i for i in range(len(through))},
        12,
    )
    return done if len(outs) + len(through) > 1 else [done]


def advance_by_kernel(facts, held, step, rows, through=(), after=()):
    done = fold_by_kernel(facts, held, step, rows, through, after)
    return onward(held, step, done[:3]), done[3:]


def last_exchange(facts, held, rows, through=()):
    step = len(LEAF_BITS) - 1
    name = PIECE_ORDERS[0][step]
    sent, *through = fold_by_kernel(facts, held, step, rows, through, joined=True)
    came = swap(sent, *name)
    total = jnp.stack(
        [sum(part_of(array, names, settled + (name,), None, rows) for array, names in terms) for terms, settled in held]
    )
    return total + came, through


def on_device(
    passages, queries, passage_ids, query_ids, batch_length, query_batch, project_in, project_out, expand_weight,
    expand_bias, reduce_weight, norm_gains, biases, term_weight, term_bias, out_grad, score_grad,
):
    members = lax.axis_size("pa")
    member_index = lax.axis_index("pa")
    local_batch = member_index // (members // BATCH_PB)
    facts = jnp.stack(
        [
            bit("pb", 1), *(bit(*name) for name in reversed(LEAF_BITS)), local_batch,
            lax.axis_index("pb") * BATCH_PB + local_batch, member_index,
        ]
    )
    n_pass, width = passages.shape
    n_query = queries.shape[0]
    count = n_pass + n_query
    deep = expand_weight.shape[1]
    slots = score_grad.shape[1]
    bias_row = expand_bias[None]
    term_row = term_weight

    blocks = deep // (2 * BLOCK)
    by_three = (3, n_pass, deep // 3)
    weights = [pltpu.VMEM(expand_weight.shape, BF16), pltpu.VMEM(reduce_weight.shape, BF16)]

    def vmem(*dims, dtype=BF16):
        return pltpu.VMEM(dims, dtype)

    def sems(number):
        return pltpu.SemaphoreType.DMA((number,))

    known_rows = 3 + slots * (-(-score_grad.shape[0] // TILE)) + 2 * (n_pass // TILE)
    (
        mixed, attended, attended_turned, stats, normed_one, inverse_one, low,
        hidden_query, slope_query, unit_query, scale_query, pre_query,
        hidden, slope, unit_pass, scale_pass, pre_pass, passage_out, known,
    ) = run(
        forward_layer,
        [
            ("h", (count, 3 * width), BF16), ("h", (count, width), BF16),
            ("h", (width, count), BF16), ("v", (HEADS, 1, count), F32), ("h", (count, width), F32),
            ("v", (count, 1), F32), ("h", (count, width), BF16), ("h", (3, n_query, deep // 3), BF16),
            ("h", (n_query, deep), BF16), ("v", (n_query, width), F32), ("v", (n_query, 1), F32), ("v", (n_query, 1), F32),
            ("h", by_three, BF16), ("h", (n_pass, deep), BF16), ("h", (n_pass, width), F32),
            ("v", (n_pass, 1), F32), ("v", (n_pass, 1), F32), ("h", (n_pass, width), BF16),
            ("v", (1, known_rows, TILE), F32),
        ],
        "ssvvhhhhvvvvsvsvv",
        [
            vmem(*project_in.shape), vmem(*project_out.shape), *weights, vmem(count, 3 * width), vmem(count, width),
            vmem(width, count), vmem(count, width, dtype=F32), vmem(count, width), vmem(n_query, deep), vmem(n_query, deep),
            vmem(n_pass, deep), vmem(n_pass, deep), vmem(n_pass, width, dtype=F32), vmem(n_pass, width),
            vmem(n_pass, n_pass, dtype=F32), vmem(n_query, n_query, dtype=F32), vmem(count, width, dtype=F32),
            sems(6), sems(5 + 2 * blocks + 2 * (deep // TILE) + 2 * (n_pass // TILE)),
        ],
        (facts, batch_length, passages, queries, project_in, project_out, expand_weight, reduce_weight, bias_row, norm_gains,
         biases, term_row, term_bias, query_ids[None], query_batch, score_grad.T, passage_ids[None]),
    )
    known = group_gather(known)
    def back_outs(rows):
        return [
            ("h", (width, rows), BF16), ("h", (rows, deep), BF16), ("h", (width, rows), BF16),
            ("h", (rows, width), F32), ("h", (rows, width), BF16), ("v", (8, width), F32), ("v", (1, deep), F32),
        ]

    back_kinds = "vvhhvhhvhhhvvv"

    def back_scratch(rows):
        return [
            vmem(rows, width), vmem(rows, width, dtype=F32), vmem(rows, deep), vmem(rows, width, dtype=F32), vmem(rows, width),
            *weights, vmem(rows, deep), vmem(width, rows), vmem(width, rows), vmem(rows, width, dtype=F32), vmem(rows, width),
            vmem(rows, width, dtype=F32), vmem(rows, width),
            sems(3 + 2 * blocks + 2 * (rows // TILE)), sems(2 + blocks + 2 * (rows // TILE)),
        ]

    def back_args(term_grad, pre, unit, scale, slope_here):
        return (term_grad, pre, out_grad, unit, scale, slope_here, normed_one, inverse_one, low,
                expand_weight, reduce_weight, norm_gains, biases, term_row)

    fits = deep // members == 3 * TILE
    shard = width // members
    leaf_rows = (deep // 6 // TILE * (shard // 2) + width // 4, 4 * (shard // 2) + 8)
    if fits:
        dims = (members, 2, leaf_rows[0], TILE)
        third = deep // 6
        pass_scratch, query_scratch = back_scratch(n_pass), back_scratch(n_query)
        (
            rg_pass, eg_pass, low_pass, one_pass, bg_pass, sums_pass, shift_pass,
            rg_query, eg_query, low_query, one_query, bg_query, sums_query, shift_query, *sent, scores
        ) = run(
            partial(backward_layer, members),
            back_outs(n_pass) + back_outs(n_query) + [("h", dims, F32)] * 3 + [("v", score_grad.shape[::-1], F32)],
            "ssvvv" + back_kinds[1:] + "vhvhhh",
            pass_scratch + query_scratch[:5] + query_scratch[7:]
            + [vmem(*by_three), vmem(3, n_query, deep // 3), vmem(3, *dims, dtype=F32), sems(2), sems(6), vmem(n_pass, 1, dtype=F32),
               vmem(1, n_query, dtype=F32)],
            (facts, batch_length, known, score_grad.T, passage_ids[None])
            + back_args(None, pre_pass, unit_pass, scale_pass, slope)[1:]
            + (pre_query, unit_query, scale_query, slope_query, hidden, hidden_query),
        )
        came = [swap(part, "pb", 1) for part in sent]
        parts = []
        for piece, order in enumerate(PIECE_ORDERS):
            half = (leaf_rows[0], TILE)
            parts.append(
                run(
                    partial(inner_kept, members, piece, PLACES[piece]),
                    [("h", (members,) + half, F32)] * 2,
                    "s" + "h" * 8 + "a",
                    [
                        vmem(width, n_pass), vmem(width, n_query), vmem(n_pass, third), vmem(n_query, third),
                        vmem(width // 2, n_pass), vmem(width // 2, n_query), vmem(n_pass, deep // 3), vmem(n_query, deep // 3),
                        vmem(*dims, dtype=F32), vmem(2, members, *half, dtype=F32), sems(10), sems(4),
                    ],
                    (facts, low_pass, low_query, eg_pass, eg_query, rg_pass, rg_query, hidden,
                     hidden_query, came[piece]),
                    limit=18,
                )
            )
        inner = begun(parts)
        pins = tuple(leaving for leaving, _ in parts)
        extra = [("v", (members, 16, TILE), F32)]
        last = [("h", (3, members, 2, leaf_rows[1], TILE), F32)]
    else:
        scores, pass_term_grad, query_term_grad = run(
            match,
            [("v", score_grad.shape[::-1], F32), ("v", (n_pass, 1), F32), ("v", (1, n_query), F32)],
            "ssvvvv",
            [],
            (facts, batch_length, known, score_grad.T, passage_ids[None], pre_pass),
        )
        rg_pass, eg_pass, low_pass, one_pass, bg_pass, sums_pass, shift_pass = run(
            partial(backward_alone, True, 0), back_outs(n_pass), back_kinds, back_scratch(n_pass),
            back_args(pass_term_grad, pre_pass, unit_pass, scale_pass, slope),
        )
        rg_query, eg_query, low_query, one_query, bg_query, sums_query, shift_query = run(
            partial(backward_alone, False, n_pass), back_outs(n_query), back_kinds, back_scratch(n_query),
            back_args(query_term_grad, pre_query, unit_query, scale_query, slope_query),
        )
        pins = ()
        extra = [("v", (16 + deep // width, width), F32)]
        last = []
    mixed_grad, turned, vectors, passage_grad, query_grad, *sent = run(
        partial(backward_attention, members if fits else 0),
        [("h", (count, 3 * width), BF16), ("h", (width, count), BF16)]
        + extra
        + [("v", (n_pass, width), BF16), ("v", (n_query, width), BF16)]
        + last,
        "ssvvhhhhhv" + "hhhh" + "vvvv",
        [
            vmem(*project_out.shape), vmem(n_pass, width), vmem(n_query, width), vmem(count, 3 * width), vmem(count, width),
            vmem(count, 3 * width), vmem(width, count), vmem(count, width), vmem(HEADS, 1, count, dtype=F32),
            vmem(2, n_pass, n_pass), vmem(n_pass, n_pass, dtype=F32), vmem(n_query, n_query, dtype=F32),
            vmem(width, count), vmem(*project_in.shape), vmem(n_pass, width, dtype=F32), vmem(n_query, width, dtype=F32),
            vmem(*(last[0][1] if fits else (8, TILE)), dtype=F32), sems(9), sems(5),
        ],
        (facts, batch_length, passages, queries, bg_pass, bg_query, project_out, mixed, attended, stats, attended_turned, project_in,
         one_pass, one_query, sums_pass, sums_query, shift_pass, shift_query),
        pins,
    )
    if fits:
        inner, sent = advance_by_kernel(facts, inner, 1, leaf_rows[0], tuple(sent))
        half = (leaf_rows[1], TILE)
        dims = (3, members, 2) + half
        parts = run(
            partial(outer_kept, members, PLACES),
            [("h", (members,) + half, F32)] * 6,
            "s" + "h" * 5 + "va",
            [
                vmem(width, count), vmem(count, 3 * width // 2), vmem(width, count), vmem(n_pass, width // 2),
                vmem(n_query, width // 2), vmem(*dims, dtype=F32), vmem(3, 2, members, *half, dtype=F32), sems(8), sems(6),
            ],
            (facts, turned, mixed_grad, attended_turned, bg_pass, bg_query, vectors, swap(sent[0], "pb", 1)),
            limit=24,
        )
        inner, _ = advance_by_kernel(facts, inner, 2, leaf_rows[0], after=tuple(parts[0:6:2]))
        inner_mine, late = last_exchange(facts, inner, leaf_rows[0], (parts[2],))
        outer = begun([parts[0:2], (late[0], parts[3]), parts[4:6]])
        for step in (1, 2):
            outer = advance(outer, step, leaf_rows[1])
        outer_mine, _ = last_exchange(facts, outer, leaf_rows[1])

        def finish(kernel, mine, outs):
            near = swap(mine, "pb", 2)
            args = (facts, mine, near, swap(mine, "pb", 1), swap(near, "pb", 1))
            return run(kernel, outs, "svvvv", [], args, limit=12)

        expand_total, reduce_total = finish(
            finish_inner, inner_mine, [("v", (shard, deep), F32), ("v", (deep // members, width), F32)]
        )
        in_total, out_total, gains_grad, biases_grad, term_grad, bias_grad, expand_shift = finish(
            finish_outer, outer_mine,
            [
                ("v", (shard, 3 * width), F32), ("v", (shard, width), F32), ("v", (2, shard), F32), ("v", (6, shard), F32),
                ("v", (1, shard), F32), ("v", (1, 1), F32), ("v", (1, deep // members), F32),
            ],
        )
    else:
        in_order = [h.reshape(3, h.shape[1], -1, TILE).transpose(1, 2, 0, 3).reshape(-1, deep) for h in (hidden, hidden_query)]
        whole = [jnp.concatenate(pair, axis) for pair, axis in (
            (in_order, 0), ((rg_pass, rg_query), 1), ((eg_pass, eg_query), 0), ((bg_pass, bg_query), 0),
        )]
        reduce_total = summed_rows(whole[0], whole[1].T, ROW_FIRST)
        expand_total = summed_rows(low, whole[2], GROUP_FIRST)
        out_total = summed_rows(attended, whole[3], GROUP_FIRST)
        in_total = summed_rows(turned.T, mixed_grad, ROW_FIRST)
        vectors = total_of_all(vectors)
        mine = lax.dynamic_slice_in_dim(vectors[:10], member_index * shard, shard, axis=1)
        expand_shift = lax.dynamic_slice_in_dim(
            vectors[16:].reshape(-1), member_index * (deep // members), deep // members
        )
        gains_grad = mine[:2]
        biases_grad = jnp.concatenate([mine[8:10], mine[2:6]])
        term_grad = mine[6]
        bias_grad = mine[7, :1]
    return (
        scores.T,
        passage_out,
        passage_grad,
        query_grad,
        in_total,
        out_total,
        expand_total,
        expand_shift.reshape(-1),
        reduce_total,
        gains_grad,
        biases_grad,
        term_grad.reshape(-1),
        bias_grad.reshape(-1),
    )


def solution(mesh):
    return jax.shard_map(
        on_device,
        mesh=mesh,
        in_specs=(
            P(("pb", "pa"), None),
            P(("pb", "pa"), None),
            P(("pb", "pa")),
            P(("pb", "pa")),
            P(),
            P(("pb", "pa")),
            P(),
            P(),
            P(),
            P(),
            P(),
            P(),
            P(),
            P(),
            P(),
            P(("pb", "pa"), None),
            P("pb", "pa"),
        ),
        out_specs=(
            P("pb", "pa"),
            P(("pb", "pa"), None),
            P(("pb", "pa"), None),
            P(("pb", "pa"), None),
            P("pa", None),
            P("pa", None),
            P("pa", None),
            P("pa"),
            P("pa", None),
            P(None, "pa"),
            P(None, "pa"),
            P("pa"),
            P(),
        ),
        check_vma=False,
    )
```

```python
from functools import partial

import jax
import jax.numpy as jnp
from jax import lax
from jax.experimental import pallas as pl
from jax.experimental.pallas import tpu as pltpu
from jax.sharding import PartitionSpec as P

HEADS = 12
HEAD = 64
LONG = 512
QLEN = 32
BATCH_PB = 4

NEG = -1e30
HIGH = lax.Precision.HIGHEST
LN_EPS = 1e-12
SCALE = HEAD ** (-0.5)
BLOCK = 256
TILE = 128
F32 = jnp.float32
BF16 = jnp.bfloat16

IN_VMEM = pl.BlockSpec(memory_space=pltpu.VMEM)
IN_SMEM = pl.BlockSpec(memory_space=pltpu.SMEM)
IN_PLACE = pl.BlockSpec(memory_space=pl.ANY)


def shape(dims, dtype):
    return (tuple(dims), dtype)


def dot(left, right):
    return jnp.dot(left, right, preferred_element_type=F32)


def dot_nt(left, right, precision=None):
    return lax.dot_general(
        left, right, (((1,), (1,)), ((), ())), preferred_element_type=F32, precision=precision
    )


def dot_tn(left, right):
    return lax.dot_general(left, right, (((0,), (0,)), ((), ())), preferred_element_type=F32)


def columns(index, width, first=0):
    return pl.ds(pl.multiple_of(first + index * width, TILE), width)


def tiles(count):
    return [slice(first, first + TILE) for first in range(0, count, TILE)]


def row_sum(matrix):
    return jnp.sum(matrix, axis=0, keepdims=True)


def fetch(pairs, sems, first=0):
    copies = [
        pltpu.make_async_copy(source, target, sems.at[first + i]) for i, (source, target) in enumerate(pairs)
    ]
    for copy in copies:
        copy.start()
    return copies


def finish_all(copies):
    for copy in copies:
        copy.wait()


def norm_forward(total):
    centred = total - jnp.mean(total, axis=-1, keepdims=True)
    inverse = lax.rsqrt(jnp.mean(centred * centred, axis=-1, keepdims=True) + LN_EPS)
    return centred * inverse, inverse


def norm_backward(scaled, normed, inverse):
    centred = scaled - jnp.mean(scaled, axis=-1, keepdims=True)
    return inverse * (centred - normed * jnp.mean(scaled * normed, axis=-1, keepdims=True))


def head_lanes(sub):
    lane = lax.broadcasted_iota(jnp.int32, (1, 2 * HEAD), 1)
    return (lane // HEAD) == sub


def same_slot(count, length):
    rows = lax.broadcasted_iota(jnp.int32, (count, count), 0) // length
    cols = lax.broadcasted_iota(jnp.int32, (count, count), 1) // length
    return jnp.where(rows == cols, 0.0, NEG)


def attend(mixed, turned, stats, first, count, width, mask, unroll):
    rows = slice(first, first + count)

    def pair(hp, carry):
        key = mixed[rows, columns(hp, 2 * HEAD, width)]
        value = mixed[rows, columns(hp, 2 * HEAD, 2 * width)].T
        for sub in (0, 1):
            key_here = jnp.where(head_lanes(sub), key, jnp.zeros_like(key))
            logits = dot_nt(key_here, mixed[rows, columns(hp, 2 * HEAD)]) + mask[...]
            highest = jnp.max(logits, axis=0, keepdims=True)
            powers = jnp.exp(logits - highest)
            total = jnp.sum(powers, axis=0, keepdims=True)
            weights = (powers * (1.0 / total)).astype(BF16)
            out_rows = pl.ds(pl.multiple_of((2 * hp + sub) * HEAD, HEAD), HEAD)
            turned[out_rows, rows] = dot(value[sub * HEAD : (sub + 1) * HEAD], weights).astype(BF16)
            stats[2 * hp + sub, :, rows] = highest + jnp.log(total)
        return carry

    lax.fori_loop(0, HEADS // 2, pair, 0, unroll=unroll)


def grow(rows, first, count, expand, cols, expand_bias, hidden, slope):
    for at in range(0, count, min(BLOCK, count)):
        tile = slice(at, at + min(BLOCK, count))
        value = dot(rows[first + at : first + tile.stop, :], expand[:, cols]) + expand_bias[:, cols]
        lower = 0.5 + 0.5 * lax.erf(value * (0.5**0.5))
        hidden[tile, cols] = (value * lower).astype(BF16)
        density = jnp.exp(-0.5 * value * value) * 0.3989422804014327
        slope[tile, cols] = (lower + value * density).astype(BF16)


def by_piece(block, hidden, out):
    shard, piece = lax.div(block, 3), lax.rem(block, 3)
    return hidden.at[:, columns(block, TILE)], out.at[piece, :, columns(shard, TILE)]


def close_forward(total, normed_one, first, count, at, gains, biases, term_weight, term_bias, normed, inverse, pre, passage_out, tell):
    for i, tile in enumerate(tiles(count)):
        base = normed_one[first + tile.start : first + tile.stop, :] * gains[0:1, :] + biases[4:5, :]
        unit, scale = norm_forward(base + total[at + tile.start : at + tile.stop, :] + biases[3:4, :])
        normed[tile, :] = unit
        inverse[tile, :] = scale
        second = unit * gains[1:2, :] + biases[5:6, :]
        pre[tile, :] = jnp.sum(second * term_weight[...], axis=-1, keepdims=True) + term_bias[0]
        if passage_out is not None:
            passage_out[tile, :] = second.astype(BF16)
        tell(i, tile)


def softplus(value):
    return jnp.maximum(value, 0.0) + jnp.log1p(jnp.exp(-jnp.abs(value)))


def sigmoid(value):
    return 1.0 / (1.0 + jnp.exp(-value))


def forward_layer(
    facts, lengths, passages, queries, project_in, project_out, expand, reduce, expand_bias, gains, biases,
    term_weight, term_bias, query_ids, query_batch, score_grad, passage_ids,
    mixed_out, attended_out, turned_out, stats, normed_out, inverse_one, low_out,
    hidden_query_out, slope_query_out, unit_query, scale_query, pre_query,
    hidden_out, slope_out, unit_out, scale_pass, pre_pass, passage_out, known,
    in_here, out_here, expand_here, reduce_here, mixed, attended, turned, normed_one, low, hidden_query, slope_query,
    hidden, slope, unit_pass, second, mask, query_mask, total, sems, out_sems,
):
    n_pass, width = passages.shape
    n_query = queries.shape[0]
    count = n_pass + n_query
    parts = [slice(i * width, (i + 1) * width) for i in range(3)]
    copies = fetch(
        [(project_in.at[:, part], in_here.at[:, part]) for part in parts]
        + [(project_out, out_here), (expand, expand_here), (reduce, reduce_here)],
        sems,
    )
    mask[...] = same_slot(n_pass, lengths[facts[BATCH]])
    query_mask[...] = same_slot(n_query, QLEN)
    for part in range(3):
        copies[part].wait()
        for source, first, rows in ((passages, 0, n_pass), (queries, n_pass, n_query)):
            value = dot(source[...], in_here[:, parts[part]])
            if part != 1:
                value = value + biases[part // 2 : part // 2 + 1, :]
            if part == 0:
                value = value * SCALE
            mixed[first : first + rows, parts[part]] = value.astype(BF16)
    puts = fetch([(mixed, mixed_out)], out_sems)
    attend(mixed, turned, stats, n_pass, n_query, width, query_mask, HEADS // 2)
    attend(mixed, turned, stats, 0, n_pass, width, mask, 3)
    attended[...] = turned[...].T
    puts += fetch([(turned, turned_out), (attended, attended_out)], out_sems, 1)
    copies[3].wait()
    total[...] = dot(attended[...], out_here[...])
    for tile in reversed(tiles(count)):
        source, at = (passages, tile.start) if tile.start < n_pass else (queries, tile.start - n_pass)
        unit, scale = norm_forward(source[at : at + TILE, :].astype(F32) + total[tile, :] + biases[2:3, :])
        normed_one[tile, :] = unit
        inverse_one[tile, :] = scale
        low[tile, :] = (unit * gains[0:1, :] + biases[4:5, :]).astype(BF16)
    puts += fetch([(normed_one, normed_out), (low, low_out)], out_sems, 3)
    copies[4].wait()
    wide = 2 * BLOCK
    per = wide // TILE
    blocks = expand.shape[1] // wide
    at = 5
    for j in range(blocks):
        cols = columns(j, wide)
        grow(low, 0, n_pass, expand_here, cols, expand_bias, hidden, slope)
        grow(low, n_pass, n_query, expand_here, cols, expand_bias, hidden_query, slope_query)
        pairs = [(slope.at[:, cols], slope_out.at[:, cols]), (slope_query.at[:, cols], slope_query_out.at[:, cols])]
        for i in range(j * per, (j + 1) * per):
            pairs += [by_piece(i, hidden, hidden_out), by_piece(i, hidden_query, hidden_query_out)]
        puts += fetch(pairs, out_sems, at)
        at += len(pairs)
    copies[5].wait()
    total[0:n_pass, :] = dot(hidden[...], reduce_here[...])
    total[n_pass:count, :] = dot(hidden_query[...], reduce_here[...])

    def tell(i, tile):
        pairs = [(unit_pass.at[tile, :], unit_out.at[tile, :]), (second.at[tile, :], passage_out.at[tile, :])]
        puts.extend(fetch(pairs, out_sems, at + 2 * i))

    close = (gains, biases, term_weight, term_bias)
    close_forward(total, normed_one, 0, n_pass, 0, *close, unit_pass, scale_pass, pre_pass, second, tell)
    close_forward(
        total, normed_one, n_pass, n_query, n_pass, *close, unit_query, scale_query, pre_query, None, lambda i, tile: None
    )
    known[...] = jnp.zeros_like(known)
    known[0, 0:1, :] = jnp.broadcast_to(softplus(pre_query[...]), (n_query, TILE)).T[0:1, :]
    known[0, 1:2, :] = query_ids[...].astype(F32)
    owner = lax.broadcasted_iota(jnp.int32, (1, n_query), 1) // QLEN
    tags = jnp.zeros((1, n_query), F32)
    for query in range(n_query // QLEN):
        tags = jnp.where(owner == query, query_batch[query].astype(F32), tags)
    known[0, 2:3, :] = tags
    slots, number = score_grad.shape
    row = 3
    for first in range(0, number, TILE):
        size = min(TILE, number - first)
        known[0, row : row + slots, 0:size] = score_grad[:, first : first + size]
        row += slots
    terms = jnp.broadcast_to(softplus(pre_pass[...]), (n_pass, TILE)).T[0:1, :]
    for source in (terms, passage_ids[...].astype(F32)):
        for tile in tiles(n_pass):
            known[0, row : row + 1, :] = source[:, tile]
            row += 1
    finish_all(puts)


def match(facts, lengths, known, score_grad, passage_ids, pre, scores, pass_grad, query_grad):
    members, _, tokens = known.shape
    n_pass = passage_ids.shape[1]
    slots, queries = scores.shape
    per_query = queries // members
    together = min(members, 8)
    slot = lax.broadcasted_iota(jnp.int32, (n_pass, slots), 0) // lengths[facts[BATCH]]
    table = slot == lax.broadcasted_iota(jnp.int32, (n_pass, slots), 1)
    placed = jnp.where(table, softplus(pre[...]), 0.0).astype(BF16)
    who = lax.broadcasted_iota(jnp.int32, (queries, together * tokens), 0)
    token = lax.broadcasted_iota(jnp.int32, (queries, together * tokens), 1) // QLEN
    mine = jnp.broadcast_to(passage_ids[...].astype(F32), (8, n_pass)).T[:, 0:1]

    def several(c, carry):
        scored, placed_grads = carry
        first = c * together
        wide = jnp.concatenate([known[first + i, 0:3, :] for i in range(together)], axis=1)
        matches = jnp.where(mine == wide[1:2, :], 1.0, 0.0).astype(BF16)
        per_token = dot_tn(placed, matches)
        masked = jnp.where(wide[2:3, :] == facts[BATCH_IN_GROUP].astype(F32), 1.0, 0.0)
        weighted = wide[0:1, :] * masked
        spread = jnp.where(who == token + first * per_query, 1.0, 0.0)
        grad = jnp.dot(score_grad[...], spread, preferred_element_type=F32, precision=HIGH)
        placed_grads = placed_grads + dot_nt(matches, (grad * weighted).astype(BF16))
        scored = scored + dot_nt(per_token * weighted, spread, HIGH)
        return scored, placed_grads

    carry = (jnp.zeros(scores.shape, F32), jnp.zeros((n_pass, slots), F32))
    if members == together:
        scored, placed_grads = several(0, carry)
    else:
        scored, placed_grads = lax.fori_loop(0, members // together, several, carry)
    scores[...] = scored
    pass_grad[...] = jnp.sum(jnp.where(table, placed_grads, 0.0), axis=1, keepdims=True)
    me = facts[MEMBER]
    own = known[me, 0:3, :]
    ids = jnp.broadcast_to(own[1:2, :], (TILE, tokens)).T[:, 0:1]
    chunks = -(-queries // TILE)
    who = lax.broadcasted_iota(jnp.int32, (TILE, tokens), 0)
    token = lax.broadcasted_iota(jnp.int32, (TILE, tokens), 1) // QLEN + me * per_query
    spreads = [jnp.where(who + i * TILE == token, 1.0, 0.0) for i in range(chunks)]
    place = lax.broadcasted_iota(jnp.int32, (slots, n_pass), 1)
    slot = lax.broadcasted_iota(jnp.int32, (slots, n_pass), 0)
    per_batch = members // BATCH_PB
    first_batch = facts[BATCH] - facts[BATCH_IN_GROUP]

    def against(n, total):
        batch = lax.div(n, per_batch)
        row = 3
        grad = jnp.zeros((slots, tokens), F32)
        for spread in spreads:
            part = known[n, row : row + slots, :]
            grad = grad + jnp.dot(part, spread, preferred_element_type=F32, precision=HIGH)
            row += slots
        wide = []
        for _ in range(2):
            rows = [known[n, row + i : row + i + 1, :] for i in range(n_pass // TILE)]
            wide.append(jnp.concatenate(rows, axis=1))
            row += n_pass // TILE
        placed = jnp.where(lax.div(place, lengths[first_batch + batch]) == slot, wide[0], 0.0).astype(BF16)
        matches = jnp.where(ids == wide[1], 1.0, 0.0).astype(BF16)
        part = row_sum(grad * dot_nt(placed, matches))
        return total + jnp.where(own[2:3, :] == batch.astype(F32), part, 0.0)

    query_grad[...] = lax.fori_loop(
        0, members, against, jnp.zeros((1, tokens), F32), unroll=min(members, 8)
    )


def backward_rows(
    with_out, first, term_grad, pre, out_grad, normed_two, inverse_two, slope, normed_one, inverse_one, low_one, expand, reduce,
    gains, biases, term_weight,
    reduce_turned, expanded_grad, low_turned, sum_one, branch_grad, sums, expand_shift,
    grad_here, two_here, slope_here, one_here, low_here, expand_here, reduce_here, grown, turned, low_side, sum_here, branch_here,
    sum_two, reduce_out_grad, sems, out_sems, load=True,
):
    count, width = branch_grad.shape
    deep = slope.shape[1]
    wide = 2 * BLOCK
    blocks = deep // wide
    here = pl.ds(first, count)
    early = [
        fetch(
            [(normed_two.at[tile, :], two_here.at[tile, :])]
            + ([(out_grad.at[tile, :], grad_here.at[tile, :])] if with_out else []),
            sems,
            2 * i,
        )
        for i, tile in enumerate(tiles(count))
    ]
    base = 2 * (count // TILE)
    chunks = [
        fetch(
            [(slope.at[:, columns(j, wide)], slope_here.at[:, columns(j, wide)])]
            + ([(reduce.at[columns(j, wide), :], reduce_here.at[columns(j, wide), :])] if load else []),
            sems,
            base + 2 * j,
        )
        for j in range(blocks)
    ]
    base += 2 * blocks
    late = fetch(
        [(low_one.at[here, :], low_here), (normed_one.at[here, :], one_here)] + ([(expand, expand_here)] if load else []), sems, base
    )
    yield
    if not with_out:
        spread = jnp.broadcast_to(term_grad[...], (TILE, count)).T
    totals = [jnp.zeros((1, width), F32) for _ in range(8)]
    for i, tile in enumerate(tiles(count)):
        grad_in = term_grad[tile, :] if with_out else spread[:, 0:1]
        pre_grad = grad_in * sigmoid(pre[tile, :])
        finish_all(early[i])
        unit = two_here[tile, :]
        second_grad = pre_grad * term_weight[...]
        if with_out:
            second_grad = second_grad + grad_here[tile, :].astype(F32)
        back = norm_backward(second_grad * gains[1:2, :], unit, inverse_two[tile, :])
        rounded = back.astype(BF16)
        sum_two[tile, :] = back
        reduce_out_grad[tile, :] = rounded
        totals[1] = totals[1] + row_sum(second_grad * unit)
        totals[3] = totals[3] + row_sum(rounded.astype(F32))
        totals[5] = totals[5] + row_sum(second_grad)
        totals[6] = totals[6] + row_sum(pre_grad * (unit * gains[1:2, :] + biases[5:6, :]))
        totals[7] = totals[7] + row_sum(jnp.broadcast_to(pre_grad, (TILE, width)))
    turned[...] = reduce_out_grad[...].T
    puts = fetch([(turned, reduce_turned)], out_sems)
    for j in range(blocks):
        cols = columns(j, wide)
        finish_all(chunks[j])
        grad = dot_nt(reduce_out_grad[...], reduce_here[cols, :]) * slope_here[:, cols].astype(F32)
        rounded = grad.astype(BF16)
        grown[:, cols] = rounded
        expand_shift[:, cols] = row_sum(rounded.astype(F32))
        puts += fetch([(grown.at[:, cols], expanded_grad.at[:, cols])], out_sems, 1 + j)
    late[0].wait()
    low_side[...] = low_here[...].T
    puts += fetch([(low_side, low_turned)], out_sems, 1 + blocks)
    finish_all(late[1:])
    sum_two[...] = sum_two[...] + dot_nt(grown[...], expand_here[...])
    for i, tile in enumerate(tiles(count)):
        first_grad = sum_two[tile, :]
        unit = one_here[tile, :]
        back = norm_backward(first_grad * gains[0:1, :], unit, inverse_one[first + tile.start : first + tile.stop, :])
        rounded = back.astype(BF16)
        sum_here[tile, :] = back
        branch_here[tile, :] = rounded
        puts += fetch(
            [(sum_here.at[tile, :], sum_one.at[tile, :]), (branch_here.at[tile, :], branch_grad.at[tile, :])], out_sems, 2 + blocks + 2 * i
        )
        totals[0] = totals[0] + row_sum(first_grad * unit)
        totals[2] = totals[2] + row_sum(rounded.astype(F32))
        totals[4] = totals[4] + row_sum(first_grad)
    for i, total in enumerate(totals):
        sums[i : i + 1, :] = total
    return puts


def completed(rows):
    try:
        next(rows)
    except StopIteration as done:
        return done.value


def backward_alone(with_out, first, *refs):
    rows = backward_rows(with_out, first, *refs)
    next(rows)
    finish_all(completed(rows))


def backward_layer(members, facts, lengths, known, score_grad, passage_ids, *refs):
    pre, normed_two, inverse_two, slope, hidden_pass, hidden_query = refs[13:19]
    pass_out, query_out, sent, scores = refs[19:26], refs[26:33], refs[33:36], refs[36]
    pass_own, query_own, (hid_p, hid_q, buffers, sems, out_sems, pass_term, query_term) = refs[37:53], refs[53:67], refs[67:]
    pass_in = (pass_term,) + refs[:13]
    expand_here, reduce_here, grown_p, turned_p, low_p = pass_own[5:10]
    grown_q, turned_q, low_q = query_own[5:8]
    query_in = (query_term, pre, pass_in[2], normed_two, inverse_two, slope) + pass_in[6:]
    pass_rows = backward_rows(True, 0, *pass_in, *pass_out, *pass_own)
    query_rows = backward_rows(
        False, grown_p.shape[0], *query_in, *query_out, *query_own[:5], expand_here, reduce_here, *query_own[5:], load=False
    )
    next(pass_rows)
    next(query_rows)
    copies = fetch([(hidden_pass, hid_p), (hidden_query, hid_q)], sems)
    match(facts, lengths, known, score_grad, passage_ids, pass_in[1], scores, pass_term, query_term)
    puts = completed(pass_rows) + completed(query_rows)
    finish_all(copies)
    core = 1 - facts[0]
    spread = grown_p.shape[1]
    width = low_p.shape[0]
    third = spread // 6
    half = pl.ds(pl.multiple_of(core * (width // 2), TILE), width // 2)
    for piece in range(3):

        def emit(leaf, side, row, part):
            buffers[piece, leaf, side, row : row + part.shape[0], :] = part

        def tell(rows, place):
            puts.extend(
                fetch([(buffers.at[piece, :, :, rows, :], sent[piece].at[:, :, rows, :])], out_sems, 2 * piece + place)
            )

        cols = pl.ds(pl.multiple_of(core * (spread // 2) + piece * third, TILE), third)
        inner_leaves(
            members, low_p, low_q, grown_p.at[:, cols], grown_q.at[:, cols], turned_p.at[half, :], turned_q.at[half, :],
            hid_p.at[piece], hid_q.at[piece], emit, tell,
        )
    finish_all(puts)


def attend_backward(mixed, attended_grad, stats, inner, mixed_grad, logit_grads, first, count, width, mask, tell):
    rows = slice(first, first + count)
    step = min(BLOCK, count)

    def pair(hp, carry):
        query = mixed[rows, columns(hp, 2 * HEAD)]
        grad = attended_grad[rows, columns(hp, 2 * HEAD)]
        query_grad = jnp.zeros((count, 2 * HEAD), F32)
        kept = []
        for sub in (0, 1):
            lanes = head_lanes(sub)
            total = stats[2 * hp + sub, :, rows]
            level = inner[2 * hp + sub, :, rows]
            for at in range(0, count, step):
                tile = slice(at, at + step)
                here = slice(first + at, first + at + step)
                key = mixed[here, columns(hp, 2 * HEAD, width)]
                value = mixed[here, columns(hp, 2 * HEAD, 2 * width)]
                key_here = jnp.where(lanes, key, jnp.zeros_like(key))
                value_here = jnp.where(lanes, value, jnp.zeros_like(value))
                weights = jnp.exp(dot_nt(key_here, query) + (mask[tile, :] - total))
                logit_grad = (weights * (dot_nt(value_here, grad) - level)).astype(BF16)
                logit_grads[sub, tile, 0:count] = logit_grad
                kept.append((dot(logit_grad, query), dot(weights.astype(BF16), grad)))
        for i, at in enumerate(range(0, count, step)):
            here = slice(first + at, first + at + step)
            for part in (0, 1):
                mixed_grad[here, columns(hp, 2 * HEAD, (part + 1) * width)] = jnp.where(
                    head_lanes(0), kept[i][part], kept[i + count // step][part]
                ).astype(BF16)
        for sub in (0, 1):
            key = mixed[rows, columns(hp, 2 * HEAD, width)]
            key_here = jnp.where(head_lanes(sub), key, jnp.zeros_like(key))
            query_grad = query_grad + dot_tn(logit_grads[sub, 0:count, 0:count], key_here)
        mixed_grad[rows, columns(hp, 2 * HEAD)] = (query_grad * SCALE).astype(BF16)
        tell(hp)
        return carry

    lax.fori_loop(0, HEADS // 2, pair, 0)


def backward_attention(
    members, sides, lengths, passages, queries, pass_grad, query_grad, project_out, mixed, attended, stats,
    attended_turned, project_in, pass_sum, query_sum, sums_pass, sums_query, shift_pass, shift_query,
    grad_out, turned_out, vectors, pass_out, query_out, *rest,
):
    sent = rest[0] if members else None
    (
        out_here, pass_here, query_here, mixed_here, attended_here, mixed_grad, turned,
        attended_grad, inner, logit_grads, mask, query_mask, across_here, in_here, pass_sum_here, query_sum_here, buffers,
        sems, out_sems,
    ) = rest[-19:]
    n_pass, width = passages.shape
    n_query = queries.shape[0]
    count = n_pass + n_query
    copies = fetch(
        [
            (project_out, out_here), (pass_grad, pass_here), (query_grad, query_here), (attended, attended_here),
            (mixed, mixed_here), (attended_turned, across_here), (project_in, in_here), (pass_sum, pass_sum_here),
            (query_sum, query_sum_here),
        ],
        sems,
    )
    query_mask[...] = same_slot(n_query, QLEN)
    mask[...] = same_slot(n_pass, lengths[sides[BATCH]])
    turned[:, 0:n_pass] = passages[...].T
    turned[:, n_pass:count] = queries[...].T
    puts = fetch([(turned, turned_out)], out_sems)
    finish_all(copies[:3])
    attended_grad[0:n_pass, :] = dot_nt(pass_here[...], out_here[...]).astype(BF16)
    attended_grad[n_pass:count, :] = dot_nt(query_here[...], out_here[...]).astype(BF16)
    heads = 16
    owner = lax.broadcasted_iota(jnp.int32, (heads, width), 1) // HEAD
    spread = jnp.where(owner == lax.broadcasted_iota(jnp.int32, (heads, width), 0), 1.0, 0.0)
    copies[3].wait()
    for tile in tiles(count):
        product = attended_grad[tile, :].astype(F32) * attended_here[tile, :].astype(F32)
        levels = dot_nt(spread, product, HIGH)
        for head in range(HEADS):
            inner[head, :, tile] = levels[head : head + 1, :]
    copies[4].wait()
    nothing = lambda hp: None
    attend_backward(mixed_here, attended_grad, stats, inner, mixed_grad, logit_grads, n_pass, n_query, width, query_mask, nothing)
    attend_backward(mixed_here, attended_grad, stats, inner, mixed_grad, logit_grads, 0, n_pass, width, mask, nothing)
    puts += fetch([(mixed_grad, grad_out)], out_sems, 1)
    shifts = [row_sum(mixed_grad[:, first : first + width].astype(F32)) for first in (0, 2 * width)]
    whole = jnp.concatenate([sums_pass[...] + sums_query[...], *shifts, jnp.zeros((6, width), F32)])
    deep_shift = shift_pass[...] + shift_query[...]
    if members:
        shard = width // members
        lane = lax.broadcasted_iota(jnp.int32, (width, TILE), 1)
        source = lax.broadcasted_iota(jnp.int32, (width, TILE), 0)
        row = lax.broadcasted_iota(jnp.int32, (16, TILE), 0)
        for leaf in range(members):
            chosen = jnp.where((source == lane + leaf * shard) & (lane < shard), 1.0, 0.0)
            block = jnp.dot(whole, chosen, preferred_element_type=F32, precision=HIGH)
            for i in range(3):
                part = deep_shift[:, (3 * leaf + i) * TILE : (3 * leaf + i + 1) * TILE]
                block = jnp.where(row == 10 + i, part, block)
            vectors[leaf] = block
        finish_all(copies[5:6])
        core = 1 - sides[0]
        wide = width // 2
        for piece in range(3):

            def emit(leaf, side, row, part):
                buffers[piece, leaf, side, row : row + part.shape[0], :] = part

            narrow = pl.ds(pl.multiple_of(core * wide + piece * TILE, TILE), TILE)
            outer_leaves(
                members, turned, mixed_grad.at[:, pl.ds(pl.multiple_of(core * 3 * wide + piece * wide, TILE), wide)],
                across_here, pass_here.at[:, narrow], query_here.at[:, narrow], emit,
            )
            vector_leaves(members, piece, core, vectors, buffers.shape[3] - 8, emit)
            puts += fetch([(buffers.at[piece], sent.at[piece])], out_sems, 2 + piece)
        late = copies[6:]
    else:
        vectors[0:16, :] = whole
        for i in range(deep_shift.shape[1] // width):
            vectors[16 + i : 17 + i, :] = deep_shift[:, i * width : (i + 1) * width]
        late = copies[5:]
    finish_all(late)
    for first in range(0, width, BLOCK):
        cols = slice(first, first + BLOCK)
        weight = in_here[cols, :]
        pass_out[:, cols] = (dot_nt(mixed_grad[0:n_pass, :], weight) + pass_sum_here[:, cols]).astype(BF16)
        query_out[:, cols] = (dot_nt(mixed_grad[n_pass:count, :], weight) + query_sum_here[:, cols]).astype(BF16)
    finish_all(puts)


def inner_leaves(members, low_p, low_q, grad_p, grad_q, turn_p, turn_q, hid_p, hid_q, emit, tell):
    width = low_p.shape[0]
    shard = width // members
    for first in range(0, width, width // 2):
        rows = slice(first, first + width // 2)
        part = dot(low_p[rows, :], grad_p[...]) + dot(low_q[rows, :], grad_q[...])
        for at in range(0, width // 2, shard // 2):
            leaf, side = divmod((first + at) // (shard // 2), 2)
            for block in range(part.shape[1] // TILE):
                emit(leaf, side, block * (shard // 2), part[at : at + shard // 2, block * TILE : (block + 1) * TILE])
    base = (shard // 2) * (grad_p.shape[1] // TILE)
    tell(slice(0, base), 0)
    for leaf in range(0, members, 4):
        span = slice(leaf * TILE, (leaf + 4) * TILE)
        part = dot(turn_p[...], hid_p[:, span]) + dot(turn_q[...], hid_q[:, span])
        for i in range(4):
            for side in (0, 1):
                emit(leaf + i, side, base, part[side * (width // 4) : (side + 1) * (width // 4), i * TILE : (i + 1) * TILE])
    tell(slice(base, base + width // 4), 1)


def outer_leaves(members, turned, grad, attended, branch_p, branch_q, emit):
    width = turned.shape[0]
    n_pass = branch_p.shape[0]
    shard = width // members
    for first in range(0, width, width // 2):
        rows = slice(first, first + width // 2)
        parts = [
            dot(turned[rows, :], grad[...]),
            dot(attended[rows, 0:n_pass], branch_p[...]) + dot(attended[rows, n_pass:], branch_q[...]),
        ]
        for at in range(0, width // 2, shard // 2):
            leaf, side = divmod((first + at) // (shard // 2), 2)
            block = 0
            for part in parts:
                for lane in range(0, part.shape[1], TILE):
                    emit(leaf, side, block * (shard // 2), part[at : at + shard // 2, lane : lane + TILE])
                    block += 1


def side_of(bit_at, mine, leaf, side):
    index = 2 * leaf + side
    high, bit, rest = index >> (bit_at + 1), (index >> bit_at) & 1, index & ((1 << bit_at) - 1)
    return jnp.where(mine == bit, 0, 1), (high << bit_at) + rest


def inner_kept(
    members, piece, bit_at, sides, low_pass, low_query, grad_pass, grad_query, reduce_pass, reduce_query, hidden_pass, hidden_query,
    received, leaves, stays,
    low_p, low_q, grad_p, grad_q, turn_p, turn_q, hid_p, hid_q, came, both, sems, out_sems,
):
    width = low_pass.shape[0]
    spread = grad_pass.shape[1]
    third = spread // 6
    cols = pl.ds(pl.multiple_of(sides[0] * (spread // 2) + piece * third, TILE), third)
    half = pl.ds(pl.multiple_of(sides[0] * (width // 2), TILE), width // 2)
    base = (width // members // 2) * (third // TILE)
    spans = [slice(0, base), slice(base, base + width // 4)]
    early = fetch(
        [
            (low_pass, low_p), (low_query, low_q), (grad_pass.at[:, cols], grad_p), (grad_query.at[:, cols], grad_q),
            (received.at[:, :, spans[0], :], came.at[:, :, spans[0], :]),
        ],
        sems,
    )
    late = fetch(
        [
            (reduce_pass.at[half, :], turn_p), (reduce_query.at[half, :], turn_q),
            (hidden_pass.at[piece], hid_p), (hidden_query.at[piece], hid_q),
            (received.at[:, :, spans[1], :], came.at[:, :, spans[1], :]),
        ],
        sems, 5,
    )
    puts = []

    def emit(leaf, side, row, part):
        rows = slice(row, row + part.shape[0])
        both[*side_of(bit_at, sides[1 + piece], leaf, side), rows, :] = part + came[leaf, side, rows, :]

    def tell(rows, place):
        pairs = [(both.at[1, :, rows, :], leaves.at[:, rows, :]), (both.at[0, :, rows, :], stays.at[:, rows, :])]
        puts.extend(fetch(pairs, out_sems, 2 * place))
        if place == 0:
            finish_all(late)

    finish_all(early)
    inner_leaves(members, low_p, low_q, grad_p, grad_q, turn_p, turn_q, hid_p, hid_q, emit, tell)
    finish_all(puts)


def outer_kept(
    members, places, sides, turned, mixed_grad, attended, branch_pass, branch_query, vectors, received, *refs
):
    leaves, stays = refs[0:6:2], refs[1:6:2]
    rows_here, grad, attended_here, branch_p, branch_q, came, both, sems, out_sems = refs[6:]
    width = turned.shape[0]
    wide = width // 2
    cols = pl.ds(pl.multiple_of(sides[0] * 3 * wide, TILE), 3 * wide)
    narrow = pl.ds(pl.multiple_of(sides[0] * wide, TILE), wide)
    copies = fetch(
        [
            (turned, rows_here), (mixed_grad.at[:, cols], grad), (attended, attended_here),
            (branch_pass.at[:, narrow], branch_p), (branch_query.at[:, narrow], branch_q),
        ]
        + [(received.at[piece], came.at[piece]) for piece in range(3)],
        sems,
    )
    finish_all(copies[:5])
    puts = []
    for piece in range(3):
        copies[5 + piece].wait()

        def emit(leaf, side, row, part):
            rows = slice(row, row + part.shape[0])
            both[piece, *side_of(places[piece], sides[1 + piece], leaf, side), rows, :] = part + came[piece, leaf, side, rows, :]

        outer_leaves(
            members, rows_here, grad.at[:, piece * wide : (piece + 1) * wide], attended_here,
            branch_p.at[:, piece * TILE : (piece + 1) * TILE], branch_q.at[:, piece * TILE : (piece + 1) * TILE], emit,
        )
        vector_leaves(members, piece, sides[0], vectors, both.shape[3] - 8, emit)
        puts += fetch([(both.at[piece, 1], leaves[piece]), (both.at[piece, 0], stays[piece])], out_sems, 2 * piece)
    finish_all(puts)


def vector_leaves(members, piece, core, vectors, row, emit):
    for leaf in range(members):
        for side in (0, 1):
            if piece == 0:
                part = jnp.where(core == 0, vectors[leaf, 8 * side : 8 * side + 8, :], 0.0)
            else:
                part = jnp.zeros((8, TILE), F32)
            emit(leaf, side, row, part)


def finish_inner(sides, mine, near, other, beyond, expand, reduce):
    rows, wide = expand.shape
    half = rows // 2
    blocks = wide // 6 // TILE
    deep = reduce.shape[1] // 2
    for far, pair in enumerate(((mine, near), (other, beyond))):
        core = jnp.bitwise_xor(sides[0], far)
        for piece in range(3):
            for there, source in enumerate(pair):
                side = pl.multiple_of(jnp.bitwise_xor(sides[1], there) * half, 8)
                for block in range(blocks):
                    at = core * (wide // 2) + (piece * blocks + block) * TILE
                    expand[pl.ds(side, half), pl.ds(pl.multiple_of(at, TILE), TILE)] = source[
                        piece, block * half : (block + 1) * half, :
                    ]
            parts = [source[piece, blocks * half :, :] for source in pair]
            low = jnp.where(sides[1] == 0, parts[0], parts[1])
            high = jnp.where(sides[1] == 0, parts[1], parts[0])
            reduce[piece * TILE : (piece + 1) * TILE, pl.ds(pl.multiple_of(core * deep, TILE), deep)] = (
                jnp.concatenate([low, high]).T
            )


def finish_outer(sides, mine, near, other, beyond, project_in, project_out, gains, biases, term_weight, term_bias, expand_bias):
    rows, wide = project_in.shape
    half = rows // 2
    for far, pair in enumerate(((mine, near), (other, beyond))):
        core = jnp.bitwise_xor(sides[0], far)
        for there, source in enumerate(pair):
            side = pl.multiple_of(jnp.bitwise_xor(sides[1], there) * half, 8)
            for piece in range(3):
                for block in range(4):
                    part = source[piece, block * half : (block + 1) * half, :]
                    if block < 3:
                        at = core * (wide // 2) + (piece * 3 + block) * TILE
                        project_in[pl.ds(side, half), pl.ds(pl.multiple_of(at, TILE), TILE)] = part
                    else:
                        at = core * (wide // 6) + piece * TILE
                        project_out[pl.ds(side, half), pl.ds(pl.multiple_of(at, TILE), TILE)] = part
    at = mine.shape[1] - 8
    parts = [
        jnp.where(sides[0] == 0, a[0, at:, :], b[0, at:, :]) for a, b in ((mine, other), (near, beyond))
    ]
    low = jnp.where(sides[1] == 0, parts[0], parts[1])
    high = jnp.where(sides[1] == 0, parts[1], parts[0])
    gains[...] = low[0:2, :rows]
    biases[0:2, :] = high[0:2, :rows]
    biases[2:6, :] = low[2:6, :rows]
    term_weight[...] = low[6:7, :rows]
    term_bias[...] = low[7:8, 0:1]
    for i in range(expand_bias.shape[1] // TILE):
        expand_bias[:, i * TILE : (i + 1) * TILE] = high[2 + i : 3 + i, :]


def finish_both(sides, *refs):
    finish_inner(sides, *refs[:4], *refs[8:10])
    finish_outer(sides, *refs[4:8], *refs[10:])


def run(kernel, outs, kinds, scratch, args, after=(), aliases=None, limit=58):
    specs = {"s": IN_SMEM, "v": IN_VMEM, "h": IN_PLACE, "a": IN_PLACE}
    shapes = [
        pltpu.HBM(dims, dtype) if kind == "h" else jax.ShapeDtypeStruct(dims, dtype) for kind, dims, dtype in outs
    ]
    given = [
        pltpu.with_memory_space_constraint(a, pltpu.HBM) if kind == "h" else a for a, kind in zip(args, kinds)
    ]
    many = len(outs) > 1
    known = len(args)

    def body(*refs):
        kernel(*refs[:known], *refs[known + len(after) :])

    return pl.pallas_call(
        body,
        out_shape=shapes if many else shapes[0],
        in_specs=[specs[kind] for kind in kinds] + [IN_PLACE] * len(after),
        out_specs=[specs[o[0]] for o in outs] if many else specs[outs[0][0]],
        scratch_shapes=scratch,
        input_output_aliases=aliases or {},
        compiler_params=pltpu.CompilerParams(vmem_limit_bytes=limit << 20),

    )(*given, *[pltpu.with_memory_space_constraint(a, pltpu.HBM) for a in after])


def contract_rows(left, right):
    return lax.dot_general(
        left, right, (((0,), (0,)), ((), ())), preferred_element_type=F32
    )


GROUP_FIRST = (("pb", 2), ("pa", 1))
ROW_FIRST = (("pa", 1), ("pb", 2))


def swap(value, axis, distance):
    return lax.ppermute(
        value, axis, [(i, i ^ distance) for i in range(lax.axis_size(axis))]
    )


def bit(axis, distance):
    return (lax.axis_index(axis) >> (distance.bit_length() - 1)) & 1


def pick(value, index, dim):
    return lax.dynamic_index_in_dim(value, index, dim, keepdims=False)


def group_gather(mine):
    distance = 1
    while distance < lax.axis_size("pa"):
        other = swap(mine, "pa", distance)
        mine = jnp.where(
            bit("pa", distance) == 0, jnp.concatenate([mine, other]), jnp.concatenate([other, mine])
        )
        distance *= 2
    return mine


def steps_of(order):
    steps = [(axis, distance) for axis, distance in order]
    distance = 2
    while distance < lax.axis_size("pa"):
        steps.append(("pa", distance))
        distance *= 2
    return steps


def tree_sum(send, keep, order):
    names = []
    distance = lax.axis_size("pa") // 2
    while distance:
        names.append(("pa", distance))
        distance //= 2
    names.append(("pb", 2))
    received = swap(send, "pb", 1)
    for axis, distance in steps_of(order):
        dim = names.index((axis, distance))
        names.pop(dim)
        mine = bit(axis, distance)
        send = pick(keep, 1 - mine, dim) + pick(received, 1 - mine, dim)
        keep = pick(keep, mine, dim) + pick(received, mine, dim)
        received = swap(send, axis, distance)
    mine = keep + received
    other = swap(mine, "pb", 2)
    high = bit("pb", 2)
    return jnp.where(high == 0, jnp.stack([mine, other]), jnp.stack([other, mine]))


def cut(matrix):
    bits = lax.axis_size("pa").bit_length() - 1
    rows = matrix.shape[0] >> (bits + 1)
    return matrix.reshape((2,) * (bits + 1) + (rows, matrix.shape[1]))


def summed_rows(left, right, order):
    core = bit("pb", 1)
    half = right.shape[1] // 2
    parts = [
        cut(contract_rows(left, lax.dynamic_slice_in_dim(right, side * half, half, axis=1)))
        for side in (1 - core, core)
    ]
    mine = tree_sum(parts[0], parts[1], order)
    mine = mine.reshape(-1, half)
    other = swap(mine, "pb", 1)
    return jnp.where(
        core == 0, jnp.concatenate([mine, other], 1), jnp.concatenate([other, mine], 1)
    )


def total_of_all(value):
    distance = 1
    while distance < lax.axis_size("pb"):
        value = value + swap(value, "pb", distance)
        distance *= 2
    distance = 1
    while distance < lax.axis_size("pa"):
        value = value + swap(value, "pa", distance)
        distance *= 2
    return value


BATCH_IN_GROUP, BATCH, MEMBER = 5, 6, 7
LEAF_BITS = (("pa", 4), ("pa", 2), ("pa", 1), ("pb", 2))
PIECE_ORDERS = (
    (("pb", 2), ("pa", 1), ("pa", 2), ("pa", 4)),
    (("pa", 1), ("pa", 2), ("pb", 2), ("pa", 4)),
    (("pa", 2), ("pb", 2), ("pa", 1), ("pa", 4)),
)
PLACES = tuple(len(LEAF_BITS) - 1 - LEAF_BITS.index(order[0]) for order in PIECE_ORDERS)


def begun(parts):
    held = []
    for (leaving, staying), order in zip(parts, PIECE_ORDERS):
        rest = tuple(b for b in LEAF_BITS if b != order[0])
        held.append(([(staying, rest), (swap(leaving, *order[0]), rest)], (order[0],)))
    return held


def chosen(names, settled, current=None):
    return tuple(1 if name == current else 0 if name in settled else None for name in names)


def part_of(array, names, settled, current, rows):
    wants = chosen(names, settled, current)
    starts = [0 if want is None else bit(*name) ^ want for name, want in zip(names, wants)]
    sizes = [2 if want is None else 1 for want in wants]
    part = lax.dynamic_slice(array.reshape((2,) * len(names) + (rows, TILE)), starts + [0, 0], sizes + [rows, TILE])
    return part.reshape((2,) * wants.count(None) + (rows, TILE))


def onward(held, step, sent):
    moved = []
    for (terms, settled), order, leaving in zip(held, PIECE_ORDERS, sent):
        left = tuple(b for b in LEAF_BITS if b not in settled and b != order[step])
        moved.append((terms + [(swap(leaving, *order[step]), left)], settled + (order[step],)))
    return moved


def advance(held, step, rows):
    sent = []
    for (terms, settled), order in zip(held, PIECE_ORDERS):
        sent.append(sum(part_of(array, names, settled, order[step], rows) for array, names in terms))
    return onward(held, step, sent)


def fold(plans, through, joined, facts, *refs):
    count = sum(len(plan) for plan in plans)
    terms = refs[:count]
    outs = refs[count + through : count + through + (1 if joined else len(plans))]
    scratch = refs[count + through + len(outs) + through :]
    sems, out_sems = scratch[-2:]
    pairs = []
    at = 0
    for plan in plans:
        for wants in plan:
            index = tuple(
                slice(None) if want is None else jnp.bitwise_xor(facts[len(LEAF_BITS) - LEAF_BITS.index(name)], want) for name, want in wants
            )
            pairs.append((terms[at].at[index], scratch[at]))
            at += 1
    copies = fetch(pairs, sems)
    puts = []
    at = 0
    for i, plan in enumerate(plans):
        finish_all(copies[at : at + len(plan)])
        total = scratch[at][...]
        for k in range(1, len(plan)):
            total = total + scratch[at + k][...]
        scratch[at][...] = total
        puts += fetch([(scratch[at], outs[0].at[i] if joined else outs[i])], out_sems, i)
        at += len(plan)
    finish_all(puts)


def fold_by_kernel(facts, held, step, rows, through=(), after=(), joined=False):
    plans = []
    args = []
    kinds = ""
    scratch = []
    outs = []
    for (terms, settled), order in zip(held, PIECE_ORDERS):
        plan = []
        for array, names in terms:
            wants = chosen(names, settled, order[step])
            plan.append(tuple(zip(names, wants)))
            args.append(array.reshape((2,) * len(names) + (rows, TILE)))
            kinds += "a" if plan[1:] else "h"
            dims = (2,) * wants.count(None) + (rows, TILE)
            scratch.append(pltpu.VMEM(dims, F32))
        plans.append(plan)
        outs.append(("h", dims, F32))
    if joined:
        outs = [("h", (len(plans), rows, TILE), F32)]
    done = run(
        partial(fold, plans, len(through), joined),
        outs + [("h", a.shape, a.dtype) for a in through],
        "s" + kinds + "h" * len(through),
        scratch + [pltpu.SemaphoreType.DMA((len(args),)), pltpu.SemaphoreType.DMA((len(plans),))],
        (facts, *args, *through),
        after,
        {1 + len(args) + i: len(outs) + i for i in range(len(through))},
        12,
    )
    return done if len(outs) + len(through) > 1 else [done]


def advance_by_kernel(facts, held, step, rows, through=(), after=()):
    done = fold_by_kernel(facts, held, step, rows, through, after)
    return onward(held, step, done[:3]), done[3:]


def last_exchange(facts, held, rows, through=()):
    step = len(LEAF_BITS) - 1
    name = PIECE_ORDERS[0][step]
    sent, *through = fold_by_kernel(facts, held, step, rows, through, joined=True)
    came = swap(sent, *name)
    total = jnp.stack(
        [sum(part_of(array, names, settled + (name,), None, rows) for array, names in terms) for terms, settled in held]
    )
    return total + came, through


def on_device(
    passages, queries, passage_ids, query_ids, batch_length, query_batch, project_in, project_out, expand_weight,
    expand_bias, reduce_weight, norm_gains, biases, term_weight, term_bias, out_grad, score_grad,
):
    members = lax.axis_size("pa")
    member_index = lax.axis_index("pa")
    local_batch = member_index // (members // BATCH_PB)
    facts = jnp.stack(
        [
            bit("pb", 1), *(bit(*name) for name in reversed(LEAF_BITS)), local_batch,
            lax.axis_index("pb") * BATCH_PB + local_batch, member_index,
        ]
    )
    n_pass, width = passages.shape
    n_query = queries.shape[0]
    count = n_pass + n_query
    deep = expand_weight.shape[1]
    slots = score_grad.shape[1]
    bias_row = expand_bias[None]
    term_row = term_weight

    blocks = deep // (2 * BLOCK)
    by_three = (3, n_pass, deep // 3)
    weights = [pltpu.VMEM(expand_weight.shape, BF16), pltpu.VMEM(reduce_weight.shape, BF16)]

    def vmem(*dims, dtype=BF16):
        return pltpu.VMEM(dims, dtype)

    def sems(number):
        return pltpu.SemaphoreType.DMA((number,))

    known_rows = 3 + slots * (-(-score_grad.shape[0] // TILE)) + 2 * (n_pass // TILE)
    (
        mixed, attended, attended_turned, stats, normed_one, inverse_one, low,
        hidden_query, slope_query, unit_query, scale_query, pre_query,
        hidden, slope, unit_pass, scale_pass, pre_pass, passage_out, known,
    ) = run(
        forward_layer,
        [
            ("h", (count, 3 * width), BF16), ("h", (count, width), BF16),
            ("h", (width, count), BF16), ("v", (HEADS, 1, count), F32), ("h", (count, width), F32),
            ("v", (count, 1), F32), ("h", (count, width), BF16), ("h", (3, n_query, deep // 3), BF16),
            ("h", (n_query, deep), BF16), ("v", (n_query, width), F32), ("v", (n_query, 1), F32), ("v", (n_query, 1), F32),
            ("h", by_three, BF16), ("h", (n_pass, deep), BF16), ("h", (n_pass, width), F32),
            ("v", (n_pass, 1), F32), ("v", (n_pass, 1), F32), ("h", (n_pass, width), BF16),
            ("v", (1, known_rows, TILE), F32),
        ],
        "ssvvhhhhvvvvsvsvv",
        [
            vmem(*project_in.shape), vmem(*project_out.shape), *weights, vmem(count, 3 * width), vmem(count, width),
            vmem(width, count), vmem(count, width, dtype=F32), vmem(count, width), vmem(n_query, deep), vmem(n_query, deep),
            vmem(n_pass, deep), vmem(n_pass, deep), vmem(n_pass, width, dtype=F32), vmem(n_pass, width),
            vmem(n_pass, n_pass, dtype=F32), vmem(n_query, n_query, dtype=F32), vmem(count, width, dtype=F32),
            sems(6), sems(5 + 2 * blocks + 2 * (deep // TILE) + 2 * (n_pass // TILE)),
        ],
        (facts, batch_length, passages, queries, project_in, project_out, expand_weight, reduce_weight, bias_row, norm_gains,
         biases, term_row, term_bias, query_ids[None], query_batch, score_grad.T, passage_ids[None]),
    )
    known = group_gather(known)
    def back_outs(rows):
        return [
            ("h", (width, rows), BF16), ("h", (rows, deep), BF16), ("h", (width, rows), BF16),
            ("h", (rows, width), F32), ("h", (rows, width), BF16), ("v", (8, width), F32), ("v", (1, deep), F32),
        ]

    back_kinds = "vvhhvhhvhhhvvv"

    def back_scratch(rows):
        return [
            vmem(rows, width), vmem(rows, width, dtype=F32), vmem(rows, deep), vmem(rows, width, dtype=F32), vmem(rows, width),
            *weights, vmem(rows, deep), vmem(width, rows), vmem(width, rows), vmem(rows, width, dtype=F32), vmem(rows, width),
            vmem(rows, width, dtype=F32), vmem(rows, width),
            sems(3 + 2 * blocks + 2 * (rows // TILE)), sems(2 + blocks + 2 * (rows // TILE)),
        ]

    def back_args(term_grad, pre, unit, scale, slope_here):
        return (term_grad, pre, out_grad, unit, scale, slope_here, normed_one, inverse_one, low,
                expand_weight, reduce_weight, norm_gains, biases, term_row)

    fits = deep // members == 3 * TILE
    shard = width // members
    leaf_rows = (deep // 6 // TILE * (shard // 2) + width // 4, 4 * (shard // 2) + 8)
    if fits:
        dims = (members, 2, leaf_rows[0], TILE)
        third = deep // 6
        pass_scratch, query_scratch = back_scratch(n_pass), back_scratch(n_query)
        (
            rg_pass, eg_pass, low_pass, one_pass, bg_pass, sums_pass, shift_pass,
            rg_query, eg_query, low_query, one_query, bg_query, sums_query, shift_query, *sent, scores
        ) = run(
            partial(backward_layer, members),
            back_outs(n_pass) + back_outs(n_query) + [("h", dims, F32)] * 3 + [("v", score_grad.shape[::-1], F32)],
            "ssvvv" + back_kinds[1:] + "vhvhhh",
            pass_scratch + query_scratch[:5] + query_scratch[7:]
            + [vmem(*by_three), vmem(3, n_query, deep // 3), vmem(3, *dims, dtype=F32), sems(2), sems(6), vmem(n_pass, 1, dtype=F32),
               vmem(1, n_query, dtype=F32)],
            (facts, batch_length, known, score_grad.T, passage_ids[None])
            + back_args(None, pre_pass, unit_pass, scale_pass, slope)[1:]
            + (pre_query, unit_query, scale_query, slope_query, hidden, hidden_query),
        )
        came = [swap(part, "pb", 1) for part in sent]
        parts = []
        for piece, order in enumerate(PIECE_ORDERS):
            half = (leaf_rows[0], TILE)
            parts.append(
                run(
                    partial(inner_kept, members, piece, PLACES[piece]),
                    [("h", (members,) + half, F32)] * 2,
                    "s" + "h" * 8 + "a",
                    [
                        vmem(width, n_pass), vmem(width, n_query), vmem(n_pass, third), vmem(n_query, third),
                        vmem(width // 2, n_pass), vmem(width // 2, n_query), vmem(n_pass, deep // 3), vmem(n_query, deep // 3),
                        vmem(*dims, dtype=F32), vmem(2, members, *half, dtype=F32), sems(10), sems(4),
                    ],
                    (facts, low_pass, low_query, eg_pass, eg_query, rg_pass, rg_query, hidden,
                     hidden_query, came[piece]),
                    limit=18,
                )
            )
        inner = begun(parts)
        pins = tuple(leaving for leaving, _ in parts)
        extra = [("v", (members, 16, TILE), F32)]
        last = [("h", (3, members, 2, leaf_rows[1], TILE), F32)]
    else:
        scores, pass_term_grad, query_term_grad = run(
            match,
            [("v", score_grad.shape[::-1], F32), ("v", (n_pass, 1), F32), ("v", (1, n_query), F32)],
            "ssvvvv",
            [],
            (facts, batch_length, known, score_grad.T, passage_ids[None], pre_pass),
        )
        rg_pass, eg_pass, low_pass, one_pass, bg_pass, sums_pass, shift_pass = run(
            partial(backward_alone, True, 0), back_outs(n_pass), back_kinds, back_scratch(n_pass),
            back_args(pass_term_grad, pre_pass, unit_pass, scale_pass, slope),
        )
        rg_query, eg_query, low_query, one_query, bg_query, sums_query, shift_query = run(
            partial(backward_alone, False, n_pass), back_outs(n_query), back_kinds, back_scratch(n_query),
            back_args(query_term_grad, pre_query, unit_query, scale_query, slope_query),
        )
        pins = ()
        extra = [("v", (16 + deep // width, width), F32)]
        last = []
    mixed_grad, turned, vectors, passage_grad, query_grad, *sent = run(
        partial(backward_attention, members if fits else 0),
        [("h", (count, 3 * width), BF16), ("h", (width, count), BF16)]
        + extra
        + [("v", (n_pass, width), BF16), ("v", (n_query, width), BF16)]
        + last,
        "ssvvhhhhhv" + "hhhh" + "vvvv",
        [
            vmem(*project_out.shape), vmem(n_pass, width), vmem(n_query, width), vmem(count, 3 * width), vmem(count, width),
            vmem(count, 3 * width), vmem(width, count), vmem(count, width), vmem(HEADS, 1, count, dtype=F32),
            vmem(2, n_pass, n_pass), vmem(n_pass, n_pass, dtype=F32), vmem(n_query, n_query, dtype=F32),
            vmem(width, count), vmem(*project_in.shape), vmem(n_pass, width, dtype=F32), vmem(n_query, width, dtype=F32),
            vmem(*(last[0][1] if fits else (8, TILE)), dtype=F32), sems(9), sems(5),
        ],
        (facts, batch_length, passages, queries, bg_pass, bg_query, project_out, mixed, attended, stats, attended_turned, project_in,
         one_pass, one_query, sums_pass, sums_query, shift_pass, shift_query),
        pins,
    )
    if fits:
        inner, sent = advance_by_kernel(facts, inner, 1, leaf_rows[0], tuple(sent))
        half = (leaf_rows[1], TILE)
        dims = (3, members, 2) + half
        parts = run(
            partial(outer_kept, members, PLACES),
            [("h", (members,) + half, F32)] * 6,
            "s" + "h" * 5 + "va",
            [
                vmem(width, count), vmem(count, 3 * width // 2), vmem(width, count), vmem(n_pass, width // 2),
                vmem(n_query, width // 2), vmem(*dims, dtype=F32), vmem(3, 2, members, *half, dtype=F32), sems(8), sems(6),
            ],
            (facts, turned, mixed_grad, attended_turned, bg_pass, bg_query, vectors, swap(sent[0], "pb", 1)),
            limit=24,
        )
        inner, _ = advance_by_kernel(facts, inner, 2, leaf_rows[0], after=tuple(parts[0:6:2]))
        inner_mine, late = last_exchange(facts, inner, leaf_rows[0], (parts[2],))
        outer = begun([parts[0:2], (late[0], parts[3]), parts[4:6]])
        for step in (1, 2):
            outer = advance(outer, step, leaf_rows[1])
        outer_mine, _ = last_exchange(facts, outer, leaf_rows[1])

        near = [swap(mine, "pb", 2) for mine in (inner_mine, outer_mine)]
        parts = [
            (mine, other, swap(mine, "pb", 1), swap(other, "pb", 1)) for mine, other in zip((inner_mine, outer_mine), near)
        ]
        expand_total, reduce_total, in_total, out_total, gains_grad, biases_grad, term_grad, bias_grad, expand_shift = run(
            finish_both,
            [
                ("v", (shard, deep), F32), ("v", (deep // members, width), F32),
                ("v", (shard, 3 * width), F32), ("v", (shard, width), F32), ("v", (2, shard), F32), ("v", (6, shard), F32),
                ("v", (1, shard), F32), ("v", (1, 1), F32), ("v", (1, deep // members), F32),
            ],
            "s" + "v" * 8, [], (facts,) + parts[0] + parts[1], limit=16,
        )
    else:
        in_order = [h.reshape(3, h.shape[1], -1, TILE).transpose(1, 2, 0, 3).reshape(-1, deep) for h in (hidden, hidden_query)]
        whole = [jnp.concatenate(pair, axis) for pair, axis in (
            (in_order, 0), ((rg_pass, rg_query), 1), ((eg_pass, eg_query), 0), ((bg_pass, bg_query), 0),
        )]
        reduce_total = summed_rows(whole[0], whole[1].T, ROW_FIRST)
        expand_total = summed_rows(low, whole[2], GROUP_FIRST)
        out_total = summed_rows(attended, whole[3], GROUP_FIRST)
        in_total = summed_rows(turned.T, mixed_grad, ROW_FIRST)
        vectors = total_of_all(vectors)
        mine = lax.dynamic_slice_in_dim(vectors[:10], member_index * shard, shard, axis=1)
        expand_shift = lax.dynamic_slice_in_dim(
            vectors[16:].reshape(-1), member_index * (deep // members), deep // members
        )
        gains_grad = mine[:2]
        biases_grad = jnp.concatenate([mine[8:10], mine[2:6]])
        term_grad = mine[6]
        bias_grad = mine[7, :1]
    return (
        scores.T,
        passage_out,
        passage_grad,
        query_grad,
        in_total,
        out_total,
        expand_total,
        expand_shift.reshape(-1),
        reduce_total,
        gains_grad,
        biases_grad,
        term_grad.reshape(-1),
        bias_grad.reshape(-1),
    )


def solution(mesh):
    return jax.shard_map(
        on_device,
        mesh=mesh,
        in_specs=(
            P(("pb", "pa"), None),
            P(("pb", "pa"), None),
            P(("pb", "pa")),
            P(("pb", "pa")),
            P(),
            P(("pb", "pa")),
            P(),
            P(),
            P(),
            P(),
            P(),
            P(),
            P(),
            P(),
            P(),
            P(("pb", "pa"), None),
            P("pb", "pa"),
        ),
        out_specs=(
            P("pb", "pa"),
            P(("pb", "pa"), None),
            P(("pb", "pa"), None),
            P(("pb", "pa"), None),
            P("pa", None),
            P("pa", None),
            P("pa", None),
            P("pa"),
            P("pa", None),
            P(None, "pa"),
            P(None, "pa"),
            P("pa"),
            P(),
        ),
        check_vma=False,
    )
```
